128 devices in a mesh: band: 4 (over y), base: 32 (over z, x, core).
Axes of the slice: x: 4, y: 4, z: 4, core: 2. Of those that a mesh axis runs over, the one named last changes fastest.
Arguments:
- visibilities: bfloat16 [8, 64, 256, 256], P(None, 'base', 'band'), may hold values from -6 to 6
- model: bfloat16 [8, 64, 256, 256], P(None, 'base', 'band'), may hold values from -6 to 6
- start_gains: float32 [8, 128, 512], P(None, 'band', 'base'), may hold values from -1.5 to 2.5
- penalty: float32 [512], P('base'), may hold values from 0.5 to 5
- pairs: int32 [64, 2], P('base'), may hold values from 0 to 31, as said below
- flags: int32 [64, 256], P('base'), may hold values 0 or 1
- chan_band: int32 [256], P('band'), may hold values from 0 to 127, as said below
Outputs:
- gains: float32 [8, 128, 512], P(None, 'band', 'base')
- coefficients: float32 [8, 9, 512], P(None, None, 'base')
The draws below stay inside these ranges and needn't reach their ends.
Inputs may be any that keep to these rules, and one draw needn't show every extreme that they name: `pairs`: each tile joins blocks a <= b, and no two tiles join the same pair of blocks. `chan_band`: the 64 channels of the k-th block of 64 channels map, never falling, onto the intervals k * 32 to k * 32 + 31, each interval holding one channel or more.
All inputs are finite; a program needn't handle non-finite values. No bound on the sum of `flags` on one device may be relied on, other than what follows from the above.
Results may differ from the reference program's by a relative error of at most 0.0003.
Values sent between devices are 32-bit elements; how exact they have to be, the bound alone decides.
A program may use at most 128 MiB of HBM per device.

```python
import math
import jax
import jax.numpy as jnp
from jax import lax

NST = 512
BLOCK = 16
NBLK = 32
NPOLY = 9
TILES = 64
CH_DEV = 64
NCHAN = 256
SOL_DEV = 32
SOL = 128
ITERS = 3


def draw_start_gains(key, part):
    key = jax.random.fold_in(key, 5)
    noise = 0.3 * jnp.clip(jax.random.normal(key, (8, SOL, NST), jnp.float32), -4.0, 4.0)
    ident = jnp.zeros((8, 1, 1), jnp.float32).at[0].set(1.0).at[3].set(1.0)
    return noise + ident


def draw_pairs(key, part):
    key = jax.random.fold_in(key, 7)
    lower_ids, upper_ids = jnp.triu_indices(NBLK)
    total = lower_ids.shape[0]
    planted = NBLK - 1
    scores = jax.random.permutation(key, total).astype(jnp.int32)
    scores = jnp.where(jnp.arange(total, dtype=jnp.int32) == planted, -1, scores)
    chosen = jnp.argsort(scores, stable=True)[:TILES]
    return jnp.stack([lower_ids[chosen], upper_ids[chosen]], 1).astype(jnp.int32)


def draw_chan_band(key, part):
    key = jax.random.fold_in(key, 11)
    groups = NCHAN // CH_DEV

    def one_group(index):
        cuts = jax.random.permutation(jax.random.fold_in(key, index), CH_DEV - 1)[:SOL_DEV - 1] + 1
        places = jnp.arange(CH_DEV, dtype=jnp.int32)
        local = jnp.sum((places[:, None] >= cuts[None, :]).astype(jnp.int32), 1)
        return local + index * SOL_DEV
    return jax.vmap(one_group)(jnp.arange(groups, dtype=jnp.int32)).reshape(-1).astype(jnp.int32)


def set_ends(entries, stream_key, low, largest):
    longest = entries.shape.index(max(entries.shape))
    spots = []
    for shift in (0, 1):
        where = [jax.random.randint(jax.random.fold_in(stream_key, axis), (), 0, length) for axis, length in enumerate(entries.shape)]
        where[longest] = (where[longest] + shift) % entries.shape[longest]
        spots.append(tuple(where))
    return entries.at[spots[0]].set(low).at[spots[1]].set(largest)


def levels(rng, dims, pieces, low, high):
    def one(axis_at, shards_of):
        draws = jax.random.uniform(jax.random.fold_in(jax.random.fold_in(rng, 6), axis_at), (shards_of,), jnp.float32, low / len(pieces), high / len(pieces))
        return jnp.repeat(jnp.exp(draws), dims[axis_at] // shards_of).reshape((-1,) + (1,) * (len(dims) - axis_at - 1))

    level = one(*pieces[0])
    for cut in pieces[1:]:
        level = level * one(*cut)
    return level


def centred(key, extent, scale, most, pieces=(), held_as=jnp.bfloat16):
    values = jax.random.normal(key, extent, jnp.float32) * scale
    if len(pieces) > 0:
        values = levels(key, extent, pieces, -0.22, 0.18) * values
    return jnp.clip(values, min=-most, max=most).astype(held_as)


def setup_inputs(seed: int = 0) -> dict:
    key_of = jax.random.split(jax.random.key(seed), 8)
    return {
        "visibilities": centred(key_of[0], (8, TILES, NCHAN, BLOCK * BLOCK), 1.0, 6.0, ((1, 32), (2, 4))),
        "model": centred(key_of[1], (8, TILES, NCHAN, BLOCK * BLOCK), 1.0, 6.0, ((1, 32), (2, 4))),
        "start_gains": draw_start_gains(jax.random.fold_in(key_of[7], 71), 0),
        "penalty": jnp.clip(jnp.exp(math.log(5.0) - 2.3025851 * jax.random.uniform(key_of[3], (NST,), jnp.float32) ** levels(key_of[3], (NST,), ((0, 32),), -0.2, 0.2)), 0.5, 5.0),
        "pairs": draw_pairs(jax.random.fold_in(key_of[7], 71), 0),
        "flags": set_ends((jax.random.randint(key_of[5], (TILES, BLOCK * BLOCK), 0, 8) < 7).astype(jnp.int32), jax.random.fold_in(key_of[5], 1), 0, 1),
        "chan_band": draw_chan_band(jax.random.fold_in(key_of[7], 71), 0),
    }


ridge = 0.5

def cmul(left, right):

    def product(upper, lower):
        return jnp.stack([jnp.stack([upper[row_at, 0] * lower[0, col_at] + upper[row_at, 1] * lower[1, col_at] for col_at in range(2)]) for row_at in range(2)])
    return jnp.stack([product(left[0], right[0]) - product(left[1], right[1]), product(left[0], right[1]) + product(left[1], right[0])])

def cherm(matrix):
    return jnp.stack([jnp.swapaxes(matrix[0], 0, 1), -jnp.swapaxes(matrix[1], 0, 1)])

def pack_terms(gain_part, outer_part):
    flat = gain_part.reshape((8,) + gain_part.shape[3:])
    hermit = jnp.stack([outer_part[0, 0, 0], outer_part[0, 1, 1], outer_part[0, 0, 1], outer_part[1, 0, 1]])
    return jnp.concatenate([flat, hermit], 0)

def tile_terms(vis, mdl, first, second, weight):
    along = cmul(mdl, cherm(second))
    gain_first = jnp.sum(weight * cmul(vis, cherm(along)), -1)
    outer_first = jnp.sum(weight * cmul(along, cherm(along)), -1)
    back = cmul(first, mdl)
    gain_second = jnp.sum(weight * cmul(cherm(vis), back), -2)
    outer_second = jnp.sum(weight * cmul(cherm(back), back), -2)
    return (pack_terms(gain_first, outer_first), pack_terms(gain_second, outer_second))

def solve_gains(normal, counts, consensus, dual, penalty):
    scale = 1.0 / jnp.maximum(counts, 1.0)
    rhs = normal[:8] * scale + penalty * (consensus - dual)
    h_first = normal[8] * scale + penalty
    h_second = normal[9] * scale + penalty
    h_real = normal[10] * scale
    h_imag = normal[11] * scale
    determ = h_first * h_second - h_real * h_real - h_imag * h_imag
    zeros = jnp.zeros_like(determ)
    inv_re = jnp.stack([jnp.stack([h_second, -h_real]), jnp.stack([-h_real, h_first])]) / determ
    inv_im = jnp.stack([jnp.stack([zeros, -h_imag]), jnp.stack([h_imag, zeros])]) / determ
    solved = cmul(rhs.reshape((2, 2, 2) + rhs.shape[1:]), jnp.stack([inv_re, inv_im]))
    return solved.reshape(rhs.shape)

def chebyshev(centre):
    terms = [jnp.ones_like(centre), centre]
    for order in range(2, NPOLY):
        terms.append(2.0 * centre * terms[-1] - terms[-2])
    return jnp.stack(terms[:NPOLY], 1)

def reference(visibilities, model, start_gains, penalty, pairs, flags, chan_band):
    high = lax.Precision.HIGHEST
    onehot = (chan_band[:, None] == jnp.arange(SOL, dtype=jnp.int32)[None, :]).astype(jnp.float32)
    chans = jnp.sum(onehot, 0)
    xpos = -1.0 + (2.0 * jnp.arange(NCHAN, dtype=jnp.float32) + 1.0) / NCHAN
    centre = jnp.sum(onehot * xpos[:, None], 0) / chans
    basis = chebyshev(centre)
    gram = jnp.dot(basis.T, basis, precision=high) + ridge * jnp.eye(NPOLY, dtype=jnp.float32)
    factor = jnp.linalg.cholesky(gram)
    same = (pairs[:, 0] == pairs[:, 1]).astype(jnp.float32)
    weights = flags.reshape(TILES, BLOCK, BLOCK).astype(jnp.float32) * (1.0 - same[:, None, None] * jnp.eye(BLOCK, dtype=jnp.float32))
    inside = jnp.arange(BLOCK, dtype=jnp.int32)
    station_w = jnp.zeros((NST,), jnp.float32)
    station_w = station_w.at[(pairs[:, 0:1] * BLOCK + inside[None, :]).reshape(-1)].add(jnp.sum(weights, 2).reshape(-1))
    station_w = station_w.at[(pairs[:, 1:2] * BLOCK + inside[None, :]).reshape(-1)].add(jnp.sum(weights, 1).reshape(-1))
    counts = chans[:, None] * station_w[None, :]
    gains = start_gains
    consensus = start_gains
    dual = jnp.zeros_like(start_gains)
    coeff = jnp.zeros((NPOLY, 8, NST), jnp.float32)
    for step in range(ITERS):

        def per_tile(index, total):
            vis = lax.dynamic_index_in_dim(visibilities, index, 1, keepdims=False).astype(jnp.float32).reshape(2, 2, 2, NCHAN, BLOCK, BLOCK)
            mdl = lax.dynamic_index_in_dim(model, index, 1, keepdims=False).astype(jnp.float32).reshape(2, 2, 2, NCHAN, BLOCK, BLOCK)
            start_a = (pairs[index, 0] * BLOCK).astype(jnp.int32)
            start_b = (pairs[index, 1] * BLOCK).astype(jnp.int32)
            first = jnp.einsum('ksi,cs->kci', lax.dynamic_slice_in_dim(gains, start_a, BLOCK, 2), onehot, precision=high)
            second = jnp.einsum('ksi,cs->kci', lax.dynamic_slice_in_dim(gains, start_b, BLOCK, 2), onehot, precision=high)
            terms_a, terms_b = tile_terms(vis, mdl, first.reshape(2, 2, 2, NCHAN, BLOCK, 1), second.reshape(2, 2, 2, NCHAN, 1, BLOCK), weights[index])
            sum_a = jnp.einsum('kci,cs->ksi', terms_a, onehot, precision=high)
            sum_b = jnp.einsum('kci,cs->ksi', terms_b, onehot, precision=high)
            total = lax.dynamic_update_slice_in_dim(total, lax.dynamic_slice_in_dim(total, start_a, BLOCK, 2) + sum_a, start_a, 2)
            total = lax.dynamic_update_slice_in_dim(total, lax.dynamic_slice_in_dim(total, start_b, BLOCK, 2) + sum_b, start_b, 2)
            return total
        normal = lax.fori_loop(0, TILES, per_tile, jnp.zeros((12, SOL, NST), jnp.float32))
        gains = solve_gains(normal, counts, consensus, dual, penalty)
        total = jnp.einsum('sk,msn->kmn', basis, gains + dual, precision=high)
        coeff = jax.scipy.linalg.cho_solve((factor, True), total.reshape(NPOLY, -1)).reshape(NPOLY, 8, NST)
        consensus = jnp.einsum('sk,kmn->msn', basis, coeff, precision=high)
        dual = dual + gains - consensus
    return (gains, jnp.transpose(coeff, (1, 0, 2)))
```

```python
import functools

import jax
import jax.numpy as jnp
from jax import lax
from jax.experimental import pallas as pl
from jax.experimental.pallas import tpu as pltpu
from jax.sharding import PartitionSpec as P

BLOCK = 16
NPOLY = 9
ITERS = 3
RIDGE = 0.5
MESH = pl.DeviceIdType.MESH
F32 = jnp.float32
BF16 = jnp.bfloat16
SIDE = 4
CHIPS = SIDE * SIDE
BANDS = 4
TILES = 2
CHANS = 64
CELLS = BLOCK * BLOCK
SOLS = 32
LANES = 128
ROWS = SOLS + SOLS // 2
NCOEF = 48
PAIRS = [(0, 1), (0, 2), (0, 3), (1, 2), (1, 3), (2, 3)]


def lanes(x, idx):
    numbers = lax.GatherDimensionNumbers(
        offset_dims=(),
        collapsed_slice_dims=(1,),
        start_index_map=(1,),
        operand_batching_dims=(0,),
        start_indices_batching_dims=(0,),
    )
    return lax.gather(
        x, idx[..., None], numbers, (1, 1), mode=lax.GatherScatterMode.PROMISE_IN_BOUNDS
    )


def iota(shape, axis):
    return lax.broadcasted_iota(jnp.int32, shape, axis)


def merge(a, b, lane, bit):
    clear = (lane & bit) == 0
    return jnp.where(clear, a, b) + lanes(jnp.where(clear, b, a), lane ^ bit)


def merge_all(arrays, lane, top):
    bit = top
    while len(arrays) > 1:
        half = len(arrays) // 2
        arrays = [merge(a, b, lane, bit) for a, b in zip(arrays[:half], arrays[half:])]
        bit //= 2
    return arrays[0]


def mul(a, b):
    return (a[0] * b[0] - a[1] * b[1], a[0] * b[1] + a[1] * b[0])


def mul_conj(a, b):
    return (a[0] * b[0] + a[1] * b[1], a[0] * b[1] - a[1] * b[0])


def conj(a):
    return (a[0], -a[1])


def add(*terms):
    re, im = terms[0]
    for t in terms[1:]:
        re, im = re + t[0], im + t[1]
    return (re, im)


def scaled(a, r):
    return (a[0] * r, a[1] * r)


def outer(j):
    c = [(j[k], j[4 + k]) for k in range(4)]
    q00 = c[0][0] * c[0][0] + c[0][1] * c[0][1] + c[2][0] * c[2][0] + c[2][1] * c[2][1]
    q11 = c[1][0] * c[1][0] + c[1][1] * c[1][1] + c[3][0] * c[3][0] + c[3][1] * c[3][1]
    q01 = add(mul_conj(c[0], c[1]), mul_conj(c[2], c[3]))
    return q00, q11, q01


def station_terms(load, jp, jq):
    p = [(jp[k], jp[4 + k]) for k in range(4)]
    q = [(jq[k], jq[4 + k]) for k in range(4)]
    cross = {}
    for ab in range(4):
        for cd in range(4):
            cross[ab, cd] = (load(4 * ab + cd), load(16 + 4 * ab + cd))
    gp, gq = [], []
    for a in range(2):
        for d in range(2):
            gp.append(
                add(
                    *[
                        mul(cross[2 * a + b, 2 * d + c], q[2 * b + c])
                        for b in range(2)
                        for c in range(2)
                    ]
                )
            )
            gq.append(
                add(
                    *[
                        mul_conj(cross[2 * b + a, 2 * c + d], p[2 * b + c])
                        for b in range(2)
                        for c in range(2)
                    ]
                )
            )
    diag = [load(32 + k) for k in range(4)]
    off = {pair: (load(36 + 2 * n), load(37 + 2 * n)) for n, pair in enumerate(PAIRS)}
    q00, q11, q01 = outer(jq)
    two = scaled(q01, 2.0)
    hp = [
        diag[0] * q00 + diag[1] * q11 + mul_conj(conj(off[0, 1]), two)[0],
        diag[2] * q00 + diag[3] * q11 + mul_conj(conj(off[2, 3]), two)[0],
        *add(
            scaled(off[0, 2], q00),
            mul(off[0, 3], q01),
            mul_conj(q01, off[1, 2]),
            scaled(off[1, 3], q11),
        ),
    ]
    r00, r11, r01 = outer(jp)
    two = scaled(r01, 2.0)
    hq = [
        diag[0] * r00 + diag[2] * r11 + mul_conj(off[0, 2], two)[0],
        diag[1] * r00 + diag[3] * r11 + mul_conj(off[1, 3], two)[0],
        *add(
            scaled(conj(off[0, 1]), r00),
            mul_conj(off[0, 3], r01),
            mul_conj(r01, off[1, 2]),
            scaled(conj(off[2, 3]), r11),
        ),
    ]
    gp = [g[0] for g in gp] + [g[1] for g in gp]
    gq = [g[0] for g in gq] + [g[1] for g in gq]
    return gp, hp, gq, hq


def kernel(
    vis_hbm, mdl_hbm, start_hbm, pen_hbm, pairs_hbm, flags_hbm, chan_hbm,
    gains_out, coeff_out,
    vis, mdl, start, pen_in, pairs, flags, chan,
    vf, mf, coef, every, terms, sterms, sbuf, rbuf, prec, pv, spv, wrec, wsum, swsum,
    basis, scale, pen, cons, dual, ginv,
    loc, ag_s, ag_r, sx_s, sx_r, ts_s, ts_r, rs_s, rs_r, ps_s, ps_r, one,
):
    band = lax.axis_index("band")
    base = lax.axis_index("base")
    core = base % 2
    chip = base // 2
    cz = chip // SIDE
    cx = chip % SIDE
    sibling = chip * 2 + (1 - core)

    def peer_chip(r):
        return ((cz + r // SIDE) % SIDE) * SIDE + (cx + r % SIDE) % SIDE

    def copy(src, dst, send, recv, band_to, base_to):
        return pltpu.make_async_remote_copy(
            src_ref=src, dst_ref=dst, send_sem=send, recv_sem=recv,
            device_id=(band_to, base_to), device_id_type=MESH,
        )

    def to_chips(make):
        def step(r, carry):
            k = peer_chip(CHIPS - r)
            make(k).start()
            return carry

        lax.fori_loop(1, CHIPS, step, 0)

    local = [
        pltpu.make_async_copy(src, dst, loc.at[n])
        for n, (src, dst) in enumerate(
            [
                (start_hbm, start), (pairs_hbm, pairs), (flags_hbm, flags), (chan_hbm, chan),
                (pen_hbm, pen_in), (mdl_hbm, mdl), (vis_hbm, vis),
            ]
        )
    ]
    for c in local:
        c.start()

    barrier = pltpu.get_barrier_semaphore()

    def greet_chip(r, carry):
        pl.semaphore_signal(
            barrier, inc=1, device_id=(band, peer_chip(r) * 2 + core), device_id_type=MESH
        )
        return carry

    lax.fori_loop(1, CHIPS, greet_chip, 0)
    pl.semaphore_signal(barrier, inc=1, device_id=(band, sibling), device_id_type=MESH)

    def greet_band(r, carry):
        pl.semaphore_signal(
            barrier, inc=1, device_id=((band + r) % BANDS, base), device_id_type=MESH
        )
        return carry

    lax.fori_loop(1, BANDS, greet_band, 0)

    lane8 = iota((8, LANES), 1)
    row8 = iota((8, LANES), 0)
    for c in local[:5]:
        c.wait()
    mine = jnp.concatenate([start[k] for k in range(8)], axis=1)
    every[0, core, chip] = mine
    cons[...] = mine
    dual[...] = jnp.zeros_like(mine)

    pl.semaphore_wait(barrier, CHIPS + BANDS - 1)

    def send_gains(it):
        to_chips(
            lambda k: copy(
                every.at[it, core, chip], every.at[it, core, chip], ag_s.at[it], ag_r.at[it],
                band, 2 * k + core,
            )
        )

    send_gains(0)

    ends = [pairs[t, side] for t in range(TILES) for side in range(2)]
    named = jnp.zeros((8, LANES), jnp.int32)
    for e, b in enumerate(ends):
        named = jnp.where(row8 == e, b, named)
    pv[...] = named
    pairs_copy = copy(pv, spv, one.at[0], one.at[1], band, sibling)
    pairs_copy.start()

    cell = iota((1, CELLS), 1)
    eye = (cell // BLOCK == cell % BLOCK).astype(F32)
    weights = []
    for t in range(TILES):
        same = jnp.where(ends[2 * t] == ends[2 * t + 1], 1.0, 0.0)
        weights.append(flags[t : t + 1, :].astype(F32) * (1.0 - same * eye))
    both = jnp.concatenate([*weights, jnp.zeros((6, CELLS), F32)], axis=0).astype(BF16)
    fold_row = iota((CELLS, LANES), 0)
    fold_lane = iota((CELLS, LANES), 1) % BLOCK
    at_first = jnp.dot(
        both, (fold_row // BLOCK == fold_lane).astype(F32).astype(BF16),
        preferred_element_type=F32,
    )
    at_second = jnp.dot(
        both, (fold_row % BLOCK == fold_lane).astype(F32).astype(BF16),
        preferred_element_type=F32,
    )
    partial = jnp.zeros((8, LANES), F32)
    for e, b in enumerate(ends):
        t = e // 2
        at_end = (at_second if e % 2 else at_first)[t : t + 1, :]
        here = (row8 == (b >> 3)) & (lane8 // BLOCK == (b & 7))
        partial = partial + jnp.where(here, jnp.broadcast_to(at_end, (8, LANES)), 0.0)
    wrec[chip] = partial
    to_chips(
        lambda k: copy(wrec.at[chip], wrec.at[chip], one.at[2], one.at[3], band, 2 * k + core)
    )

    sol = band * SOLS + iota((SOLS, CHANS), 0)
    chan_row = chan[...]
    member = (jnp.broadcast_to(chan_row, (SOLS, CHANS)) == sol).astype(F32)
    where_c = (band * CHANS + iota((SOLS, CHANS), 1)).astype(F32)
    xpos = -1.0 + (2.0 * where_c + 1.0) / (CHANS * BANDS)
    chans = jnp.sum(member, axis=1, keepdims=True)
    centre = jnp.broadcast_to(
        jnp.sum(member * xpos, axis=1, keepdims=True) / chans, (SOLS, LANES)
    )
    cheb = [jnp.ones_like(centre), centre]
    for _ in range(2, NPOLY):
        cheb.append(2.0 * centre * cheb[-1] - cheb[-2])
    for k in range(NPOLY):
        basis[k] = cheb[k]
    member2 = jnp.concatenate([member, member], axis=1).astype(BF16)

    for c in local[5:]:
        c.wait()

    def collapse(t, carry):
        w = jnp.where(t == 0, weights[0], weights[1])
        for k in range(8):
            vf[k] = vis[k, t].astype(F32)
            mf[k] = mdl[k, t].astype(F32) * w

        def put(n, product):
            high = product.astype(BF16)
            low = (product - high.astype(F32)).astype(BF16)
            coef[n, t] = jnp.dot(
                member2, jnp.concatenate([high, low], axis=0), preferred_element_type=F32
            )

        for ab in range(4):
            vr, vi = vf[ab], vf[4 + ab]
            for cd in range(4):
                mr, mi = mf[cd], mf[4 + cd]
                put(4 * ab + cd, vr * mr + vi * mi)
                put(16 + 4 * ab + cd, vi * mr - vr * mi)
        for ab in range(4):
            put(32 + ab, mf[ab] * mf[ab] + mf[4 + ab] * mf[4 + ab])
        for n, (x, y) in enumerate(PAIRS):
            put(36 + 2 * n, mf[x] * mf[y] + mf[4 + x] * mf[4 + y])
            put(37 + 2 * n, mf[4 + x] * mf[y] - mf[x] * mf[4 + y])
        return carry

    lax.fori_loop(0, TILES, collapse, 0)

    def all_of(buffer, sem):
        part = buffer.at[pl.ds(0, CHIPS - 1)]
        pltpu.make_async_copy(part, part, sem).wait()

    all_of(wrec, one.at[3])
    wsum[...] = functools.reduce(lambda a, b: a + b, [wrec[k] for k in range(CHIPS)])
    sums_copy = copy(wsum, swsum, one.at[4], one.at[5], band, sibling)
    sums_copy.start()
    pairs_copy.wait_recv()
    sums_copy.wait_recv()
    row = wsum[pl.ds(base // 8, 1), :] + swsum[pl.ds(base // 8, 1), :]
    row = jnp.broadcast_to(row, (8, LANES))
    row = lanes(row, (base % 8) * BLOCK + lane8 % BLOCK)
    counts = chans * jnp.broadcast_to(row[0:1, :], (SOLS, LANES))
    scale[...] = 1.0 / jnp.maximum(counts, 1.0)
    pen[...] = jnp.broadcast_to(
        jnp.concatenate([pen_in[...]] * 8, axis=1), (8, LANES)
    )

    def total_of(it, values):
        lane = iota((SOLS, LANES), 1)
        columns = jnp.zeros((SOLS, LANES), F32)
        for k in range(NPOLY):
            columns = jnp.where(lane == k, basis[k], columns)
        rows = [jnp.sum(basis[k] * values, axis=0, keepdims=True) for k in range(NPOLY)]
        gram = [jnp.sum(basis[k] * columns, axis=0, keepdims=True) for k in range(NPOLY)]
        pad = [jnp.zeros((16 - NPOLY, LANES), F32)]
        prec[it, band] = jnp.concatenate(rows + pad + gram + pad, axis=0)

        def step(r, carry):
            copy(
                prec.at[it, band], prec.at[it, band], ps_s.at[it], ps_r.at[it],
                (band + r) % BANDS, base,
            ).start()
            return carry

        lax.fori_loop(1, BANDS, step, 0)

    def coefficients(it, first):
        part = prec.at[it, pl.ds(0, BANDS - 1)]
        pltpu.make_async_copy(part, part, ps_r.at[it]).wait()
        total = prec[it, 0] + prec[it, 1] + prec[it, 2] + prec[it, 3]

        def invert():
            r, l = iota((16, LANES), 0), iota((16, LANES), 1)
            m = total[16:, :] + jnp.where((r == l) & (r < NPOLY), RIDGE, 0.0)
            m = m + jnp.where((l == r + 16) & (r < NPOLY), 1.0, 0.0)
            for p in range(NPOLY):
                pivot = m[p : p + 1, :] / m[p : p + 1, p : p + 1]
                m = jnp.where(r == p, pivot, m - m[:, p : p + 1] * pivot)
            for k in range(NPOLY):
                ginv[k] = jnp.broadcast_to(m[:, 16 + k : 17 + k], (16, LANES))

        if first is not None:
            pl.when(first)(invert)
        out = ginv[0] * total[0:1, :]
        for k in range(1, NPOLY):
            out = out + ginv[k] * total[k : k + 1, :]
        return out

    step_rows = 16
    lane = iota((step_rows, LANES), 1)
    inner = lane % BLOCK
    natural = (inner % 8) * BLOCK + (inner // 8) * 8 + lane // BLOCK

    def iteration(it, carry):
        @pl.when(it > 0)
        def _():
            every[it, core, chip] = every[ITERS, core, chip]
            send_gains(it)
            coeff = coefficients(it - 1, it == 1)
            agreed = basis[0] * coeff[0:1, :]
            for k in range(1, NPOLY):
                agreed = agreed + basis[k] * coeff[k : k + 1, :]
            dual[...] = dual[...] + every[it, core, chip] - agreed
            cons[...] = agreed

        all_of(every.at[it, core], ag_r.at[it])
        across = copy(
            every.at[it, core], every.at[it, core], sx_s.at[it], sx_r.at[it], band, sibling
        )
        across.start()
        incoming = every.at[it, 1 - core]
        pltpu.make_async_copy(incoming, incoming, sx_r.at[it]).wait()

        def tile(t, carry):
            first, second = pairs[t, 0], pairs[t, 1]
            packed = []
            for part in range(2):
                rows = pl.ds(part * step_rows, step_rows)
                of_p = every[it, first & 1, first >> 1, rows, :]
                of_q = every[it, second & 1, second >> 1, rows, :]
                jq = [lanes(of_q, k * BLOCK + inner) for k in range(8)]
                gp, hp, gq, hq = [], [], [], []
                for half in range(2):
                    jp = [lanes(of_p, k * BLOCK + half * 8 + lane // BLOCK) for k in range(8)]

                    def load(n):
                        return coef[n, t, rows, pl.ds(half * LANES, LANES)]

                    a, b, c, d = station_terms(load, jp, jq)
                    gp.append(a)
                    hp.append(b)
                    gq.append(c)
                    hq.append(d)
                terms[it, 2 * t, rows, :] = lanes(merge_all(gp[0] + gp[1], lane, 8), natural)
                summed = [x + y for x, y in zip(gq[0], gq[1])]
                terms[it, 2 * t + 1, rows, :] = merge_all(summed, lane, 64)
                packed.append((hp, [x + y for x, y in zip(hq[0], hq[1])]))
            rows = pl.ds(SOLS, step_rows)
            (hp0, hq0), (hp1, hq1) = packed
            arrays = hp0[0] + hp1[0] + hp0[1] + hp1[1]
            terms[it, 2 * t, rows, :] = lanes(merge_all(arrays, lane, 8), natural)
            terms[it, 2 * t + 1, rows, :] = merge_all(hq0 + hq1, lane, 64)
            pair = pl.ds(2 * t, 2)
            copy(
                terms.at[it, pair], sterms.at[it, pair], ts_s.at[it], ts_r.at[it], band, sibling
            ).start()
            return carry

        lax.fori_loop(0, TILES, tile, 0)
        incoming = sterms.at[it]
        pltpu.make_async_copy(incoming, incoming, ts_r.at[it]).wait()

        def share(k):
            target = 2 * k + core
            out = jnp.zeros((ROWS, LANES), F32)
            for names, held in ((pv, terms), (spv, sterms)):
                for e in range(2 * TILES):
                    hit = jnp.where(names[e : e + 1, :] == target, 1.0, 0.0)
                    out = out + hit * held[it, e]
            return out

        def send_share(r, carry):
            k = peer_chip(CHIPS - r)
            sbuf[it, k] = share(k)
            copy(
                sbuf.at[it, k], rbuf.at[it, chip], rs_s.at[it], rs_r.at[it], band, 2 * k + core
            ).start()
            return carry

        lax.fori_loop(1, CHIPS, send_share, 0)
        rbuf[it, chip] = share(chip)
        all_of(rbuf.at[it], rs_r.at[it])
        normal = functools.reduce(lambda a, b: a + b, [rbuf[it, k] for k in range(CHIPS)])

        l = iota((SOLS, LANES), 1)
        part = l % BLOCK
        upper = (l & BLOCK) != 0
        packed = normal[SOLS:, :]
        outer_part = jnp.concatenate([packed, pltpu.roll(packed, 64, 1)], axis=0)
        per = scale[...]
        rho = pen[0:1, :]
        rhs = normal[:SOLS, :] * per + rho * (cons[...] - dual[...])
        h_diag = lanes(outer_part, jnp.where(upper, part, BLOCK + part)) * per + rho
        h_real = lanes(outer_part, 2 * BLOCK + part) * per
        h_imag = lanes(outer_part, 3 * BLOCK + part) * per
        determ = h_diag * lanes(h_diag, l ^ BLOCK) - h_real * h_real - h_imag * h_imag
        sign = jnp.where(upper == (l < 64), 1.0, -1.0)
        solved = (
            rhs * h_diag
            - lanes(rhs, l ^ BLOCK) * h_real
            + sign * lanes(rhs, l ^ (64 + BLOCK)) * h_imag
        ) / determ
        every[ITERS, core, chip] = solved
        total_of(it, solved + dual[...])
        return carry

    lax.fori_loop(0, ITERS, iteration, 0)

    gains = every[ITERS, core, chip]
    for k in range(8):
        gains_out[k] = gains[:, k * BLOCK : (k + 1) * BLOCK]
    coeff = coefficients(ITERS - 1, None)
    for k in range(8):
        coeff_out[k] = coeff[:NPOLY, k * BLOCK : (k + 1) * BLOCK]

    def sent(ref, sem):
        pltpu.make_async_copy(ref, ref, sem).wait()

    pairs_copy.wait_send()
    sums_copy.wait_send()
    sent(wrec.at[pl.ds(0, CHIPS - 1)], one.at[2])
    for it in range(ITERS):
        sent(every.at[it, 0, pl.ds(0, CHIPS - 1)], ag_s.at[it])
        sent(every.at[it, 0], sx_s.at[it])
        sent(terms.at[it], ts_s.at[it])
        sent(sbuf.at[it, pl.ds(0, CHIPS - 1)], rs_s.at[it])
        sent(prec.at[it, pl.ds(0, BANDS - 1)], ps_s.at[it])


def on_device(visibilities, model, start_gains, penalty, pairs, flags, chan_band):
    vmem, dma = pltpu.VMEM, pltpu.SemaphoreType.DMA
    block = (SOLS, LANES)
    gains, coeff = pl.pallas_call(
        kernel,
        out_shape=(
            jax.ShapeDtypeStruct((8, SOLS, BLOCK), F32),
            jax.ShapeDtypeStruct((8, NPOLY, BLOCK), F32),
        ),
        in_specs=[pl.BlockSpec(memory_space=pl.ANY)] * 7,
        out_specs=(pl.BlockSpec(memory_space=vmem), pl.BlockSpec(memory_space=vmem)),
        scratch_shapes=[
            vmem((8, TILES, CHANS, CELLS), BF16),
            vmem((8, TILES, CHANS, CELLS), BF16),
            vmem((8, SOLS, BLOCK), F32),
            vmem((1, BLOCK), F32),
            pltpu.SMEM((TILES, 2), jnp.int32),
            vmem((TILES, CELLS), jnp.int32),
            vmem((1, CHANS), jnp.int32),
            vmem((8, CHANS, CELLS), F32),
            vmem((8, CHANS, CELLS), F32),
            vmem((NCOEF, TILES, SOLS, CELLS), F32),
            vmem((ITERS + 1, 2, CHIPS, *block), F32),
            vmem((ITERS, 2 * TILES, ROWS, LANES), F32),
            vmem((ITERS, 2 * TILES, ROWS, LANES), F32),
            vmem((ITERS, CHIPS, ROWS, LANES), F32),
            vmem((ITERS, CHIPS, ROWS, LANES), F32),
            vmem((ITERS, BANDS, 32, LANES), F32),
            vmem((8, LANES), jnp.int32),
            vmem((8, LANES), jnp.int32),
            vmem((CHIPS, 8, LANES), F32),
            vmem((8, LANES), F32),
            vmem((8, LANES), F32),
            vmem((NPOLY, *block), F32),
            vmem(block, F32),
            vmem((8, LANES), F32),
            vmem(block, F32),
            vmem(block, F32),
            vmem((NPOLY, 16, LANES), F32),
            dma((7,)),
            *[dma((ITERS,))] * 10,
            dma((6,)),
        ],
        compiler_params=pltpu.CompilerParams(
            collective_id=0, has_side_effects=True, vmem_limit_bytes=40 * 1024 * 1024
        ),
        cost_estimate=pl.CostEstimate(
            flops=60_000_000, bytes_accessed=3_000_000, transcendentals=0
        ),
        name="admm",
    )(
        visibilities, model, start_gains, penalty.reshape(1, BLOCK), pairs, flags,
        chan_band.reshape(1, CHANS),
    )
    return gains, coeff


def solution(mesh):
    in_specs = (
        P(None, "base", "band", None),
        P(None, "base", "band", None),
        P(None, "band", "base"),
        P("base"),
        P("base", None),
        P("base", None),
        P("band"),
    )
    out_specs = (P(None, "band", "base"), P(None, None, "base"))
    return jax.shard_map(
        on_device, mesh=mesh, in_specs=in_specs, out_specs=out_specs, check_vma=False
    )
```

```python
import functools

import jax
import jax.numpy as jnp
from jax import lax
from jax.experimental import pallas as pl
from jax.experimental.pallas import tpu as pltpu
from jax.sharding import PartitionSpec as P

BLOCK = 16
NPOLY = 9
ITERS = 3
RIDGE = 0.5
MESH = pl.DeviceIdType.MESH
F32 = jnp.float32
BF16 = jnp.bfloat16
SIDE = 4
CHIPS = SIDE * SIDE
BANDS = 4
TILES = 2
CHANS = 64
CELLS = BLOCK * BLOCK
SOLS = 32
LANES = 128
HALF = SOLS // 2
ROWS = HALF + HALF // 2
FAR = sorted(
    [(dz, dx) for dz in range(SIDE) for dx in range(SIDE) if dz or dx],
    key=lambda d: -sum(min(n, SIDE - n) for n in d),
)
NCOEF = 48
PAIRS = [(0, 1), (0, 2), (0, 3), (1, 2), (1, 3), (2, 3)]


def lanes(x, idx):
    numbers = lax.GatherDimensionNumbers(
        offset_dims=(),
        collapsed_slice_dims=(1,),
        start_index_map=(1,),
        operand_batching_dims=(0,),
        start_indices_batching_dims=(0,),
    )
    return lax.gather(
        x, idx[..., None], numbers, (1, 1), mode=lax.GatherScatterMode.PROMISE_IN_BOUNDS
    )


def iota(shape, axis):
    return lax.broadcasted_iota(jnp.int32, shape, axis)


def merge(a, b, lane, bit):
    clear = (lane & bit) == 0
    return jnp.where(clear, a, b) + lanes(jnp.where(clear, b, a), lane ^ bit)


def merge_all(arrays, lane, top):
    bit = top
    while len(arrays) > 1:
        half = len(arrays) // 2
        arrays = [merge(a, b, lane, bit) for a, b in zip(arrays[:half], arrays[half:])]
        bit //= 2
    return arrays[0]


def mul(a, b):
    return (a[0] * b[0] - a[1] * b[1], a[0] * b[1] + a[1] * b[0])


def mul_conj(a, b):
    return (a[0] * b[0] + a[1] * b[1], a[0] * b[1] - a[1] * b[0])


def conj(a):
    return (a[0], -a[1])


def add(*terms):
    re, im = terms[0]
    for t in terms[1:]:
        re, im = re + t[0], im + t[1]
    return (re, im)


def scaled(a, r):
    return (a[0] * r, a[1] * r)


def outer(j):
    c = [(j[k], j[4 + k]) for k in range(4)]
    q00 = c[0][0] * c[0][0] + c[0][1] * c[0][1] + c[2][0] * c[2][0] + c[2][1] * c[2][1]
    q11 = c[1][0] * c[1][0] + c[1][1] * c[1][1] + c[3][0] * c[3][0] + c[3][1] * c[3][1]
    q01 = add(mul_conj(c[0], c[1]), mul_conj(c[2], c[3]))
    return q00, q11, q01


def station_terms(load, jp, jq):
    p = [(jp[k], jp[4 + k]) for k in range(4)]
    q = [(jq[k], jq[4 + k]) for k in range(4)]
    cross = {}
    for ab in range(4):
        for cd in range(4):
            cross[ab, cd] = (load(4 * ab + cd), load(16 + 4 * ab + cd))
    gp, gq = [], []
    for a in range(2):
        for d in range(2):
            gp.append(
                add(
                    *[
                        mul(cross[2 * a + b, 2 * d + c], q[2 * b + c])
                        for b in range(2)
                        for c in range(2)
                    ]
                )
            )
            gq.append(
                add(
                    *[
                        mul_conj(cross[2 * b + a, 2 * c + d], p[2 * b + c])
                        for b in range(2)
                        for c in range(2)
                    ]
                )
            )
    diag = [load(32 + k) for k in range(4)]
    off = {pair: (load(36 + 2 * n), load(37 + 2 * n)) for n, pair in enumerate(PAIRS)}
    q00, q11, q01 = outer(jq)
    two = scaled(q01, 2.0)
    hp = [
        diag[0] * q00 + diag[1] * q11 + mul_conj(conj(off[0, 1]), two)[0],
        diag[2] * q00 + diag[3] * q11 + mul_conj(conj(off[2, 3]), two)[0],
        *add(
            scaled(off[0, 2], q00),
            mul(off[0, 3], q01),
            mul_conj(q01, off[1, 2]),
            scaled(off[1, 3], q11),
        ),
    ]
    r00, r11, r01 = outer(jp)
    two = scaled(r01, 2.0)
    hq = [
        diag[0] * r00 + diag[2] * r11 + mul_conj(off[0, 2], two)[0],
        diag[1] * r00 + diag[3] * r11 + mul_conj(off[1, 3], two)[0],
        *add(
            scaled(conj(off[0, 1]), r00),
            mul_conj(off[0, 3], r01),
            mul_conj(r01, off[1, 2]),
            scaled(conj(off[2, 3]), r11),
        ),
    ]
    gp = [g[0] for g in gp] + [g[1] for g in gp]
    gq = [g[0] for g in gq] + [g[1] for g in gq]
    return gp, hp, gq, hq


def kernel(
    vis_hbm, mdl_hbm, start_hbm, pen_hbm, pairs_hbm, flags_hbm, chan_hbm,
    gains_out, coeff_out,
    vis, mdl, start, pen_in, pairs, flags, chan, ends,
    vf, mf, coef, half_out, mine, every, terms, sbuf, rbuf, prec, names, away, wsend, wrec,
    solved_now, final, basis, scale, pen, cons, dual, ginv,
    loc, ag_s, ag_r, rs_s, rs_r, ps_s, ps_r, one,
):
    band = lax.axis_index("band")
    base = lax.axis_index("base")
    core = base % 2
    chip = base // 2
    cz = chip // SIDE
    cx = chip % SIDE
    sibling = chip * 2 + (1 - core)

    def at(dz, dx):
        return ((cz + dz) % SIDE) * SIDE + (cx + dx) % SIDE

    def copy(src, dst, send, recv, band_to, base_to):
        return pltpu.make_async_remote_copy(
            src_ref=src, dst_ref=dst, send_sem=send, recv_sem=recv,
            device_id=(band_to, base_to), device_id_type=MESH,
        )

    local = [
        pltpu.make_async_copy(src, dst, loc.at[n])
        for n, (src, dst) in enumerate(
            [
                (start_hbm, start), (pairs_hbm, pairs), (flags_hbm, flags), (chan_hbm, chan),
                (pen_hbm, pen_in), (mdl_hbm, mdl), (vis_hbm, vis),
            ]
        )
    ]
    for c in local:
        c.start()

    barrier = pltpu.get_barrier_semaphore()

    def greet(band_to, base_to):
        pl.semaphore_signal(barrier, inc=1, device_id=(band_to, base_to), device_id_type=MESH)

    for dz, dx in FAR:
        for c in range(2):
            greet(band, 2 * at(dz, dx) + c)
    for d in (2, 1, 3):
        for c in range(2):
            greet((band + d) % BANDS, 2 * chip + c)
    greet(band, sibling)

    lane8 = iota((8, LANES), 1)
    row8 = iota((8, LANES), 0)
    for c in local[:5]:
        c.wait()
    mine[...] = start[...].reshape(8 * BLOCK, SOLS).T
    keep = pl.ds(pl.multiple_of(core * HALF, HALF), HALF)
    give = pl.ds(pl.multiple_of((1 - core) * HALF, HALF), HALF)
    every[0, base] = mine[keep, :]

    for t in range(TILES):
        for side in range(2):
            ends[t, side] = pairs[t, side]
    blocks = [pairs[t, side] for t in range(TILES) for side in range(2)]
    named = jnp.zeros((8, LANES), jnp.int32)
    for e, b in enumerate(blocks):
        named = jnp.where(row8 == e, b, named)
    names[0] = named
    cell = iota((1, CELLS), 1)
    eye = (cell // BLOCK == cell % BLOCK).astype(F32)
    weights = []
    for t in range(TILES):
        same = jnp.where(blocks[2 * t] == blocks[2 * t + 1], 1.0, 0.0)
        weights.append(flags[t : t + 1, :].astype(F32) * (1.0 - same * eye))
    both = jnp.concatenate([*weights, jnp.zeros((6, CELLS), F32)], axis=0).astype(BF16)
    fold_row = iota((CELLS, LANES), 0)
    fold_lane = iota((CELLS, LANES), 1) % BLOCK
    at_first = jnp.dot(
        both, (fold_row // BLOCK == fold_lane).astype(F32).astype(BF16),
        preferred_element_type=F32,
    )
    at_second = jnp.dot(
        both, (fold_row % BLOCK == fold_lane).astype(F32).astype(BF16),
        preferred_element_type=F32,
    )
    pen_row = jnp.concatenate([pen_in[...]] * 8, axis=1)
    away[0] = jnp.concatenate(
        [at_first[0:1], at_second[0:1], at_first[1:2], at_second[1:2], pen_row]
        + [jnp.zeros((3, LANES), F32)],
        axis=0,
    )

    pl.semaphore_wait(barrier, 2 * CHIPS - 1 + 2 * (BANDS - 1))

    for dz, dx in FAR:
        for c in range(2):
            copy(
                mine.at[pl.ds(HALF * c, HALF)], every.at[0, base], ag_s.at[0], ag_r.at[0],
                band, 2 * at(dz, dx) + c,
            ).start()
    copy(mine.at[give], every.at[0, base], ag_s.at[0], ag_r.at[0], band, sibling).start()
    names_copy = copy(names.at[0], names.at[1], one.at[0], one.at[1], band, sibling)
    away_copy = copy(away.at[0], away.at[1], one.at[2], one.at[3], band, sibling)
    names_copy.start()
    away_copy.start()

    row = iota((SOLS, CHANS), 0)
    sol = band * SOLS + ((row // HALF + core) % 2) * HALF + row % HALF
    member = (jnp.broadcast_to(chan[...], (SOLS, CHANS)) == sol).astype(F32)
    where_c = (band * CHANS + iota((SOLS, CHANS), 1)).astype(F32)
    xpos = -1.0 + (2.0 * where_c + 1.0) / (CHANS * BANDS)
    chans = jnp.sum(member, axis=1, keepdims=True)
    centre = jnp.sum(member * xpos, axis=1, keepdims=True) / chans
    centre = jnp.broadcast_to(centre[:HALF], (HALF, LANES))
    cheb = [jnp.ones_like(centre), centre]
    for _ in range(2, NPOLY):
        cheb.append(2.0 * centre * cheb[-1] - cheb[-2])
    for k in range(NPOLY):
        basis[k] = cheb[k]
    member2 = jnp.concatenate([member, member], axis=1).astype(BF16)

    for c in local[5:]:
        c.wait()

    def collapse(t, carry):
        w = jnp.where(t == 0, weights[0], weights[1])
        for k in range(8):
            vf[k] = vis[k, t].astype(F32)
            mf[k] = mdl[k, t].astype(F32) * w

        def put(n, product):
            high = product.astype(BF16)
            low = (product - high.astype(F32)).astype(BF16)
            out = jnp.dot(
                member2, jnp.concatenate([high, low], axis=0), preferred_element_type=F32
            )
            coef[t, n] = out[:HALF]
            half_out[t, n] = out[HALF:]

        for ab in range(4):
            vr, vi = vf[ab], vf[4 + ab]
            for cd in range(4):
                mr, mi = mf[cd], mf[4 + cd]
                put(4 * ab + cd, vr * mr + vi * mi)
                put(16 + 4 * ab + cd, vi * mr - vr * mi)
        for ab in range(4):
            put(32 + ab, mf[ab] * mf[ab] + mf[4 + ab] * mf[4 + ab])
        for n, (x, y) in enumerate(PAIRS):
            put(36 + 2 * n, mf[x] * mf[y] + mf[4 + x] * mf[4 + y])
            put(37 + 2 * n, mf[4 + x] * mf[y] - mf[x] * mf[4 + y])
        copy(half_out.at[t], coef.at[TILES + t], one.at[4], one.at[5], band, sibling).start()
        return carry

    lax.fori_loop(0, TILES, collapse, 0)

    names_copy.wait_recv()
    away_copy.wait_recv()
    for t in range(TILES):
        for side in range(2):
            ends[TILES + t, side] = names[1, 2 * t + side, 0]

    def weight_rows(k):
        out = jnp.zeros((8, LANES), F32)
        for own in range(2):
            for e in range(2 * TILES):
                hit = row8 + 2 * k == names[own, e : e + 1, :]
                at_end = jnp.broadcast_to(away[own, e : e + 1, :], (8, LANES))
                out = out + jnp.where(hit, at_end, 0.0)
        return out

    for dz, dx in FAR:
        k = at(dz, dx)
        wsend[k] = weight_rows(k)
        copy(
            wsend.at[k], wrec.at[chip], one.at[6], one.at[7], band, 2 * k + core
        ).start()
    wrec[chip] = weight_rows(chip)
    own_pen = jnp.broadcast_to(away[0, 4:5, :], (HALF, LANES))
    its_pen = jnp.broadcast_to(away[1, 4:5, :], (HALF, LANES))
    pen[0] = jnp.where(core == 0, own_pen, its_pen)
    pen[1] = jnp.where(core == 0, its_pen, own_pen)

    def arrived(ref, sem):
        pltpu.make_async_copy(ref, ref, sem).wait()

    arrived(half_out, one.at[5])

    def total_of(it, values):
        lane = iota((HALF, LANES), 1)
        columns = jnp.zeros((HALF, LANES), F32)
        for k in range(NPOLY):
            columns = jnp.where(lane == k, basis[k], columns)
        pad = [jnp.zeros((16 - NPOLY, LANES), F32)]
        out = []
        for part in (values[0], values[1], columns):
            out += [jnp.sum(basis[k] * part, axis=0, keepdims=True) for k in range(NPOLY)] + pad
        me = 2 * band + core
        prec[it, me] = jnp.concatenate(out, axis=0)

        def send(band_to, base_to):
            copy(
                prec.at[it, me], prec.at[it, me], ps_s.at[it], ps_r.at[it], band_to, base_to
            ).start()

        for d in (2, 1, 3):
            for c in range(2):
                send((band + d) % BANDS, 2 * chip + c)
        send(band, sibling)

    def coefficients(it, first):
        arrived(prec.at[it, pl.ds(0, 2 * BANDS - 1)], ps_r.at[it])
        total = functools.reduce(lambda a, b: a + b, [prec[it, k] for k in range(2 * BANDS)])

        def invert():
            r, l = iota((16, LANES), 0), iota((16, LANES), 1)
            m = total[32:, :] + jnp.where((r == l) & (r < NPOLY), RIDGE, 0.0)
            m = m + jnp.where((l == r + 16) & (r < NPOLY), 1.0, 0.0)
            for p in range(NPOLY):
                pivot = m[p : p + 1, :] / m[p : p + 1, p : p + 1]
                m = jnp.where(r == p, pivot, m - m[:, p : p + 1] * pivot)
            for k in range(NPOLY):
                ginv[k] = jnp.broadcast_to(m[:, 16 + k : 17 + k], (16, LANES))

        if first is not None:
            pl.when(first)(invert)
        out = []
        for b in range(2):
            rhs = total[16 * b : 16 * b + 16, :]
            x = ginv[0] * rhs[0:1, :]
            for k in range(1, NPOLY):
                x = x + ginv[k] * rhs[k : k + 1, :]
            out.append(x)
        return out

    lane = iota((HALF, LANES), 1)
    inner = lane % BLOCK

    def natural(l):
        return (l % 8) * BLOCK + ((l % BLOCK) // 8) * 8 + l // BLOCK

    own_blocks = pl.ds(2 * chip, 2)

    def iteration(it, carry):
        @pl.when(it > 0)
        def _():
            every[it, own_blocks] = solved_now[...]
            for dz, dx in FAR:
                copy(
                    every.at[it, own_blocks], every.at[it, own_blocks], ag_s.at[it], ag_r.at[it],
                    band, 2 * at(dz, dx) + core,
                ).start()
            coeff = coefficients(it - 1, it == 1)
            for b in range(2):
                agreed = basis[0] * coeff[b][0:1, :]
                for k in range(1, NPOLY):
                    agreed = agreed + basis[k] * coeff[b][k : k + 1, :]
                dual[b] = dual[b] + solved_now[b] - agreed
                cons[b] = agreed
            arrived(every.at[it, pl.ds(0, 2 * CHIPS - 2)], ag_r.at[it])

        @pl.when(it == 0)
        def _():
            arrived(every.at[0, pl.ds(0, 2 * CHIPS - 1)], ag_r.at[0])
            cons[...] = every[0, own_blocks]
            dual[...] = jnp.zeros((2, HALF, LANES), F32)

        def tile(t, carry):
            of_p = every[it, ends[t, 0]]
            of_q = every[it, ends[t, 1]]
            jq = [lanes(of_q, k * BLOCK + inner) for k in range(8)]
            gp, hp, gq, hq = [], [], [], []
            for half in range(2):
                jp = [lanes(of_p, k * BLOCK + half * 8 + lane // BLOCK) for k in range(8)]

                def load(n):
                    return coef[t, n, :, pl.ds(half * LANES, LANES)]

                a, b, c, d = station_terms(load, jp, jq)
                gp += a
                hp += b
                gq.append(c)
                hq.append(d)
            terms[2 * t, pl.ds(0, HALF), :] = lanes(merge_all(gp, lane, 8), natural(lane))
            summed = [x + y for x, y in zip(gq[0], gq[1])]
            terms[2 * t + 1, pl.ds(0, HALF), :] = merge_all(summed, lane, 64)
            summed = [x + y for x, y in zip(hq[0], hq[1])]
            rows = pl.ds(HALF, 8)
            arrays = [x[:8] for x in hp[:4]] + [x[8:] for x in hp[:4]]
            arrays += [x[:8] for x in hp[4:]] + [x[8:] for x in hp[4:]]
            terms[2 * t, rows, :] = lanes(merge_all(arrays, lane8, 8), natural(lane8))
            arrays = [x[:8] for x in summed] + [x[8:] for x in summed]
            terms[2 * t + 1, rows, :] = merge_all(arrays, lane8, 64)
            return carry

        lax.fori_loop(0, 2 * TILES, tile, 0)

        def share(k):
            out = [jnp.zeros((ROWS, LANES), F32) for _ in range(2)]
            for own in range(2):
                for e in range(2 * TILES):
                    held = terms[2 * TILES * own + e]
                    for b in range(2):
                        hit = jnp.where(names[own, e : e + 1, :] == 2 * k + b, 1.0, 0.0)
                        out[b] = out[b] + hit * held
            return out

        for dz, dx in FAR:
            k = at(dz, dx)
            out = share(k)
            sbuf[it, k, 0] = out[0]
            sbuf[it, k, 1] = out[1]
            copy(
                sbuf.at[it, k], rbuf.at[it, chip], rs_s.at[it], rs_r.at[it], band, 2 * k + core
            ).start()
        out = share(chip)
        rbuf[it, chip, 0] = out[0]
        rbuf[it, chip, 1] = out[1]

        @pl.when(it == 0)
        def _():
            arrived(wrec.at[pl.ds(0, CHIPS - 1)], one.at[7])
            total = functools.reduce(lambda a, b: a + b, [wrec[k] for k in range(CHIPS)])
            for b in range(2):
                at_station = jnp.broadcast_to(total[b : b + 1, :], (HALF, LANES))
                scale[b] = 1.0 / jnp.maximum(chans[:HALF] * at_station, 1.0)

        arrived(rbuf.at[it, pl.ds(0, CHIPS - 1)], rs_r.at[it])

        part = lane % BLOCK
        upper = (lane & BLOCK) != 0
        sign = jnp.where(upper == (lane < 64), 1.0, -1.0)
        result = []
        for b in range(2):
            normal = functools.reduce(lambda x, y: x + y, [rbuf[it, k, b] for k in range(CHIPS)])
            packed = normal[HALF:, :]
            outer_part = jnp.concatenate([packed, pltpu.roll(packed, 64, 1)], axis=0)
            per = scale[b]
            rho = pen[b]
            rhs = normal[:HALF, :] * per + rho * (cons[b] - dual[b])
            h_diag = lanes(outer_part, jnp.where(upper, part, BLOCK + part)) * per + rho
            h_real = lanes(outer_part, 2 * BLOCK + part) * per
            h_imag = lanes(outer_part, 3 * BLOCK + part) * per
            determ = h_diag * lanes(h_diag, lane ^ BLOCK) - h_real * h_real - h_imag * h_imag
            solved = (
                rhs * h_diag
                - lanes(rhs, lane ^ BLOCK) * h_real
                + sign * lanes(rhs, lane ^ (64 + BLOCK)) * h_imag
            ) / determ
            solved_now[b] = solved
            result.append(solved + dual[b])
        total_of(it, result)
        return carry

    lax.fori_loop(0, ITERS, iteration, 0)

    final_copy = copy(
        solved_now.at[1 - core], final.at[core], one.at[8], one.at[9], band, sibling
    )
    final_copy.start()
    final[core] = solved_now[core]
    final_copy.wait_recv()
    gains = jnp.concatenate([final[0], final[1]], axis=0)
    for k in range(8):
        gains_out[k] = gains[:, k * BLOCK : (k + 1) * BLOCK]
    pair = coefficients(ITERS - 1, None)
    coeff = jnp.where(core == 0, pair[0], pair[1])
    for k in range(8):
        coeff_out[k] = coeff[:NPOLY, k * BLOCK : (k + 1) * BLOCK]

    names_copy.wait_send()
    away_copy.wait_send()
    final_copy.wait_send()
    arrived(half_out, one.at[4])
    arrived(wsend.at[pl.ds(0, CHIPS - 1)], one.at[6])
    arrived(every.at[0, pl.ds(0, 2 * CHIPS - 1)], ag_s.at[0])
    for it in range(ITERS):
        if it > 0:
            arrived(every.at[it, pl.ds(0, 2 * CHIPS - 2)], ag_s.at[it])
        arrived(sbuf.at[it, pl.ds(0, CHIPS - 1)], rs_s.at[it])
        arrived(prec.at[it, pl.ds(0, 2 * BANDS - 1)], ps_s.at[it])


def on_device(visibilities, model, start_gains, penalty, pairs, flags, chan_band):
    vmem, dma = pltpu.VMEM, pltpu.SemaphoreType.DMA
    gains, coeff = pl.pallas_call(
        kernel,
        out_shape=(
            jax.ShapeDtypeStruct((8, SOLS, BLOCK), F32),
            jax.ShapeDtypeStruct((8, NPOLY, BLOCK), F32),
        ),
        in_specs=[pl.BlockSpec(memory_space=pltpu.HBM)] * 7,
        out_specs=(pl.BlockSpec(memory_space=vmem), pl.BlockSpec(memory_space=vmem)),
        scratch_shapes=[
            vmem((8, TILES, CHANS, CELLS), BF16),
            vmem((8, TILES, CHANS, CELLS), BF16),
            vmem((8, BLOCK, SOLS), F32),
            vmem((1, BLOCK), F32),
            pltpu.SMEM((TILES, 2), jnp.int32),
            vmem((TILES, CELLS), jnp.int32),
            vmem((1, CHANS), jnp.int32),
            pltpu.SMEM((2 * TILES, 2), jnp.int32),
            vmem((8, CHANS, CELLS), F32),
            vmem((8, CHANS, CELLS), F32),
            vmem((2 * TILES, NCOEF, HALF, CELLS), F32),
            vmem((TILES, NCOEF, HALF, CELLS), F32),
            vmem((SOLS, LANES), F32),
            vmem((ITERS, 2 * CHIPS, HALF, LANES), F32),
            vmem((4 * TILES, ROWS, LANES), F32),
            vmem((ITERS, CHIPS, 2, ROWS, LANES), F32),
            vmem((ITERS, CHIPS, 2, ROWS, LANES), F32),
            vmem((ITERS, 2 * BANDS, 48, LANES), F32),
            vmem((2, 8, LANES), jnp.int32),
            vmem((2, 8, LANES), F32),
            vmem((CHIPS, 8, LANES), F32),
            vmem((CHIPS, 8, LANES), F32),
            vmem((2, HALF, LANES), F32),
            vmem((2, HALF, LANES), F32),
            vmem((NPOLY, HALF, LANES), F32),
            vmem((2, HALF, LANES), F32),
            vmem((2, HALF, LANES), F32),
            vmem((2, HALF, LANES), F32),
            vmem((2, HALF, LANES), F32),
            vmem((NPOLY, 16, LANES), F32),
            dma((7,)),
            *[dma((ITERS,))] * 6,
            dma((10,)),
        ],
        compiler_params=pltpu.CompilerParams(
            collective_id=0, has_side_effects=True, vmem_limit_bytes=40 * 1024 * 1024
        ),
        cost_estimate=pl.CostEstimate(
            flops=60_000_000, bytes_accessed=3_000_000, transcendentals=0
        ),
        name="admm",
    )(
        visibilities, model, jnp.swapaxes(start_gains, 1, 2), penalty.reshape(1, BLOCK), pairs, flags,
        chan_band.reshape(1, CHANS),
    )
    return gains, coeff


def solution(mesh):
    in_specs = (
        P(None, "base", "band", None),
        P(None, "base", "band", None),
        P(None, "band", "base"),
        P("base"),
        P("base", None),
        P("base", None),
        P("band"),
    )
    out_specs = (P(None, "band", "base"), P(None, None, "base"))
    return jax.shard_map(
        on_device, mesh=mesh, in_specs=in_specs, out_specs=out_specs, check_vma=False
    )
```

```python
import functools

import jax
import jax.numpy as jnp
from jax import lax
from jax.experimental import pallas as pl
from jax.experimental.pallas import tpu as pltpu
from jax.sharding import PartitionSpec as P

BLOCK = 16
NPOLY = 9
ITERS = 3
RIDGE = 0.5
MESH = pl.DeviceIdType.MESH
F32 = jnp.float32
BF16 = jnp.bfloat16
SIDE = 4
CHIPS = SIDE * SIDE
BANDS = 4
TILES = 2
CHANS = 64
CELLS = BLOCK * BLOCK
SOLS = 32
LANES = 128
HALF = SOLS // 2
ROWS = HALF + HALF // 2
FAR = sorted(
    [(dz, dx) for dz in range(SIDE) for dx in range(SIDE) if dz or dx],
    key=lambda d: -sum(min(n, SIDE - n) for n in d),
)
NCOEF = 48
PAIRS = [(0, 1), (0, 2), (0, 3), (1, 2), (1, 3), (2, 3)]


def lanes(x, idx):
    numbers = lax.GatherDimensionNumbers(
        offset_dims=(),
        collapsed_slice_dims=(1,),
        start_index_map=(1,),
        operand_batching_dims=(0,),
        start_indices_batching_dims=(0,),
    )
    return lax.gather(
        x, idx[..., None], numbers, (1, 1), mode=lax.GatherScatterMode.PROMISE_IN_BOUNDS
    )


def iota(shape, axis):
    return lax.broadcasted_iota(jnp.int32, shape, axis)


def merge(a, b, lane, bit):
    clear = (lane & bit) == 0
    return jnp.where(clear, a, b) + lanes(jnp.where(clear, b, a), lane ^ bit)


def merge_all(arrays, lane, top):
    bit = top
    while len(arrays) > 1:
        half = len(arrays) // 2
        arrays = [merge(a, b, lane, bit) for a, b in zip(arrays[:half], arrays[half:])]
        bit //= 2
    return arrays[0]


def mul(a, b):
    return (a[0] * b[0] - a[1] * b[1], a[0] * b[1] + a[1] * b[0])


def mul_conj(a, b):
    return (a[0] * b[0] + a[1] * b[1], a[0] * b[1] - a[1] * b[0])


def conj(a):
    return (a[0], -a[1])


def add(*terms):
    re, im = terms[0]
    for t in terms[1:]:
        re, im = re + t[0], im + t[1]
    return (re, im)


def scaled(a, r):
    return (a[0] * r, a[1] * r)


def outer(j):
    c = [(j[k], j[4 + k]) for k in range(4)]
    q00 = c[0][0] * c[0][0] + c[0][1] * c[0][1] + c[2][0] * c[2][0] + c[2][1] * c[2][1]
    q11 = c[1][0] * c[1][0] + c[1][1] * c[1][1] + c[3][0] * c[3][0] + c[3][1] * c[3][1]
    q01 = add(mul_conj(c[0], c[1]), mul_conj(c[2], c[3]))
    return q00, q11, q01


def station_terms(load, jp, jq):
    p = [(jp[k], jp[4 + k]) for k in range(4)]
    q = [(jq[k], jq[4 + k]) for k in range(4)]
    cross = {}
    for ab in range(4):
        for cd in range(4):
            cross[ab, cd] = (load(4 * ab + cd), load(16 + 4 * ab + cd))
    gp, gq = [], []
    for a in range(2):
        for d in range(2):
            gp.append(
                add(
                    *[
                        mul(cross[2 * a + b, 2 * d + c], q[2 * b + c])
                        for b in range(2)
                        for c in range(2)
                    ]
                )
            )
            gq.append(
                add(
                    *[
                        mul_conj(cross[2 * b + a, 2 * c + d], p[2 * b + c])
                        for b in range(2)
                        for c in range(2)
                    ]
                )
            )
    diag = [load(32 + k) for k in range(4)]
    off = {pair: (load(36 + 2 * n), load(37 + 2 * n)) for n, pair in enumerate(PAIRS)}
    q00, q11, q01 = outer(jq)
    two = scaled(q01, 2.0)
    hp = [
        diag[0] * q00 + diag[1] * q11 + mul_conj(conj(off[0, 1]), two)[0],
        diag[2] * q00 + diag[3] * q11 + mul_conj(conj(off[2, 3]), two)[0],
        *add(
            scaled(off[0, 2], q00),
            mul(off[0, 3], q01),
            mul_conj(q01, off[1, 2]),
            scaled(off[1, 3], q11),
        ),
    ]
    r00, r11, r01 = outer(jp)
    two = scaled(r01, 2.0)
    hq = [
        diag[0] * r00 + diag[2] * r11 + mul_conj(off[0, 2], two)[0],
        diag[1] * r00 + diag[3] * r11 + mul_conj(off[1, 3], two)[0],
        *add(
            scaled(conj(off[0, 1]), r00),
            mul_conj(off[0, 3], r01),
            mul_conj(r01, off[1, 2]),
            scaled(conj(off[2, 3]), r11),
        ),
    ]
    gp = [g[0] for g in gp] + [g[1] for g in gp]
    gq = [g[0] for g in gq] + [g[1] for g in gq]
    return gp, hp, gq, hq


def kernel(
    vis_hbm, mdl_hbm, start_hbm, pen_hbm, pairs_hbm, flags_hbm, chan_hbm,
    gains_out, coeff_out,
    vis, mdl, start, pen_in, pairs, flags, chan, ends,
    vf, mf, coef, half_out, mine, every, terms, sbuf, rbuf, prec, names, away, wsend, wrec,
    mixed, final, last, basis, scale, pen, cons, dual, ginv,
    loc, ag_s, ag_r, rs_s, rs_r, ps_s, ps_r, one,
):
    band = lax.axis_index("band")
    base = lax.axis_index("base")
    core = base % 2
    chip = base // 2
    cz = chip // SIDE
    cx = chip % SIDE
    sibling = chip * 2 + (1 - core)

    def at(dz, dx):
        return ((cz + dz) % SIDE) * SIDE + (cx + dx) % SIDE

    def copy(src, dst, send, recv, band_to, base_to):
        return pltpu.make_async_remote_copy(
            src_ref=src, dst_ref=dst, send_sem=send, recv_sem=recv,
            device_id=(band_to, base_to), device_id_type=MESH,
        )

    local = [
        pltpu.make_async_copy(src, dst, loc.at[n])
        for n, (src, dst) in enumerate(
            [
                (start_hbm, start), (pairs_hbm, pairs), (flags_hbm, flags), (chan_hbm, chan),
                (pen_hbm, pen_in), (mdl_hbm, mdl), (vis_hbm, vis),
            ]
        )
    ]
    for c in local:
        c.start()

    barrier = pltpu.get_barrier_semaphore()

    def greet(band_to, base_to):
        pl.semaphore_signal(barrier, inc=1, device_id=(band_to, base_to), device_id_type=MESH)

    for dz, dx in FAR:
        for c in range(2):
            greet(band, 2 * at(dz, dx) + c)
    for d in (2, 1, 3):
        for c in range(2):
            greet((band + d) % BANDS, 2 * chip + c)
    greet(band, sibling)

    lane8 = iota((8, LANES), 1)
    row8 = iota((8, LANES), 0)
    for c in local[:5]:
        c.wait()
    mine[...] = start[...].reshape(8 * BLOCK, SOLS).T
    keep = pl.ds(pl.multiple_of(core * HALF, HALF), HALF)
    give = pl.ds(pl.multiple_of((1 - core) * HALF, HALF), HALF)
    every[0, base] = mine[keep, :]

    for t in range(TILES):
        for side in range(2):
            ends[t, side] = pairs[t, side]
    blocks = [pairs[t, side] for t in range(TILES) for side in range(2)]
    named = jnp.zeros((8, LANES), jnp.int32)
    for e, b in enumerate(blocks):
        named = jnp.where(row8 == e, b, named)
    names[0] = named
    cell = iota((1, CELLS), 1)
    eye = (cell // BLOCK == cell % BLOCK).astype(F32)
    weights = []
    for t in range(TILES):
        same = jnp.where(blocks[2 * t] == blocks[2 * t + 1], 1.0, 0.0)
        weights.append(flags[t : t + 1, :].astype(F32) * (1.0 - same * eye))
    both = jnp.concatenate([*weights, jnp.zeros((6, CELLS), F32)], axis=0).astype(BF16)
    fold_row = iota((CELLS, LANES), 0)
    fold_lane = iota((CELLS, LANES), 1) % BLOCK
    at_first = jnp.dot(
        both, (fold_row // BLOCK == fold_lane).astype(F32).astype(BF16),
        preferred_element_type=F32,
    )
    at_second = jnp.dot(
        both, (fold_row % BLOCK == fold_lane).astype(F32).astype(BF16),
        preferred_element_type=F32,
    )
    pen_row = jnp.concatenate([pen_in[...]] * 8, axis=1)
    away[0] = jnp.concatenate(
        [at_first[0:1], at_second[0:1], at_first[1:2], at_second[1:2], pen_row]
        + [jnp.zeros((3, LANES), F32)],
        axis=0,
    )

    pl.semaphore_wait(barrier, 2 * CHIPS - 1 + 2 * (BANDS - 1))

    for dz, dx in FAR:
        for c in range(2):
            copy(
                mine.at[pl.ds(HALF * c, HALF)], every.at[0, base], ag_s.at[0], ag_r.at[0],
                band, 2 * at(dz, dx) + c,
            ).start()
    copy(mine.at[give], every.at[0, base], ag_s.at[0], ag_r.at[0], band, sibling).start()
    names_copy = copy(names.at[0], names.at[1], one.at[0], one.at[1], band, sibling)
    away_copy = copy(away.at[0], away.at[1], one.at[2], one.at[3], band, sibling)
    names_copy.start()
    away_copy.start()

    row = iota((SOLS, CHANS), 0)
    sol = band * SOLS + ((row // HALF + core) % 2) * HALF + row % HALF
    member = (jnp.broadcast_to(chan[...], (SOLS, CHANS)) == sol).astype(F32)
    where_c = (band * CHANS + iota((SOLS, CHANS), 1)).astype(F32)
    xpos = -1.0 + (2.0 * where_c + 1.0) / (CHANS * BANDS)
    chans = jnp.sum(member, axis=1, keepdims=True)
    centre = jnp.sum(member * xpos, axis=1, keepdims=True) / chans
    centre = jnp.broadcast_to(centre[:HALF], (HALF, LANES))
    cheb = [jnp.ones_like(centre), centre]
    for _ in range(2, NPOLY):
        cheb.append(2.0 * centre * cheb[-1] - cheb[-2])
    for k in range(NPOLY):
        basis[k] = cheb[k]
    member2 = jnp.concatenate([member, member], axis=1).astype(BF16)

    for c in local[5:]:
        c.wait()

    def collapse(t, carry):
        w = jnp.where(t == 0, weights[0], weights[1])
        for k in range(8):
            vf[k] = vis[k, t].astype(F32)
            mf[k] = mdl[k, t].astype(F32) * w

        def put(n, product):
            high = product.astype(BF16)
            low = (product - high.astype(F32)).astype(BF16)
            out = jnp.dot(
                member2, jnp.concatenate([high, low], axis=0), preferred_element_type=F32
            )
            coef[t, n] = out[:HALF]
            half_out[t, n] = out[HALF:]

        for ab in range(4):
            vr, vi = vf[ab], vf[4 + ab]
            for cd in range(4):
                mr, mi = mf[cd], mf[4 + cd]
                put(4 * ab + cd, vr * mr + vi * mi)
                put(16 + 4 * ab + cd, vi * mr - vr * mi)
        for ab in range(4):
            put(32 + ab, mf[ab] * mf[ab] + mf[4 + ab] * mf[4 + ab])
        for n, (x, y) in enumerate(PAIRS):
            put(36 + 2 * n, mf[x] * mf[y] + mf[4 + x] * mf[4 + y])
            put(37 + 2 * n, mf[4 + x] * mf[y] - mf[x] * mf[4 + y])
        copy(half_out.at[t], coef.at[TILES + t], one.at[4], one.at[5], band, sibling).start()
        return carry

    lax.fori_loop(0, TILES, collapse, 0)

    names_copy.wait_recv()
    away_copy.wait_recv()
    for t in range(TILES):
        for side in range(2):
            ends[TILES + t, side] = names[1, 2 * t + side, 0]

    def weight_rows(k):
        out = jnp.zeros((8, LANES), F32)
        for own in range(2):
            for e in range(2 * TILES):
                hit = row8 + 2 * k == names[own, e : e + 1, :]
                at_end = jnp.broadcast_to(away[own, e : e + 1, :], (8, LANES))
                out = out + jnp.where(hit, at_end, 0.0)
        return out

    for dz, dx in FAR:
        k = at(dz, dx)
        wsend[k] = weight_rows(k)
        copy(
            wsend.at[k], wrec.at[chip], one.at[6], one.at[7], band, 2 * k + core
        ).start()
    wrec[chip] = weight_rows(chip)
    own_pen = jnp.broadcast_to(away[0, 4:5, :], (HALF, LANES))
    its_pen = jnp.broadcast_to(away[1, 4:5, :], (HALF, LANES))
    pen[0] = jnp.where(core == 0, own_pen, its_pen)
    pen[1] = jnp.where(core == 0, its_pen, own_pen)

    def arrived(ref, sem):
        pltpu.make_async_copy(ref, ref, sem).wait()

    arrived(half_out, one.at[5])

    pad = [jnp.zeros((16 - NPOLY, LANES), F32)]
    me = 2 * band + core

    def along_basis(part):
        return [jnp.sum(basis[k] * part, axis=0, keepdims=True) for k in range(NPOLY)] + pad

    def total_of(it):
        column = iota((HALF, LANES), 1)
        columns = jnp.zeros((HALF, LANES), F32)
        for k in range(NPOLY):
            columns = jnp.where(column == k, basis[k], columns)
        out = along_basis(mixed[0]) + along_basis(mixed[1]) + along_basis(columns)
        prec[it, me] = jnp.concatenate(out, axis=0)

        def send(band_to, base_to):
            copy(
                prec.at[it, me], prec.at[it, me], ps_s.at[it], ps_r.at[it], band_to, base_to
            ).start()

        for d in (2, 1, 3):
            for c in range(2):
                send((band + d) % BANDS, 2 * chip + c)
        send(band, sibling)

    def total_at(it):
        arrived(prec.at[it, pl.ds(0, 2 * BANDS - 1)], ps_r.at[it])
        return functools.reduce(lambda a, b: a + b, [prec[it, k] for k in range(2 * BANDS)])

    def solve_gram(rhs):
        x = ginv[0] * rhs[0:1, :]
        for k in range(1, NPOLY):
            x = x + ginv[k] * rhs[k : k + 1, :]
        return x

    def from_total(total, first):
        @pl.when(first)
        def _():
            r, l = iota((16, LANES), 0), iota((16, LANES), 1)
            m = total[32:, :] + jnp.where((r == l) & (r < NPOLY), RIDGE, 0.0)
            m = m + jnp.where((l == r + 16) & (r < NPOLY), 1.0, 0.0)
            for p in range(NPOLY):
                pivot = m[p : p + 1, :] / m[p : p + 1, p : p + 1]
                m = jnp.where(r == p, pivot, m - m[:, p : p + 1] * pivot)
            for k in range(NPOLY):
                ginv[k] = jnp.broadcast_to(m[:, 16 + k : 17 + k], (16, LANES))

        return [solve_gram(total[16 * b : 16 * b + 16, :]) for b in range(2)]

    lane = iota((HALF, LANES), 1)
    inner = lane % BLOCK

    def natural(l):
        return (l % 8) * BLOCK + ((l % BLOCK) // 8) * 8 + l // BLOCK

    own_blocks = pl.ds(2 * chip, 2)

    def iteration(it, carry):
        @pl.when(it > 0)
        def _():
            coeff = from_total(total_at(it - 1), it == 1)
            for b in range(2):
                agreed = basis[0] * coeff[b][0:1, :]
                for k in range(1, NPOLY):
                    agreed = agreed + basis[k] * coeff[b][k : k + 1, :]
                dual[b] = mixed[b] - agreed
                cons[b] = agreed
            arrived(every.at[it, pl.ds(0, 2 * CHIPS - 2)], ag_r.at[it])

        @pl.when(it == 0)
        def _():
            arrived(every.at[0, pl.ds(0, 2 * CHIPS - 1)], ag_r.at[0])
            cons[...] = every[0, own_blocks]
            dual[...] = jnp.zeros((2, HALF, LANES), F32)

        def tile(t, carry):
            of_p = every[it, ends[t, 0]]
            of_q = every[it, ends[t, 1]]
            jq = [lanes(of_q, k * BLOCK + inner) for k in range(8)]
            gp, hp, gq, hq = [], [], [], []
            for half in range(2):
                jp = [lanes(of_p, k * BLOCK + half * 8 + lane // BLOCK) for k in range(8)]

                def load(n):
                    return coef[t, n, :, pl.ds(half * LANES, LANES)]

                a, b, c, d = station_terms(load, jp, jq)
                gp += a
                hp += b
                gq.append(c)
                hq.append(d)
            terms[2 * t, pl.ds(0, HALF), :] = lanes(merge_all(gp, lane, 8), natural(lane))
            summed = [x + y for x, y in zip(gq[0], gq[1])]
            terms[2 * t + 1, pl.ds(0, HALF), :] = merge_all(summed, lane, 64)
            summed = [x + y for x, y in zip(hq[0], hq[1])]
            rows = pl.ds(HALF, 8)
            arrays = [x[:8] for x in hp[:4]] + [x[8:] for x in hp[:4]]
            arrays += [x[:8] for x in hp[4:]] + [x[8:] for x in hp[4:]]
            terms[2 * t, rows, :] = lanes(merge_all(arrays, lane8, 8), natural(lane8))
            arrays = [x[:8] for x in summed] + [x[8:] for x in summed]
            terms[2 * t + 1, rows, :] = merge_all(arrays, lane8, 64)
            return carry

        lax.fori_loop(0, 2 * TILES, tile, 0, unroll=2)

        def share(k):
            out = [jnp.zeros((ROWS, LANES), F32) for _ in range(2)]
            for own in range(2):
                for e in range(2 * TILES):
                    held = terms[2 * TILES * own + e]
                    for b in range(2):
                        hit = jnp.where(names[own, e : e + 1, :] == 2 * k + b, 1.0, 0.0)
                        out[b] = out[b] + hit * held
            return out

        for dz, dx in FAR:
            k = at(dz, dx)
            out = share(k)
            sbuf[it, k, 0] = out[0]
            sbuf[it, k, 1] = out[1]
            copy(
                sbuf.at[it, k], rbuf.at[it, chip], rs_s.at[it], rs_r.at[it], band, 2 * k + core
            ).start()
        out = share(chip)
        rbuf[it, chip, 0] = out[0]
        rbuf[it, chip, 1] = out[1]

        @pl.when(it == 0)
        def _():
            arrived(wrec.at[pl.ds(0, CHIPS - 1)], one.at[7])
            total = functools.reduce(lambda a, b: a + b, [wrec[k] for k in range(CHIPS)])
            for b in range(2):
                at_station = jnp.broadcast_to(total[b : b + 1, :], (HALF, LANES))
                scale[b] = 1.0 / jnp.maximum(chans[:HALF] * at_station, 1.0)

        arrived(rbuf.at[it, pl.ds(0, CHIPS - 1)], rs_r.at[it])

        part = lane % BLOCK
        upper = (lane & BLOCK) != 0
        sign = jnp.where(upper == (lane < 64), 1.0, -1.0)
        result = []
        for b in range(2):
            normal = functools.reduce(lambda x, y: x + y, [rbuf[it, k, b] for k in range(CHIPS)])
            packed = normal[HALF:, :]
            outer_part = jnp.concatenate([packed, pltpu.roll(packed, 64, 1)], axis=0)
            per = scale[b]
            rho = pen[b]
            rhs = normal[:HALF, :] * per + rho * (cons[b] - dual[b])
            h_diag = lanes(outer_part, jnp.where(upper, part, BLOCK + part)) * per + rho
            h_real = lanes(outer_part, 2 * BLOCK + part) * per
            h_imag = lanes(outer_part, 3 * BLOCK + part) * per
            determ = h_diag * lanes(h_diag, lane ^ BLOCK) - h_real * h_real - h_imag * h_imag
            solved = (
                rhs * h_diag
                - lanes(rhs, lane ^ BLOCK) * h_real
                + sign * lanes(rhs, lane ^ (64 + BLOCK)) * h_imag
            ) / determ
            every[it + 1, 2 * chip + b] = solved
            result.append(solved)

        @pl.when(it + 1 < ITERS)
        def _():
            for dz, dx in FAR:
                copy(
                    every.at[it + 1, own_blocks], every.at[it + 1, own_blocks],
                    ag_s.at[it + 1], ag_r.at[it + 1], band, 2 * at(dz, dx) + core,
                ).start()

        for b in range(2):
            mixed[b] = result[b] + dual[b]

        @pl.when(it + 1 < ITERS)
        def _():
            total_of(it)

        return carry

    lax.fori_loop(0, ITERS, iteration, 0)

    for c in range(2):
        last[c] = jnp.concatenate(along_basis(mixed[c]), axis=0)

    def send_last(c, band_to, base_to):
        copy(
            last.at[c], last.at[2 + me], one.at[10], one.at[11], band_to, base_to
        ).start()

    for d in (2, 1, 3):
        for c in range(2):
            send_last(c, (band + d) % BANDS, 2 * chip + c)
    send_last(1 - core, band, sibling)
    final_copy = copy(
        every.at[ITERS, sibling], final.at[core], one.at[8], one.at[9], band, sibling
    )
    final_copy.start()
    last[2 + me] = last[core]
    final[core] = every[ITERS, base]
    final_copy.wait_recv()
    gains = jnp.concatenate([final[0], final[1]], axis=0)
    gains_out[...] = gains.T.reshape(8, BLOCK, SOLS)
    arrived(last.at[pl.ds(0, 2 * BANDS - 1)], one.at[11])
    coeff = solve_gram(
        functools.reduce(lambda a, b: a + b, [last[2 + k] for k in range(2 * BANDS)])
    )
    for k in range(8):
        coeff_out[:, k, :] = coeff[:NPOLY, k * BLOCK : (k + 1) * BLOCK]

    names_copy.wait_send()
    away_copy.wait_send()
    final_copy.wait_send()
    arrived(half_out, one.at[4])
    arrived(wsend.at[pl.ds(0, CHIPS - 1)], one.at[6])
    arrived(every.at[0, pl.ds(0, 2 * CHIPS - 1)], ag_s.at[0])
    for it in range(ITERS):
        if it > 0:
            arrived(every.at[it, pl.ds(0, 2 * CHIPS - 2)], ag_s.at[it])
        arrived(sbuf.at[it, pl.ds(0, CHIPS - 1)], rs_s.at[it])
        if it + 1 < ITERS:
            arrived(prec.at[it, pl.ds(0, 2 * BANDS - 1)], ps_s.at[it])
    arrived(last.at[pl.ds(0, 2 * BANDS - 1)], one.at[10])


def on_device(visibilities, model, start_gains, penalty, pairs, flags, chan_band):
    vmem, dma = pltpu.VMEM, pltpu.SemaphoreType.DMA
    gains, coeff = pl.pallas_call(
        kernel,
        out_shape=(
            jax.ShapeDtypeStruct((8, BLOCK, SOLS), F32),
            jax.ShapeDtypeStruct((NPOLY, 8, BLOCK), F32),
        ),
        in_specs=[pl.BlockSpec(memory_space=pltpu.HBM)] * 7,
        out_specs=(pl.BlockSpec(memory_space=vmem), pl.BlockSpec(memory_space=vmem)),
        scratch_shapes=[
            vmem((8, TILES, CHANS, CELLS), BF16),
            vmem((8, TILES, CHANS, CELLS), BF16),
            vmem((8, BLOCK, SOLS), F32),
            vmem((1, BLOCK), F32),
            pltpu.SMEM((TILES, 2), jnp.int32),
            vmem((TILES, CELLS), jnp.int32),
            vmem((1, CHANS), jnp.int32),
            pltpu.SMEM((2 * TILES, 2), jnp.int32),
            vmem((8, CHANS, CELLS), F32),
            vmem((8, CHANS, CELLS), F32),
            vmem((2 * TILES, NCOEF, HALF, CELLS), F32),
            vmem((TILES, NCOEF, HALF, CELLS), F32),
            vmem((SOLS, LANES), F32),
            vmem((ITERS + 1, 2 * CHIPS, HALF, LANES), F32),
            vmem((4 * TILES, ROWS, LANES), F32),
            vmem((ITERS, CHIPS, 2, ROWS, LANES), F32),
            vmem((ITERS, CHIPS, 2, ROWS, LANES), F32),
            vmem((ITERS, 2 * BANDS, 48, LANES), F32),
            vmem((2, 8, LANES), jnp.int32),
            vmem((2, 8, LANES), F32),
            vmem((CHIPS, 8, LANES), F32),
            vmem((CHIPS, 8, LANES), F32),
            vmem((2, HALF, LANES), F32),
            vmem((2, HALF, LANES), F32),
            vmem((2 + 2 * BANDS, 16, LANES), F32),
            vmem((NPOLY, HALF, LANES), F32),
            vmem((2, HALF, LANES), F32),
            vmem((2, HALF, LANES), F32),
            vmem((2, HALF, LANES), F32),
            vmem((2, HALF, LANES), F32),
            vmem((NPOLY, 16, LANES), F32),
            dma((7,)),
            *[dma((ITERS,))] * 6,
            dma((12,)),
        ],
        compiler_params=pltpu.CompilerParams(
            collective_id=0, has_side_effects=True, vmem_limit_bytes=60 * 1024 * 1024
        ),
        cost_estimate=pl.CostEstimate(
            flops=60_000_000, bytes_accessed=3_000_000, transcendentals=0
        ),
        name="admm",
    )(
        visibilities, model, jnp.swapaxes(start_gains, 1, 2), penalty.reshape(1, BLOCK), pairs, flags,
        chan_band.reshape(1, CHANS),
    )
    return jnp.swapaxes(gains, 1, 2), jnp.swapaxes(coeff, 0, 1)


def solution(mesh):
    in_specs = (
        P(None, "base", "band", None),
        P(None, "base", "band", None),
        P(None, "band", "base"),
        P("base"),
        P("base", None),
        P("base", None),
        P("band"),
    )
    out_specs = (P(None, "band", "base"), P(None, None, "base"))
    return jax.shard_map(
        on_device, mesh=mesh, in_specs=in_specs, out_specs=out_specs, check_vma=False
    )
```

```python
import functools

import jax
import jax.numpy as jnp
from jax import lax
from jax.experimental import pallas as pl
from jax.experimental.pallas import tpu as pltpu
from jax.sharding import PartitionSpec as P

BLOCK = 16
NPOLY = 9
ITERS = 3
RIDGE = 0.5
MESH = pl.DeviceIdType.MESH
F32 = jnp.float32
BF16 = jnp.bfloat16
SIDE = 4
CHIPS = SIDE * SIDE
BANDS = 4
TILES = 2
CHANS = 64
CELLS = BLOCK * BLOCK
SOLS = 32
LANES = 128
HALF = SOLS // 2
SUB = HALF // 2
ROWS = 3 * SUB
FAR = sorted(
    [(dz, dx) for dz in range(SIDE) for dx in range(SIDE) if dz or dx],
    key=lambda d: -sum(min(n, SIDE - n) for n in d),
)
NCOEF = 48
PAIRS = [(0, 1), (0, 2), (0, 3), (1, 2), (1, 3), (2, 3)]


def lanes(x, idx):
    numbers = lax.GatherDimensionNumbers(
        offset_dims=(),
        collapsed_slice_dims=(1,),
        start_index_map=(1,),
        operand_batching_dims=(0,),
        start_indices_batching_dims=(0,),
    )
    return lax.gather(
        x, idx[..., None], numbers, (1, 1), mode=lax.GatherScatterMode.PROMISE_IN_BOUNDS
    )


def iota(shape, axis):
    return lax.broadcasted_iota(jnp.int32, shape, axis)


def merge(a, b, lane, bit):
    clear = (lane & bit) == 0
    return jnp.where(clear, a, b) + lanes(jnp.where(clear, b, a), lane ^ bit)


def merge_many(jobs, lane, top):
    bit = top
    while len(jobs[0]) > 1:
        half = len(jobs[0]) // 2
        jobs = [[merge(a, b, lane, bit) for a, b in zip(job[:half], job[half:])] for job in jobs]
        bit //= 2
    return [job[0] for job in jobs]


def mul(a, b):
    return (a[0] * b[0] - a[1] * b[1], a[0] * b[1] + a[1] * b[0])


def mul_conj(a, b):
    return (a[0] * b[0] + a[1] * b[1], a[0] * b[1] - a[1] * b[0])


def conj(a):
    return (a[0], -a[1])


def add(*terms):
    re, im = terms[0]
    for t in terms[1:]:
        re, im = re + t[0], im + t[1]
    return (re, im)


def scaled(a, r):
    return (a[0] * r, a[1] * r)


def outer(j):
    c = [(j[k], j[4 + k]) for k in range(4)]
    q00 = c[0][0] * c[0][0] + c[0][1] * c[0][1] + c[2][0] * c[2][0] + c[2][1] * c[2][1]
    q11 = c[1][0] * c[1][0] + c[1][1] * c[1][1] + c[3][0] * c[3][0] + c[3][1] * c[3][1]
    q01 = add(mul_conj(c[0], c[1]), mul_conj(c[2], c[3]))
    return q00, q11, q01


def station_terms(load, jp, jq):
    p = [(jp[k], jp[4 + k]) for k in range(4)]
    q = [(jq[k], jq[4 + k]) for k in range(4)]
    cross = {}
    for ab in range(4):
        for cd in range(4):
            cross[ab, cd] = (load(4 * ab + cd), load(16 + 4 * ab + cd))
    gp, gq = [], []
    for a in range(2):
        for d in range(2):
            gp.append(
                add(
                    *[
                        mul(cross[2 * a + b, 2 * d + c], q[2 * b + c])
                        for b in range(2)
                        for c in range(2)
                    ]
                )
            )
            gq.append(
                add(
                    *[
                        mul_conj(cross[2 * b + a, 2 * c + d], p[2 * b + c])
                        for b in range(2)
                        for c in range(2)
                    ]
                )
            )
    diag = [load(32 + k) for k in range(4)]
    off = {pair: (load(36 + 2 * n), load(37 + 2 * n)) for n, pair in enumerate(PAIRS)}
    q00, q11, q01 = outer(jq)
    two = scaled(q01, 2.0)
    hp = [
        diag[0] * q00 + diag[1] * q11 + mul_conj(conj(off[0, 1]), two)[0],
        diag[2] * q00 + diag[3] * q11 + mul_conj(conj(off[2, 3]), two)[0],
        *add(
            scaled(off[0, 2], q00),
            mul(off[0, 3], q01),
            mul_conj(q01, off[1, 2]),
            scaled(off[1, 3], q11),
        ),
    ]
    r00, r11, r01 = outer(jp)
    two = scaled(r01, 2.0)
    hq = [
        diag[0] * r00 + diag[2] * r11 + mul_conj(off[0, 2], two)[0],
        diag[1] * r00 + diag[3] * r11 + mul_conj(off[1, 3], two)[0],
        *add(
            scaled(conj(off[0, 1]), r00),
            mul_conj(off[0, 3], r01),
            mul_conj(r01, off[1, 2]),
            scaled(conj(off[2, 3]), r11),
        ),
    ]
    gp = [g[0] for g in gp] + [g[1] for g in gp]
    gq = [g[0] for g in gq] + [g[1] for g in gq]
    return gp, hp, gq, hq


def kernel(
    vis_hbm, mdl_hbm, start_hbm, pen_hbm, pairs_hbm, flags_hbm, chan_hbm,
    gains_out, coeff_out,
    vis, mdl, start, pen_in, pairs, flags, chan, ends,
    vf, mf, coef, half_out, mine, every, sbuf, rbuf, prec, names, away, wsend, wrec,
    hold, jp_at, jq_at, raw, term_g, term_h, named_at, mixed, final, last, basis, scale, pen, cons, dual, ginv,
    loc, ag_s, ag_r, rs_s, rs_r, ps_s, ps_r, one,
):
    band = lax.axis_index("band")
    base = lax.axis_index("base")
    core = base % 2
    chip = base // 2
    cz = chip // SIDE
    cx = chip % SIDE
    sibling = chip * 2 + (1 - core)

    def at(dz, dx):
        return ((cz + dz) % SIDE) * SIDE + (cx + dx) % SIDE

    def copy(src, dst, send, recv, band_to, base_to):
        return pltpu.make_async_remote_copy(
            src_ref=src, dst_ref=dst, send_sem=send, recv_sem=recv,
            device_id=(band_to, base_to), device_id_type=MESH,
        )

    barrier = pltpu.get_barrier_semaphore()

    def greet(band_to, base_to):
        pl.semaphore_signal(barrier, inc=1, device_id=(band_to, base_to), device_id_type=MESH)

    for dz, dx in FAR:
        for c in range(2):
            greet(band, 2 * at(dz, dx) + c)
    for d in (2, 1, 3):
        for c in range(2):
            greet((band + d) % BANDS, 2 * chip + c)
    greet(band, sibling)

    local = [
        pltpu.make_async_copy(src, dst, loc.at[n])
        for n, (src, dst) in enumerate(
            [
                (start_hbm, start), (pairs_hbm, pairs), (flags_hbm, flags), (chan_hbm, chan),
                (pen_hbm, pen_in), (mdl_hbm, mdl), (vis_hbm, vis),
            ]
        )
    ]
    for c in local:
        c.start()

    lane8 = iota((8, LANES), 1)
    row8 = iota((8, LANES), 0)
    for c in local[:5]:
        c.wait()
    mine[...] = start[...].reshape(8 * BLOCK, SOLS).T.reshape(2, 2, SUB, LANES)
    every[0, base] = mine[core]

    for t in range(TILES):
        for side in range(2):
            ends[t, side] = pairs[t, side]
    blocks = [pairs[t, side] for t in range(TILES) for side in range(2)]
    named = jnp.zeros((8, LANES), jnp.int32)
    for e, b in enumerate(blocks):
        named = jnp.where(row8 == e, b, named)
    names[0] = named
    cell = iota((1, CELLS), 1)
    eye = (cell // BLOCK == cell % BLOCK).astype(F32)
    weights = []
    for t in range(TILES):
        same = jnp.where(blocks[2 * t] == blocks[2 * t + 1], 1.0, 0.0)
        weights.append(flags[t : t + 1, :].astype(F32) * (1.0 - same * eye))
    both = jnp.concatenate([*weights, jnp.zeros((6, CELLS), F32)], axis=0).astype(BF16)
    fold_row = iota((CELLS, LANES), 0)
    fold_lane = iota((CELLS, LANES), 1) % BLOCK
    at_first = jnp.dot(
        both, (fold_row // BLOCK == fold_lane).astype(F32).astype(BF16),
        preferred_element_type=F32,
    )
    at_second = jnp.dot(
        both, (fold_row % BLOCK == fold_lane).astype(F32).astype(BF16),
        preferred_element_type=F32,
    )
    pen_row = jnp.concatenate([pen_in[...]] * 8, axis=1)
    away[0] = jnp.concatenate(
        [at_first[0:1], at_second[0:1], at_first[1:2], at_second[1:2], pen_row]
        + [jnp.zeros((3, LANES), F32)],
        axis=0,
    )

    pl.semaphore_wait(barrier, 2 * CHIPS - 1 + 2 * (BANDS - 1))

    def send_start(half, chain, base_to):
        copy(
            mine.at[half, chain], every.at[0, base, chain], ag_s.at[chain], ag_r.at[chain],
            band, base_to,
        ).start()

    for chain in range(2):
        for dz, dx in FAR:
            for c in range(2):
                send_start(c, chain, 2 * at(dz, dx) + c)
        send_start(1 - core, chain, sibling)
    names_copy = copy(names.at[0], names.at[1], one.at[0], one.at[1], band, sibling)
    away_copy = copy(away.at[0], away.at[1], one.at[2], one.at[3], band, sibling)
    names_copy.start()
    away_copy.start()

    row = iota((SOLS, CHANS), 0)
    sol = band * SOLS + ((row // HALF + core) % 2) * HALF + row % HALF
    member = (jnp.broadcast_to(chan[...], (SOLS, CHANS)) == sol).astype(F32)
    where_c = (band * CHANS + iota((SOLS, CHANS), 1)).astype(F32)
    xpos = -1.0 + (2.0 * where_c + 1.0) / (CHANS * BANDS)
    chans = jnp.sum(member, axis=1, keepdims=True)
    centre = jnp.sum(member * xpos, axis=1, keepdims=True) / chans
    centre = jnp.broadcast_to(centre[:HALF], (HALF, LANES))
    cheb = [jnp.ones_like(centre), centre]
    for _ in range(2, NPOLY):
        cheb.append(2.0 * centre * cheb[-1] - cheb[-2])
    for k in range(NPOLY):
        basis[k] = cheb[k]
    member2 = jnp.concatenate([member, member], axis=1).astype(BF16)

    for c in local[5:]:
        c.wait()

    def collapse(t, carry):
        w = jnp.where(t == 0, weights[0], weights[1])
        for k in range(8):
            vf[k] = vis[k, t].astype(F32)
            mf[k] = mdl[k, t].astype(F32) * w

        def put(n, product):
            high = product.astype(BF16)
            low = (product - high.astype(F32)).astype(BF16)
            out = jnp.dot(
                member2, jnp.concatenate([high, low], axis=0), preferred_element_type=F32
            )
            coef[t, n] = out[:HALF]
            half_out[t, n] = out[HALF:]

        for ab in range(4):
            vr, vi = vf[ab], vf[4 + ab]
            for cd in range(4):
                mr, mi = mf[cd], mf[4 + cd]
                put(4 * ab + cd, vr * mr + vi * mi)
                put(16 + 4 * ab + cd, vi * mr - vr * mi)
        for ab in range(4):
            put(32 + ab, mf[ab] * mf[ab] + mf[4 + ab] * mf[4 + ab])
        for n, (x, y) in enumerate(PAIRS):
            put(36 + 2 * n, mf[x] * mf[y] + mf[4 + x] * mf[4 + y])
            put(37 + 2 * n, mf[4 + x] * mf[y] - mf[x] * mf[4 + y])
        copy(half_out.at[t], coef.at[TILES + t], one.at[4], one.at[5], band, sibling).start()
        return carry

    lax.fori_loop(0, TILES, collapse, 0)

    names_copy.wait_recv()
    away_copy.wait_recv()
    for t in range(TILES):
        for side in range(2):
            ends[TILES + t, side] = names[1, 2 * t + side, 0]

    def weight_rows(k):
        out = jnp.zeros((8, LANES), F32)
        for own in range(2):
            for e in range(2 * TILES):
                hit = row8 + 2 * k == names[own, e : e + 1, :]
                at_end = jnp.broadcast_to(away[own, e : e + 1, :], (8, LANES))
                out = out + jnp.where(hit, at_end, 0.0)
        return out

    for dz, dx in FAR:
        k = at(dz, dx)
        wsend[k] = weight_rows(k)
        copy(
            wsend.at[k], wrec.at[chip], one.at[6], one.at[7], band, 2 * k + core
        ).start()
    wrec[chip] = weight_rows(chip)
    own_pen = jnp.broadcast_to(away[0, 4:5, :], (SUB, LANES))
    its_pen = jnp.broadcast_to(away[1, 4:5, :], (SUB, LANES))
    pen[...] = jnp.concatenate(
        [jnp.where(core == 0, own_pen, its_pen), jnp.where(core == 0, its_pen, own_pen)], axis=0
    )
    for own in range(2):
        for e in range(2 * TILES):
            named_at[2 * TILES * own + e] = jnp.broadcast_to(names[own, e : e + 1, :], (8, LANES))

    def arrived(ref, sem):
        pltpu.make_async_copy(ref, ref, sem).wait()

    arrived(half_out, one.at[5])

    pad = [jnp.zeros((16 - NPOLY, LANES), F32)]
    me = 2 * band + core

    def along_basis(part):
        return [jnp.sum(basis[k] * part, axis=0, keepdims=True) for k in range(NPOLY)] + pad

    def of_block(b):
        return jnp.concatenate([mixed[c, SUB * b : SUB * (b + 1), :] for c in range(2)], axis=0)

    def total_of(it):
        column = iota((HALF, LANES), 1)
        columns = jnp.zeros((HALF, LANES), F32)
        for k in range(NPOLY):
            columns = jnp.where(column == k, basis[k], columns)
        out = along_basis(of_block(0)) + along_basis(of_block(1)) + along_basis(columns)
        prec[it, me] = jnp.concatenate(out, axis=0)

        def send(band_to, base_to):
            copy(
                prec.at[it, me], prec.at[it, me], ps_s.at[it], ps_r.at[it], band_to, base_to
            ).start()

        for d in (2, 1, 3):
            for c in range(2):
                send((band + d) % BANDS, 2 * chip + c)
        send(band, sibling)

    def total_at(it):
        arrived(prec.at[it, pl.ds(0, 2 * BANDS - 1)], ps_r.at[it])
        return functools.reduce(lambda a, b: a + b, [prec[it, k] for k in range(2 * BANDS)])

    def solve_gram(rhs):
        x = ginv[0] * rhs[0:1, :]
        for k in range(1, NPOLY):
            x = x + ginv[k] * rhs[k : k + 1, :]
        return x

    def from_total(total, first):
        @pl.when(first)
        def _():
            r, l = iota((16, LANES), 0), iota((16, LANES), 1)
            m = total[32:, :] + jnp.where((r == l) & (r < NPOLY), RIDGE, 0.0)
            m = m + jnp.where((l == r + 16) & (r < NPOLY), 1.0, 0.0)
            for p in range(NPOLY):
                pivot = m[p : p + 1, :] / m[p : p + 1, p : p + 1]
                m = jnp.where(r == p, pivot, m - m[:, p : p + 1] * pivot)
            for k in range(NPOLY):
                ginv[k] = jnp.broadcast_to(m[:, 16 + k : 17 + k], (16, LANES))

        return [solve_gram(total[16 * b : 16 * b + 16, :]) for b in range(2)]

    inner = lane8 % BLOCK
    station = lane8 // BLOCK
    natural_g = (lane8 % 8) * BLOCK + (inner // 8) * 8 + station
    natural_h = (lane8 % 8) * BLOCK + (inner // 8) * 8 + (station % 4) * 2
    own_blocks = pl.ds(2 * chip, 2)

    def tile_terms(it, c):
        rows = pl.ds(pl.multiple_of(SUB * c, SUB), SUB)
        tiles = range(2 * TILES)
        hold[...] = every[it, :, c]
        for t in tiles:
            of_p = hold[ends[t, 0]]
            of_q = hold[ends[t, 1]]
            for k in range(8):
                jq_at[t, k] = lanes(of_q, k * BLOCK + inner)
                for half in range(2):
                    jp_at[t, half, k] = lanes(of_p, k * BLOCK + half * 8 + station)
        for t in tiles:
            jq = [jq_at[t, k] for k in range(8)]
            sums = []
            for half in range(2):
                jp = [jp_at[t, half, k] for k in range(8)]

                def load(n):
                    return coef[t, n, rows, pl.ds(half * LANES, LANES)]

                gp, hp, gq, hq = station_terms(load, jp, jq)
                for n, x in enumerate(gp):
                    raw[t, 8 * half + n] = x
                for n, x in enumerate(hp):
                    raw[t, 16 + 4 * half + n] = x
                sums.append(gq + hq)
            for n, (x, y) in enumerate(zip(*sums)):
                raw[t, 24 + n] = x + y
        gp = merge_many([[raw[t, n] for n in range(16)] for t in tiles], lane8, 8)
        gq = merge_many([[raw[t, 24 + n] for n in range(8)] for t in tiles], lane8, 64)
        hp = merge_many([[raw[t, 16 + n] for n in range(8)] for t in tiles], lane8, 8)
        hq = merge_many([[raw[t, 32 + n] for n in range(4)] for t in tiles], lane8, 32)
        hp = [x + lanes(x, lane8 ^ 1) for x in hp]
        hq = [x + lanes(x, lane8 ^ 64) for x in hq]
        for t in tiles:
            term_g[2 * t] = lanes(gp[t], natural_g)
            term_g[2 * t + 1] = gq[t]
            term_h[2 * t] = lanes(hp[t], natural_h)
            term_h[2 * t + 1] = hq[t]

    def share(k):
        out = [jnp.zeros((SUB, LANES), F32) for _ in range(3)]
        side = 2 * k + lane8 // 64
        for e in range(4 * TILES):
            name = named_at[e]
            out[0] = out[0] + jnp.where(name == 2 * k, term_g[e], 0.0)
            out[1] = out[1] + jnp.where(name == 2 * k + 1, term_g[e], 0.0)
            out[2] = out[2] + jnp.where(name == side, term_h[e], 0.0)
        return jnp.concatenate(out, axis=0)

    lane = iota((HALF, LANES), 1)

    def solve(it, c):
        normal = functools.reduce(lambda x, y: x + y, [rbuf[it, c, k] for k in range(CHIPS)])
        part = lane % BLOCK
        upper = (lane & BLOCK) != 0
        sign = jnp.where(upper == (lane < 64), 1.0, -1.0)
        packed = normal[2 * SUB :, :]
        outer_part = jnp.concatenate([packed, pltpu.roll(packed, 64, 1)], axis=0)
        per = scale[c]
        rho = pen[...]
        rhs = normal[: 2 * SUB, :] * per + rho * (cons[c] - dual[c])
        h_diag = lanes(outer_part, jnp.where(upper, part, BLOCK + part)) * per + rho
        h_real = lanes(outer_part, 2 * BLOCK + part) * per
        h_imag = lanes(outer_part, 3 * BLOCK + part) * per
        determ = h_diag * lanes(h_diag, lane ^ BLOCK) - h_real * h_real - h_imag * h_imag
        return (
            rhs * h_diag
            - lanes(rhs, lane ^ BLOCK) * h_real
            + sign * lanes(rhs, lane ^ (64 + BLOCK)) * h_imag
        ) / determ

    def iteration(it, carry):
        def send_terms(c, carry):
            chain = 2 * it + c

            @pl.when(it > 0)
            def _():
                arrived(every.at[it, pl.ds(0, 2 * CHIPS - 2), c], ag_r.at[chain])

            @pl.when(it == 0)
            def _():
                arrived(every.at[0, pl.ds(0, 2 * CHIPS - 1), c], ag_r.at[c])

            tile_terms(it, c)
            for dz, dx in FAR:
                k = at(dz, dx)
                sbuf[it, c, k] = share(k)
                copy(
                    sbuf.at[it, c, k], rbuf.at[it, c, chip], rs_s.at[chain], rs_r.at[chain],
                    band, 2 * k + core,
                ).start()
            rbuf[it, c, chip] = share(chip)
            return carry

        lax.fori_loop(0, 2, send_terms, 0)

        @pl.when(it > 0)
        def _():
            coeff = from_total(total_at(it - 1), it == 1)
            for b in range(2):
                agreed = basis[0] * coeff[b][0:1, :]
                for k in range(1, NPOLY):
                    agreed = agreed + basis[k] * coeff[b][k : k + 1, :]
                rows = pl.ds(SUB * b, SUB)
                for c in range(2):
                    new = agreed[SUB * c : SUB * (c + 1), :]
                    dual[c, rows] = mixed[c, rows] - new
                    cons[c, rows] = new

        @pl.when(it == 0)
        def _():
            for c in range(2):
                for b in range(2):
                    cons[c, pl.ds(SUB * b, SUB)] = every[0, 2 * chip + b, c]
            dual[...] = jnp.zeros((2, HALF, LANES), F32)

        @pl.when(it == 0)
        def _():
            arrived(wrec.at[pl.ds(0, CHIPS - 1)], one.at[7])
            total = functools.reduce(lambda a, b: a + b, [wrec[k] for k in range(CHIPS)])
            for c in range(2):
                for b in range(2):
                    at_station = jnp.broadcast_to(total[b : b + 1, :], (SUB, LANES))
                    counts = chans[SUB * c : SUB * (c + 1)] * at_station
                    scale[c, pl.ds(SUB * b, SUB)] = 1.0 / jnp.maximum(counts, 1.0)

        def send_gains(c, carry):
            chain = 2 * it + c
            arrived(rbuf.at[it, c, pl.ds(0, CHIPS - 1)], rs_r.at[chain])
            solved = solve(it, c)
            every[it + 1, 2 * chip, c] = solved[:SUB]
            every[it + 1, 2 * chip + 1, c] = solved[SUB:]

            @pl.when(it + 1 < ITERS)
            def _():
                for dz, dx in FAR:
                    copy(
                        every.at[it + 1, own_blocks, c], every.at[it + 1, own_blocks, c],
                        ag_s.at[chain + 2], ag_r.at[chain + 2], band, 2 * at(dz, dx) + core,
                    ).start()

            mixed[c] = solved + dual[c]
            return carry

        lax.fori_loop(0, 2, send_gains, 0)

        @pl.when(it + 1 < ITERS)
        def _():
            total_of(it)

        return carry

    lax.fori_loop(0, ITERS, iteration, 0)

    for c in range(2):
        last[c] = jnp.concatenate(along_basis(of_block(c)), axis=0)

    def send_last(c, band_to, base_to):
        copy(
            last.at[c], last.at[2 + me], one.at[10], one.at[11], band_to, base_to
        ).start()

    for d in (2, 1, 3):
        for c in range(2):
            send_last(c, (band + d) % BANDS, 2 * chip + c)
    send_last(1 - core, band, sibling)
    final_copy = copy(
        every.at[ITERS, sibling], final.at[core], one.at[8], one.at[9], band, sibling
    )
    final_copy.start()
    last[2 + me] = last[core]
    final[core] = every[ITERS, base]
    final_copy.wait_recv()
    gains_out[...] = final[...].reshape(SOLS, LANES).T.reshape(8, BLOCK, SOLS)
    arrived(last.at[pl.ds(0, 2 * BANDS - 1)], one.at[11])
    coeff = solve_gram(
        functools.reduce(lambda a, b: a + b, [last[2 + k] for k in range(2 * BANDS)])
    )
    for k in range(8):
        coeff_out[:, k, :] = coeff[:NPOLY, k * BLOCK : (k + 1) * BLOCK]

    names_copy.wait_send()
    away_copy.wait_send()
    final_copy.wait_send()
    arrived(half_out, one.at[4])
    arrived(wsend.at[pl.ds(0, CHIPS - 1)], one.at[6])
    for c in range(2):
        arrived(every.at[0, pl.ds(0, 2 * CHIPS - 1), c], ag_s.at[c])
    for it in range(ITERS):
        for c in range(2):
            if it > 0:
                arrived(every.at[it, pl.ds(0, 2 * CHIPS - 2), c], ag_s.at[2 * it + c])
            arrived(sbuf.at[it, c, pl.ds(0, CHIPS - 1)], rs_s.at[2 * it + c])
        if it + 1 < ITERS:
            arrived(prec.at[it, pl.ds(0, 2 * BANDS - 1)], ps_s.at[it])
    arrived(last.at[pl.ds(0, 2 * BANDS - 1)], one.at[10])


def on_device(visibilities, model, start_gains, penalty, pairs, flags, chan_band):
    vmem, dma = pltpu.VMEM, pltpu.SemaphoreType.DMA
    gains, coeff = pl.pallas_call(
        kernel,
        out_shape=(
            jax.ShapeDtypeStruct((8, BLOCK, SOLS), F32),
            jax.ShapeDtypeStruct((NPOLY, 8, BLOCK), F32),
        ),
        in_specs=[pl.BlockSpec(memory_space=pltpu.HBM)] * 7,
        out_specs=(pl.BlockSpec(memory_space=vmem), pl.BlockSpec(memory_space=vmem)),
        scratch_shapes=[
            vmem((8, TILES, CHANS, CELLS), BF16),
            vmem((8, TILES, CHANS, CELLS), BF16),
            vmem((8, BLOCK, SOLS), F32),
            vmem((1, BLOCK), F32),
            pltpu.SMEM((TILES, 2), jnp.int32),
            vmem((TILES, CELLS), jnp.int32),
            vmem((1, CHANS), jnp.int32),
            pltpu.SMEM((2 * TILES, 2), jnp.int32),
            vmem((8, CHANS, CELLS), F32),
            vmem((8, CHANS, CELLS), F32),
            vmem((2 * TILES, NCOEF, HALF, CELLS), F32),
            vmem((TILES, NCOEF, HALF, CELLS), F32),
            vmem((2, 2, SUB, LANES), F32),
            vmem((ITERS + 1, 2 * CHIPS, 2, SUB, LANES), F32),
            vmem((ITERS, 2, CHIPS, ROWS, LANES), F32),
            vmem((ITERS, 2, CHIPS, ROWS, LANES), F32),
            vmem((ITERS, 2 * BANDS, 48, LANES), F32),
            vmem((2, 8, LANES), jnp.int32),
            vmem((2, 8, LANES), F32),
            vmem((CHIPS, 8, LANES), F32),
            vmem((CHIPS, 8, LANES), F32),
            vmem((2 * CHIPS, SUB, LANES), F32),
            vmem((2 * TILES, 2, 8, SUB, LANES), F32),
            vmem((2 * TILES, 8, SUB, LANES), F32),
            vmem((2 * TILES, 36, SUB, LANES), F32),
            vmem((4 * TILES, SUB, LANES), F32),
            vmem((4 * TILES, SUB, LANES), F32),
            vmem((4 * TILES, SUB, LANES), jnp.int32),
            vmem((2, HALF, LANES), F32),
            vmem((2, 2, SUB, LANES), F32),
            vmem((2 + 2 * BANDS, 16, LANES), F32),
            vmem((NPOLY, HALF, LANES), F32),
            vmem((2, HALF, LANES), F32),
            vmem((HALF, LANES), F32),
            vmem((2, HALF, LANES), F32),
            vmem((2, HALF, LANES), F32),
            vmem((NPOLY, 16, LANES), F32),
            dma((7,)),
            *[dma((2 * ITERS,))] * 4,
            *[dma((ITERS,))] * 2,
            dma((12,)),
        ],
        compiler_params=pltpu.CompilerParams(
            collective_id=0, has_side_effects=True, vmem_limit_bytes=40 * 1024 * 1024
        ),
        cost_estimate=pl.CostEstimate(
            flops=60_000_000, bytes_accessed=3_000_000, transcendentals=0
        ),
        name="admm",
    )(
        *[
            pltpu.with_memory_space_constraint(x, pltpu.HBM)
            for x in (
                visibilities, model, jnp.swapaxes(start_gains, 1, 2), penalty.reshape(1, BLOCK),
                pairs, flags, chan_band.reshape(1, CHANS),
            )
        ]
    )
    return jnp.swapaxes(gains, 1, 2), jnp.swapaxes(coeff, 0, 1)


def solution(mesh):
    in_specs = (
        P(None, "base", "band", None),
        P(None, "base", "band", None),
        P(None, "band", "base"),
        P("base"),
        P("base", None),
        P("base", None),
        P("band"),
    )
    out_specs = (P(None, "band", "base"), P(None, None, "base"))
    return jax.shard_map(
        on_device, mesh=mesh, in_specs=in_specs, out_specs=out_specs, check_vma=False
    )
```

```python
import functools

import jax
import jax.numpy as jnp
from jax import lax
from jax.experimental import pallas as pl
from jax.experimental.pallas import tpu as pltpu
from jax.sharding import PartitionSpec as P

BLOCK = 16
NPOLY = 9
ITERS = 3
RIDGE = 0.5
MESH = pl.DeviceIdType.MESH
F32 = jnp.float32
BF16 = jnp.bfloat16
SIDE = 4
CHIPS = SIDE * SIDE
BANDS = 4
TILES = 2
CHANS = 64
CELLS = BLOCK * BLOCK
SOLS = 32
LANES = 128
HALF = SOLS // 2
SUB = HALF // 2
ROWS = 3 * SUB
FAR = sorted(
    [(dz, dx) for dx in range(SIDE) for dz in range(SIDE) if dz or dx],
    key=lambda d: -sum(min(n, SIDE - n) for n in d),
)
NCOEF = 48
PAIRS = [(0, 1), (0, 2), (0, 3), (1, 2), (1, 3), (2, 3)]


def lanes(x, idx):
    numbers = lax.GatherDimensionNumbers(
        offset_dims=(),
        collapsed_slice_dims=(1,),
        start_index_map=(1,),
        operand_batching_dims=(0,),
        start_indices_batching_dims=(0,),
    )
    return lax.gather(
        x, idx[..., None], numbers, (1, 1), mode=lax.GatherScatterMode.PROMISE_IN_BOUNDS
    )


def iota(shape, axis):
    return lax.broadcasted_iota(jnp.int32, shape, axis)


def merge(a, b, lane, bit):
    clear = (lane & bit) == 0
    return jnp.where(clear, a, b) + lanes(jnp.where(clear, b, a), lane ^ bit)


def level(jobs, lane, bit):
    half = len(jobs[0]) // 2
    return [[merge(a, b, lane, bit) for a, b in zip(job[:half], job[half:])] for job in jobs]


def mul(a, b):
    return (a[0] * b[0] - a[1] * b[1], a[0] * b[1] + a[1] * b[0])


def mul_conj(a, b):
    return (a[0] * b[0] + a[1] * b[1], a[0] * b[1] - a[1] * b[0])


def conj(a):
    return (a[0], -a[1])


def add(*terms):
    re, im = terms[0]
    for t in terms[1:]:
        re, im = re + t[0], im + t[1]
    return (re, im)


def scaled(a, r):
    return (a[0] * r, a[1] * r)


def outer(j):
    c = [(j[k], j[4 + k]) for k in range(4)]
    q00 = c[0][0] * c[0][0] + c[0][1] * c[0][1] + c[2][0] * c[2][0] + c[2][1] * c[2][1]
    q11 = c[1][0] * c[1][0] + c[1][1] * c[1][1] + c[3][0] * c[3][0] + c[3][1] * c[3][1]
    q01 = add(mul_conj(c[0], c[1]), mul_conj(c[2], c[3]))
    return q00, q11, q01


def sum_of(terms):
    return functools.reduce(lambda a, b: a + b, terms)


def station_terms(load, jp, jq, outer_q):
    p = [(jp[k], jp[4 + k] - jp[k], jp[4 + k] + jp[k]) for k in range(4)]
    q = [(jq[k], jq[4 + k] - jq[k], jq[4 + k] + jq[k]) for k in range(4)]
    cross = {}
    for ab in range(4):
        for cd in range(4):
            n = 4 * ab + cd
            cross[ab, cd] = (load(n), load(16 + n), load(NCOEF + n))
    inner = [(b, c) for b in range(2) for c in range(2)]
    gp, gq = [], []
    for a in range(2):
        for d in range(2):
            x = [cross[2 * a + b, 2 * d + c] for b, c in inner]
            both = sum_of(x[n][2] * q[n][0] for n in range(4))
            re = both - sum_of(x[n][1] * q[n][2] for n in range(4))
            gp.append((re, both + sum_of(x[n][0] * q[n][1] for n in range(4))))
            x = [cross[2 * b + a, 2 * c + d] for b, c in inner]
            both = sum_of(x[n][2] * p[n][0] for n in range(4))
            re = both + sum_of(x[n][1] * p[n][1] for n in range(4))
            gq.append((re, sum_of(x[n][0] * p[n][2] for n in range(4)) - both))
    diag = [load(32 + k) for k in range(4)]
    off = {pair: (load(36 + 2 * n), load(37 + 2 * n)) for n, pair in enumerate(PAIRS)}
    q00, q11, q01 = outer_q
    two = scaled(q01, 2.0)
    hp = [
        diag[0] * q00 + diag[1] * q11 + mul_conj(conj(off[0, 1]), two)[0],
        diag[2] * q00 + diag[3] * q11 + mul_conj(conj(off[2, 3]), two)[0],
        *add(
            scaled(off[0, 2], q00),
            mul(off[0, 3], q01),
            mul_conj(q01, off[1, 2]),
            scaled(off[1, 3], q11),
        ),
    ]
    r00, r11, r01 = outer(jp)
    two = scaled(r01, 2.0)
    hq = [
        diag[0] * r00 + diag[2] * r11 + mul_conj(off[0, 2], two)[0],
        diag[1] * r00 + diag[3] * r11 + mul_conj(off[1, 3], two)[0],
        *add(
            scaled(conj(off[0, 1]), r00),
            mul_conj(off[0, 3], r01),
            mul_conj(r01, off[1, 2]),
            scaled(conj(off[2, 3]), r11),
        ),
    ]
    gp = [g[0] for g in gp] + [g[1] for g in gp]
    gq = [g[0] for g in gq] + [g[1] for g in gq]
    return gp, hp, gq, hq


def kernel(
    vis_hbm, mdl_hbm, start_hbm, pen_hbm, pairs_hbm, flags_hbm, chan_hbm,
    gains_out, coeff_out,
    vis, mdl, start, pen_in, pairs, flags, chan, ends,
    vf, mf, coef, half_out, mine, every, sbuf, rbuf, prec, names, away, wsend, wrec,
    hold, jp_at, jq_at, raw, term_g, term_h, named_at, mixed, final, last, basis, scale, pen, cons, dual, ginv,
    loc, ag_s, ag_r, rs_s, rs_r, ps_s, ps_r, one,
):
    band = lax.axis_index("band")
    base = lax.axis_index("base")
    core = base % 2
    chip = base // 2
    cz = chip // SIDE
    cx = chip % SIDE
    sibling = chip * 2 + (1 - core)

    def at(dz, dx):
        return ((cz + dz) % SIDE) * SIDE + (cx + dx) % SIDE

    def copy(src, dst, send, recv, band_to, base_to):
        return pltpu.make_async_remote_copy(
            src_ref=src, dst_ref=dst, send_sem=send, recv_sem=recv,
            device_id=(band_to, base_to), device_id_type=MESH,
        )

    barrier = pltpu.get_barrier_semaphore()

    def greet(band_to, base_to):
        pl.semaphore_signal(barrier, inc=1, device_id=(band_to, base_to), device_id_type=MESH)

    for dz, dx in FAR:
        for c in range(2):
            greet(band, 2 * at(dz, dx) + c)
    for d in (2, 1, 3):
        for c in range(2):
            greet((band + d) % BANDS, 2 * chip + c)
    greet(band, sibling)

    local = [
        pltpu.make_async_copy(src, dst, loc.at[n])
        for n, (src, dst) in enumerate(
            [
                (start_hbm, start), (pairs_hbm, pairs), (flags_hbm, flags), (chan_hbm, chan),
                (pen_hbm, pen_in), (mdl_hbm, mdl), (vis_hbm, vis),
            ]
        )
    ]
    for c in local:
        c.start()

    lane8 = iota((8, LANES), 1)
    row8 = iota((8, LANES), 0)
    for c in local[:5]:
        c.wait()
    mine[...] = start[...].reshape(8 * BLOCK, SOLS).T.reshape(2, 2, SUB, LANES)
    every[0, base] = mine[core]

    for t in range(TILES):
        for side in range(2):
            ends[t, side] = pairs[t, side]
    blocks = [pairs[t, side] for t in range(TILES) for side in range(2)]
    named = jnp.zeros((8, LANES), jnp.int32)
    for e, b in enumerate(blocks):
        named = jnp.where(row8 == e, b, named)
    names[0] = named
    cell = iota((1, CELLS), 1)
    eye = (cell // BLOCK == cell % BLOCK).astype(F32)
    weights = []
    for t in range(TILES):
        same = jnp.where(blocks[2 * t] == blocks[2 * t + 1], 1.0, 0.0)
        weights.append(flags[t : t + 1, :].astype(F32) * (1.0 - same * eye))
    both = jnp.concatenate([*weights, jnp.zeros((6, CELLS), F32)], axis=0).astype(BF16)
    fold_row = iota((CELLS, LANES), 0)
    fold_lane = iota((CELLS, LANES), 1) % BLOCK
    at_first = jnp.dot(
        both, (fold_row // BLOCK == fold_lane).astype(F32).astype(BF16),
        preferred_element_type=F32,
    )
    at_second = jnp.dot(
        both, (fold_row % BLOCK == fold_lane).astype(F32).astype(BF16),
        preferred_element_type=F32,
    )
    pen_row = jnp.concatenate([pen_in[...]] * 8, axis=1)
    away[0] = jnp.concatenate(
        [at_first[0:1], at_second[0:1], at_first[1:2], at_second[1:2], pen_row]
        + [jnp.zeros((3, LANES), F32)],
        axis=0,
    )

    pl.semaphore_wait(barrier, 2 * CHIPS - 1 + 2 * (BANDS - 1))

    def send_start(half, chain, base_to):
        copy(
            mine.at[half, chain], every.at[0, base, chain], ag_s.at[chain], ag_r.at[chain],
            band, base_to,
        ).start()

    for chain in range(2):
        for dz, dx in FAR:
            for c in range(2):
                send_start(c, chain, 2 * at(dz, dx) + c)
        send_start(1 - core, chain, sibling)
    names_copy = copy(names.at[0], names.at[1], one.at[0], one.at[1], band, sibling)
    away_copy = copy(away.at[0], away.at[1], one.at[2], one.at[3], band, sibling)
    names_copy.start()
    away_copy.start()

    row = iota((SOLS, CHANS), 0)
    sol = band * SOLS + ((row // HALF + core) % 2) * HALF + row % HALF
    member = (jnp.broadcast_to(chan[...], (SOLS, CHANS)) == sol).astype(F32)
    where_c = (band * CHANS + iota((SOLS, CHANS), 1)).astype(F32)
    xpos = -1.0 + (2.0 * where_c + 1.0) / (CHANS * BANDS)
    chans = jnp.sum(member, axis=1, keepdims=True)
    centre = jnp.sum(member * xpos, axis=1, keepdims=True) / chans
    centre = jnp.broadcast_to(centre[:HALF], (HALF, LANES))
    cheb = [jnp.ones_like(centre), centre]
    for _ in range(2, NPOLY):
        cheb.append(2.0 * centre * cheb[-1] - cheb[-2])
    for k in range(NPOLY):
        basis[k] = cheb[k]
    member2 = jnp.concatenate([member, member], axis=1).astype(BF16)

    for c in local[5:]:
        c.wait()

    def collapse(t, carry):
        w = jnp.where(t == 0, weights[0], weights[1])
        for k in range(8):
            vf[k] = vis[k, t].astype(F32)
            mf[k] = mdl[k, t].astype(F32) * w

        def put(n, product):
            high = product.astype(BF16)
            low = (product - high.astype(F32)).astype(BF16)
            out = jnp.dot(
                member2, jnp.concatenate([high, low], axis=0), preferred_element_type=F32
            )
            coef[t, n] = out[:HALF]
            half_out[t, n] = out[HALF:]

        for ab in range(4):
            vr, vi = vf[ab], vf[4 + ab]
            for cd in range(4):
                mr, mi = mf[cd], mf[4 + cd]
                put(4 * ab + cd, vr * mr + vi * mi)
                put(16 + 4 * ab + cd, vi * mr - vr * mi)
        for ab in range(4):
            put(32 + ab, mf[ab] * mf[ab] + mf[4 + ab] * mf[4 + ab])
        for n, (x, y) in enumerate(PAIRS):
            put(36 + 2 * n, mf[x] * mf[y] + mf[4 + x] * mf[4 + y])
            put(37 + 2 * n, mf[4 + x] * mf[y] - mf[x] * mf[4 + y])
        copy(
            half_out.at[t], coef.at[TILES + t, pl.ds(0, NCOEF)], one.at[4], one.at[5], band, sibling
        ).start()
        return carry

    lax.fori_loop(0, TILES, collapse, 0)

    names_copy.wait_recv()
    away_copy.wait_recv()
    for t in range(TILES):
        for side in range(2):
            ends[TILES + t, side] = names[1, 2 * t + side, 0]

    def weight_rows(k):
        out = jnp.zeros((8, LANES), F32)
        for own in range(2):
            for e in range(2 * TILES):
                hit = row8 + 2 * k == names[own, e : e + 1, :]
                at_end = jnp.broadcast_to(away[own, e : e + 1, :], (8, LANES))
                out = out + jnp.where(hit, at_end, 0.0)
        return out

    for dz, dx in FAR:
        k = at(dz, dx)
        wsend[k] = weight_rows(k)
        copy(
            wsend.at[k], wrec.at[chip], one.at[6], one.at[7], band, 2 * k + core
        ).start()
    wrec[chip] = weight_rows(chip)
    own_pen = jnp.broadcast_to(away[0, 4:5, :], (SUB, LANES))
    its_pen = jnp.broadcast_to(away[1, 4:5, :], (SUB, LANES))
    pen[...] = jnp.concatenate(
        [jnp.where(core == 0, own_pen, its_pen), jnp.where(core == 0, its_pen, own_pen)], axis=0
    )
    for own in range(2):
        for e in range(2 * TILES):
            named_at[2 * TILES * own + e] = jnp.broadcast_to(names[own, e : e + 1, :], (8, LANES))

    def arrived(ref, sem):
        pltpu.make_async_copy(ref, ref, sem).wait()

    arrived(half_out, one.at[5])
    for t in range(2 * TILES):
        for n in range(16):
            coef[t, NCOEF + n] = coef[t, n] + coef[t, 16 + n]

    pad = [jnp.zeros((16 - NPOLY, LANES), F32)]
    me = 2 * band + core

    def along_basis(part):
        return [jnp.sum(basis[k] * part, axis=0, keepdims=True) for k in range(NPOLY)] + pad

    def of_block(b):
        return jnp.concatenate([mixed[c, SUB * b : SUB * (b + 1), :] for c in range(2)], axis=0)

    def total_of(it):
        column = iota((HALF, LANES), 1)
        columns = jnp.zeros((HALF, LANES), F32)
        for k in range(NPOLY):
            columns = jnp.where(column == k, basis[k], columns)
        out = along_basis(of_block(0)) + along_basis(of_block(1)) + along_basis(columns)
        prec[it, me] = jnp.concatenate(out, axis=0)

        def send(band_to, base_to):
            copy(
                prec.at[it, me], prec.at[it, me], ps_s.at[it], ps_r.at[it], band_to, base_to
            ).start()

        for d in (2, 1, 3):
            for c in range(2):
                send((band + d) % BANDS, 2 * chip + c)
        send(band, sibling)

    def total_at(it):
        arrived(prec.at[it, pl.ds(0, 2 * BANDS - 1)], ps_r.at[it])
        return functools.reduce(lambda a, b: a + b, [prec[it, k] for k in range(2 * BANDS)])

    def solve_gram(rhs):
        x = ginv[0] * rhs[0:1, :]
        for k in range(1, NPOLY):
            x = x + ginv[k] * rhs[k : k + 1, :]
        return x

    def from_total(total, first):
        @pl.when(first)
        def _():
            r, l = iota((16, LANES), 0), iota((16, LANES), 1)
            m = total[32:, :] + jnp.where((r == l) & (r < NPOLY), RIDGE, 0.0)
            m = m + jnp.where((l == r + 16) & (r < NPOLY), 1.0, 0.0)
            for p in range(NPOLY):
                pivot = m[p : p + 1, :] / m[p : p + 1, p : p + 1]
                m = jnp.where(r == p, pivot, m - m[:, p : p + 1] * pivot)
            for k in range(NPOLY):
                ginv[k] = jnp.broadcast_to(m[:, 16 + k : 17 + k], (16, LANES))

        return [solve_gram(total[16 * b : 16 * b + 16, :]) for b in range(2)]

    inner = lane8 % BLOCK
    station = lane8 // BLOCK
    natural_g = (lane8 % 8) * BLOCK + (inner // 8) * 8 + station
    natural_h = (lane8 % 8) * BLOCK + (inner // 8) * 8 + (station % 4) * 2
    own_blocks = pl.ds(2 * chip, 2)

    def tile_terms(it, c):
        rows = pl.ds(pl.multiple_of(SUB * c, SUB), SUB)
        tiles = range(2 * TILES)
        hold[...] = every[it, :, c]
        of_p = [hold[ends[t, 0]] for t in tiles]
        of_q = [hold[ends[t, 1]] for t in tiles]
        for k in range(8):
            for t in tiles:
                jq_at[t, k] = lanes(of_q[t], k * BLOCK + inner)
        for k in range(8):
            for half in range(2):
                for t in tiles:
                    jp_at[t, half, k] = lanes(of_p[t], k * BLOCK + half * 8 + station)
        for t in tiles:
            jq = [jq_at[t, k] for k in range(8)]
            sums = []
            outer_q = outer(jq)
            for half in range(2):
                jp = [jp_at[t, half, k] for k in range(8)]

                def load(n):
                    return coef[t, n, rows, pl.ds(half * LANES, LANES)]

                gp, hp, gq, hq = station_terms(load, jp, jq, outer_q)
                for n, x in enumerate(gp):
                    raw[t, 8 * half + n] = x
                for n, x in enumerate(hp):
                    raw[t, 16 + 4 * half + n] = x
                sums.append(gq + hq)
            for n, (x, y) in enumerate(zip(*sums)):
                raw[t, 24 + n] = x + y
        gp = [[raw[t, n] for n in range(16)] for t in tiles]
        hp = [[raw[t, 16 + n] for n in range(8)] for t in tiles]
        gq = [[raw[t, 24 + n] for n in range(8)] for t in tiles]
        hq = [[raw[t, 32 + n] for n in range(4)] for t in tiles]
        gp, hp, gq = level(gp, lane8, 8), level(hp, lane8, 8), level(gq, lane8, 64)
        gp, hp, gq, hq = [level(x, lane8, b) for x, b in ((gp, 4), (hp, 4), (gq, 32), (hq, 32))]
        gp, hp, gq, hq = [level(x, lane8, b) for x, b in ((gp, 2), (hp, 2), (gq, 16), (hq, 16))]
        gp = [x for (x,) in level(gp, lane8, 1)]
        hp = [x + lanes(x, lane8 ^ 1) for (x,) in hp]
        gq = [x for (x,) in gq]
        hq = [x + pltpu.roll(x, 64, 1) for (x,) in hq]
        for t in tiles:
            term_g[2 * t] = lanes(gp[t], natural_g)
            term_g[2 * t + 1] = gq[t]
            term_h[2 * t] = lanes(hp[t], natural_h)
            term_h[2 * t + 1] = hq[t]

    def share(k):
        out = [jnp.zeros((SUB, LANES), F32) for _ in range(3)]
        side = 2 * k + lane8 // 64
        for e in range(4 * TILES):
            name = named_at[e]
            out[0] = out[0] + jnp.where(name == 2 * k, term_g[e], 0.0)
            out[1] = out[1] + jnp.where(name == 2 * k + 1, term_g[e], 0.0)
            out[2] = out[2] + jnp.where(name == side, term_h[e], 0.0)
        return jnp.concatenate(out, axis=0)

    lane = iota((HALF, LANES), 1)

    def solve(it, c):
        normal = functools.reduce(lambda x, y: x + y, [rbuf[it, c, k] for k in range(CHIPS)])
        part = lane % BLOCK
        upper = (lane & BLOCK) != 0
        sign = jnp.where(upper == (lane < 64), 1.0, -1.0)
        packed = normal[2 * SUB :, :]
        both = jnp.concatenate([packed, packed], axis=0)
        part = part + 64 * (iota((HALF, LANES), 0) // SUB)
        per = scale[c]
        rho = pen[...]
        rhs = normal[: 2 * SUB, :] * per + rho * (cons[c] - dual[c])
        h_diag = lanes(both, jnp.where(upper, part, BLOCK + part)) * per + rho
        h_swap = lanes(both, jnp.where(upper, BLOCK + part, part)) * per + rho
        h_real = lanes(both, 2 * BLOCK + part) * per
        h_imag = lanes(both, 3 * BLOCK + part) * per
        determ = h_diag * h_swap - h_real * h_real - h_imag * h_imag
        return (
            rhs * h_diag
            - lanes(rhs, lane ^ BLOCK) * h_real
            + sign * lanes(rhs, lane ^ (64 + BLOCK)) * h_imag
        ) / determ

    def iteration(it, carry):
        def send_terms(c, carry):
            chain = 2 * it + c

            @pl.when(it > 0)
            def _():
                arrived(every.at[it, pl.ds(0, 2 * CHIPS - 2), c], ag_r.at[chain])

            @pl.when(it == 0)
            def _():
                arrived(every.at[0, pl.ds(0, 2 * CHIPS - 1), c], ag_r.at[c])

            tile_terms(it, c)
            for dz, dx in FAR:
                k = at(dz, dx)
                sbuf[it, c, k] = share(k)
                copy(
                    sbuf.at[it, c, k], rbuf.at[it, c, chip], rs_s.at[chain], rs_r.at[chain],
                    band, 2 * k + core,
                ).start()
            rbuf[it, c, chip] = share(chip)
            return carry

        lax.fori_loop(0, 2, send_terms, 0)

        @pl.when(it > 0)
        def _():
            coeff = from_total(total_at(it - 1), it == 1)
            for b in range(2):
                agreed = basis[0] * coeff[b][0:1, :]
                for k in range(1, NPOLY):
                    agreed = agreed + basis[k] * coeff[b][k : k + 1, :]
                rows = pl.ds(SUB * b, SUB)
                for c in range(2):
                    new = agreed[SUB * c : SUB * (c + 1), :]
                    dual[c, rows] = mixed[c, rows] - new
                    cons[c, rows] = new

        @pl.when(it == 0)
        def _():
            for c in range(2):
                for b in range(2):
                    cons[c, pl.ds(SUB * b, SUB)] = every[0, 2 * chip + b, c]
            dual[...] = jnp.zeros((2, HALF, LANES), F32)

        @pl.when(it == 0)
        def _():
            arrived(wrec.at[pl.ds(0, CHIPS - 1)], one.at[7])
            total = functools.reduce(lambda a, b: a + b, [wrec[k] for k in range(CHIPS)])
            for c in range(2):
                for b in range(2):
                    at_station = jnp.broadcast_to(total[b : b + 1, :], (SUB, LANES))
                    counts = chans[SUB * c : SUB * (c + 1)] * at_station
                    scale[c, pl.ds(SUB * b, SUB)] = 1.0 / jnp.maximum(counts, 1.0)

        def send_gains(c, carry):
            chain = 2 * it + c
            arrived(rbuf.at[it, c, pl.ds(0, CHIPS - 1)], rs_r.at[chain])
            solved = solve(it, c)
            every[it + 1, 2 * chip, c] = solved[:SUB]
            every[it + 1, 2 * chip + 1, c] = solved[SUB:]

            @pl.when(it + 1 < ITERS)
            def _():
                for dz, dx in FAR:
                    copy(
                        every.at[it + 1, own_blocks, c], every.at[it + 1, own_blocks, c],
                        ag_s.at[chain + 2], ag_r.at[chain + 2], band, 2 * at(dz, dx) + core,
                    ).start()

            mixed[c] = solved + dual[c]
            return carry

        lax.fori_loop(0, 2, send_gains, 0)

        @pl.when(it + 1 < ITERS)
        def _():
            total_of(it)

        return carry

    lax.fori_loop(0, ITERS, iteration, 0)

    for c in range(2):
        last[c] = jnp.concatenate(along_basis(of_block(c)), axis=0)

    def send_last(c, band_to, base_to):
        copy(
            last.at[c], last.at[2 + me], one.at[10], one.at[11], band_to, base_to
        ).start()

    for d in (2, 1, 3):
        for c in range(2):
            send_last(c, (band + d) % BANDS, 2 * chip + c)
    send_last(1 - core, band, sibling)
    final_copy = copy(
        every.at[ITERS, sibling], final.at[core], one.at[8], one.at[9], band, sibling
    )
    final_copy.start()
    last[2 + me] = last[core]
    final[core] = every[ITERS, base]
    final_copy.wait_recv()
    gains_out[...] = final[...].reshape(SOLS, LANES).T.reshape(8, BLOCK, SOLS)
    arrived(last.at[pl.ds(0, 2 * BANDS - 1)], one.at[11])
    coeff = solve_gram(
        functools.reduce(lambda a, b: a + b, [last[2 + k] for k in range(2 * BANDS)])
    )
    for k in range(8):
        coeff_out[:, k, :] = coeff[:NPOLY, k * BLOCK : (k + 1) * BLOCK]

    names_copy.wait_send()
    away_copy.wait_send()
    final_copy.wait_send()
    arrived(half_out, one.at[4])
    arrived(wsend.at[pl.ds(0, CHIPS - 1)], one.at[6])
    for c in range(2):
        arrived(every.at[0, pl.ds(0, 2 * CHIPS - 1), c], ag_s.at[c])
    for it in range(ITERS):
        for c in range(2):
            if it > 0:
                arrived(every.at[it, pl.ds(0, 2 * CHIPS - 2), c], ag_s.at[2 * it + c])
            arrived(sbuf.at[it, c, pl.ds(0, CHIPS - 1)], rs_s.at[2 * it + c])
        if it + 1 < ITERS:
            arrived(prec.at[it, pl.ds(0, 2 * BANDS - 1)], ps_s.at[it])
    arrived(last.at[pl.ds(0, 2 * BANDS - 1)], one.at[10])


def on_device(visibilities, model, start_gains, penalty, pairs, flags, chan_band):
    vmem, dma = pltpu.VMEM, pltpu.SemaphoreType.DMA
    gains, coeff = pl.pallas_call(
        kernel,
        out_shape=(
            jax.ShapeDtypeStruct((8, BLOCK, SOLS), F32),
            jax.ShapeDtypeStruct((NPOLY, 8, BLOCK), F32),
        ),
        in_specs=[pl.BlockSpec(memory_space=pltpu.HBM)] * 7,
        out_specs=(pl.BlockSpec(memory_space=vmem), pl.BlockSpec(memory_space=vmem)),
        scratch_shapes=[
            vmem((8, TILES, CHANS, CELLS), BF16),
            vmem((8, TILES, CHANS, CELLS), BF16),
            vmem((8, BLOCK, SOLS), F32),
            vmem((1, BLOCK), F32),
            pltpu.SMEM((TILES, 2), jnp.int32),
            vmem((TILES, CELLS), jnp.int32),
            vmem((1, CHANS), jnp.int32),
            pltpu.SMEM((2 * TILES, 2), jnp.int32),
            vmem((8, CHANS, CELLS), F32),
            vmem((8, CHANS, CELLS), F32),
            vmem((2 * TILES, NCOEF + 16, HALF, CELLS), F32),
            vmem((TILES, NCOEF, HALF, CELLS), F32),
            vmem((2, 2, SUB, LANES), F32),
            vmem((ITERS + 1, 2 * CHIPS, 2, SUB, LANES), F32),
            vmem((ITERS, 2, CHIPS, ROWS, LANES), F32),
            vmem((ITERS, 2, CHIPS, ROWS, LANES), F32),
            vmem((ITERS, 2 * BANDS, 48, LANES), F32),
            vmem((2, 8, LANES), jnp.int32),
            vmem((2, 8, LANES), F32),
            vmem((CHIPS, 8, LANES), F32),
            vmem((CHIPS, 8, LANES), F32),
            vmem((2 * CHIPS, SUB, LANES), F32),
            vmem((2 * TILES, 2, 8, SUB, LANES), F32),
            vmem((2 * TILES, 8, SUB, LANES), F32),
            vmem((2 * TILES, 36, SUB, LANES), F32),
            vmem((4 * TILES, SUB, LANES), F32),
            vmem((4 * TILES, SUB, LANES), F32),
            vmem((4 * TILES, SUB, LANES), jnp.int32),
            vmem((2, HALF, LANES), F32),
            vmem((2, 2, SUB, LANES), F32),
            vmem((2 + 2 * BANDS, 16, LANES), F32),
            vmem((NPOLY, HALF, LANES), F32),
            vmem((2, HALF, LANES), F32),
            vmem((HALF, LANES), F32),
            vmem((2, HALF, LANES), F32),
            vmem((2, HALF, LANES), F32),
            vmem((NPOLY, 16, LANES), F32),
            dma((7,)),
            *[dma((2 * ITERS,))] * 4,
            *[dma((ITERS,))] * 2,
            dma((12,)),
        ],
        compiler_params=pltpu.CompilerParams(
            collective_id=0, has_side_effects=True, vmem_limit_bytes=40 * 1024 * 1024
        ),
        cost_estimate=pl.CostEstimate(
            flops=60_000_000, bytes_accessed=3_000_000, transcendentals=0
        ),
        name="admm",
    )(
        *[
            pltpu.with_memory_space_constraint(x, pltpu.HBM)
            for x in (
                visibilities, model, jnp.swapaxes(start_gains, 1, 2), penalty.reshape(1, BLOCK),
                pairs, flags, chan_band.reshape(1, CHANS),
            )
        ]
    )
    return jnp.swapaxes(gains, 1, 2), jnp.swapaxes(coeff, 0, 1)


def solution(mesh):
    in_specs = (
        P(None, "base", "band", None),
        P(None, "base", "band", None),
        P(None, "band", "base"),
        P("base"),
        P("base", None),
        P("base", None),
        P("band"),
    )
    out_specs = (P(None, "band", "base"), P(None, None, "base"))
    return jax.shard_map(
        on_device, mesh=mesh, in_specs=in_specs, out_specs=out_specs, check_vma=False
    )
```

```python
import functools

import jax
import jax.numpy as jnp
from jax import lax
from jax.experimental import pallas as pl
from jax.experimental.pallas import tpu as pltpu
from jax.sharding import PartitionSpec as P

BLOCK = 16
NPOLY = 9
ITERS = 3
RIDGE = 0.5
MESH = pl.DeviceIdType.MESH
F32 = jnp.float32
BF16 = jnp.bfloat16
SIDE = 4
CHIPS = SIDE * SIDE
BANDS = 4
TILES = 2
CHANS = 64
CELLS = BLOCK * BLOCK
SOLS = 32
LANES = 128
HALF = SOLS // 2
SUB = HALF // 2
ROWS = 3 * SUB
FAR = sorted(
    [(dz, dx) for dx in range(SIDE) for dz in range(SIDE) if dz or dx],
    key=lambda d: -sum(min(n, SIDE - n) for n in d),
)
NCOEF = 48
PAIRS = [(0, 1), (0, 2), (0, 3), (1, 2), (1, 3), (2, 3)]


def lanes(x, idx):
    numbers = lax.GatherDimensionNumbers(
        offset_dims=(),
        collapsed_slice_dims=(1,),
        start_index_map=(1,),
        operand_batching_dims=(0,),
        start_indices_batching_dims=(0,),
    )
    return lax.gather(
        x, idx[..., None], numbers, (1, 1), mode=lax.GatherScatterMode.PROMISE_IN_BOUNDS
    )


def iota(shape, axis):
    return lax.broadcasted_iota(jnp.int32, shape, axis)


def merge(a, b, lane, bit):
    clear = (lane & bit) == 0
    return jnp.where(clear, a, b) + lanes(jnp.where(clear, b, a), lane ^ bit)


def level(jobs, lane, bit):
    half = len(jobs[0]) // 2
    return [[merge(a, b, lane, bit) for a, b in zip(job[:half], job[half:])] for job in jobs]


def mul(a, b):
    return (a[0] * b[0] - a[1] * b[1], a[0] * b[1] + a[1] * b[0])


def mul_conj(a, b):
    return (a[0] * b[0] + a[1] * b[1], a[0] * b[1] - a[1] * b[0])


def conj(a):
    return (a[0], -a[1])


def add(*terms):
    re, im = terms[0]
    for t in terms[1:]:
        re, im = re + t[0], im + t[1]
    return (re, im)


def scaled(a, r):
    return (a[0] * r, a[1] * r)


def outer(j):
    c = [(j[k], j[4 + k]) for k in range(4)]
    q00 = c[0][0] * c[0][0] + c[0][1] * c[0][1] + c[2][0] * c[2][0] + c[2][1] * c[2][1]
    q11 = c[1][0] * c[1][0] + c[1][1] * c[1][1] + c[3][0] * c[3][0] + c[3][1] * c[3][1]
    q01 = add(mul_conj(c[0], c[1]), mul_conj(c[2], c[3]))
    return q00, q11, q01


def sum_of(terms):
    return functools.reduce(lambda a, b: a + b, terms)


def station_terms(load, jp, jq, outer_q):
    p = [(jp[k], jp[4 + k] - jp[k], jp[4 + k] + jp[k]) for k in range(4)]
    q = [(jq[k], jq[4 + k] - jq[k], jq[4 + k] + jq[k]) for k in range(4)]
    cross = {}
    for ab in range(4):
        for cd in range(4):
            n = 4 * ab + cd
            cross[ab, cd] = (load(n), load(16 + n), load(NCOEF + n))
    inner = [(b, c) for b in range(2) for c in range(2)]
    gp, gq = [], []
    for a in range(2):
        for d in range(2):
            x = [cross[2 * a + b, 2 * d + c] for b, c in inner]
            both = sum_of(x[n][2] * q[n][0] for n in range(4))
            re = both - sum_of(x[n][1] * q[n][2] for n in range(4))
            gp.append((re, both + sum_of(x[n][0] * q[n][1] for n in range(4))))
            x = [cross[2 * b + a, 2 * c + d] for b, c in inner]
            both = sum_of(x[n][2] * p[n][0] for n in range(4))
            re = both + sum_of(x[n][1] * p[n][1] for n in range(4))
            gq.append((re, sum_of(x[n][0] * p[n][2] for n in range(4)) - both))
    diag = [load(32 + k) for k in range(4)]
    off = {pair: (load(36 + 2 * n), load(37 + 2 * n)) for n, pair in enumerate(PAIRS)}
    q00, q11, q01 = outer_q
    two = scaled(q01, 2.0)
    hp = [
        diag[0] * q00 + diag[1] * q11 + mul_conj(conj(off[0, 1]), two)[0],
        diag[2] * q00 + diag[3] * q11 + mul_conj(conj(off[2, 3]), two)[0],
        *add(
            scaled(off[0, 2], q00),
            mul(off[0, 3], q01),
            mul_conj(q01, off[1, 2]),
            scaled(off[1, 3], q11),
        ),
    ]
    r00, r11, r01 = outer(jp)
    two = scaled(r01, 2.0)
    hq = [
        diag[0] * r00 + diag[2] * r11 + mul_conj(off[0, 2], two)[0],
        diag[1] * r00 + diag[3] * r11 + mul_conj(off[1, 3], two)[0],
        *add(
            scaled(conj(off[0, 1]), r00),
            mul_conj(off[0, 3], r01),
            mul_conj(r01, off[1, 2]),
            scaled(conj(off[2, 3]), r11),
        ),
    ]
    gp = [g[0] for g in gp] + [g[1] for g in gp]
    gq = [g[0] for g in gq] + [g[1] for g in gq]
    return gp, hp, gq, hq


def kernel(
    vis_hbm, mdl_hbm, start_hbm, pen_hbm, pairs_hbm, flags_hbm, chan_hbm,
    gains_out, coeff_out,
    vis, mdl, start, pen_in, pairs, flags, chan, ends,
    vf, mf, coef, half_out, mine, every, sbuf, rbuf, prec, names, away, wsend, wrec,
    hold, jp_at, jq_at, raw, term_g, term_h, named_at, mixed, final, last, basis, scale, pen, cons, dual, ginv,
    loc, ag_s, ag_r, rs_s, rs_r, ps_s, ps_r, one,
):
    band = lax.axis_index("band")
    base = lax.axis_index("base")
    core = base % 2
    chip = base // 2
    cz = chip // SIDE
    cx = chip % SIDE
    sibling = chip * 2 + (1 - core)

    def at(dz, dx):
        return ((cz + dz) % SIDE) * SIDE + (cx + dx) % SIDE

    def copy(src, dst, send, recv, band_to, base_to):
        return pltpu.make_async_remote_copy(
            src_ref=src, dst_ref=dst, send_sem=send, recv_sem=recv,
            device_id=(band_to, base_to), device_id_type=MESH,
        )

    barrier = pltpu.get_barrier_semaphore()

    def greet(band_to, base_to):
        pl.semaphore_signal(barrier, inc=1, device_id=(band_to, base_to), device_id_type=MESH)

    for dz, dx in FAR:
        for c in range(2):
            greet(band, 2 * at(dz, dx) + c)
    for d in (2, 1, 3):
        for c in range(2):
            greet((band + d) % BANDS, 2 * chip + c)
    greet(band, sibling)

    local = [
        pltpu.make_async_copy(src, dst, loc.at[n])
        for n, (src, dst) in enumerate(
            [
                (start_hbm, start), (pairs_hbm, pairs), (flags_hbm, flags), (chan_hbm, chan),
                (pen_hbm, pen_in), (mdl_hbm, mdl), (vis_hbm, vis),
            ]
        )
    ]
    for c in local:
        c.start()

    lane8 = iota((8, LANES), 1)
    row8 = iota((8, LANES), 0)
    for c in local[:5]:
        c.wait()
    mine[...] = start[...].reshape(8 * BLOCK, SOLS).T.reshape(2, 2, SUB, LANES)
    every[0, base] = mine[core]

    for t in range(TILES):
        for side in range(2):
            ends[t, side] = pairs[t, side]
    blocks = [pairs[t, side] for t in range(TILES) for side in range(2)]
    named = jnp.zeros((8, LANES), jnp.int32)
    for e, b in enumerate(blocks):
        named = jnp.where(row8 == e, b, named)
    names[0] = named
    cell = iota((1, CELLS), 1)
    eye = (cell // BLOCK == cell % BLOCK).astype(F32)
    weights = []
    for t in range(TILES):
        same = jnp.where(blocks[2 * t] == blocks[2 * t + 1], 1.0, 0.0)
        weights.append(flags[t : t + 1, :].astype(F32) * (1.0 - same * eye))
    both = jnp.concatenate([*weights, jnp.zeros((6, CELLS), F32)], axis=0).astype(BF16)
    fold_row = iota((CELLS, LANES), 0)
    fold_lane = iota((CELLS, LANES), 1) % BLOCK
    at_first = jnp.dot(
        both, (fold_row // BLOCK == fold_lane).astype(F32).astype(BF16),
        preferred_element_type=F32,
    )
    at_second = jnp.dot(
        both, (fold_row % BLOCK == fold_lane).astype(F32).astype(BF16),
        preferred_element_type=F32,
    )
    pen_row = jnp.concatenate([pen_in[...]] * 8, axis=1)
    away[0] = jnp.concatenate(
        [at_first[0:1], at_second[0:1], at_first[1:2], at_second[1:2], pen_row]
        + [jnp.zeros((3, LANES), F32)],
        axis=0,
    )

    pl.semaphore_wait(barrier, 2 * CHIPS - 1 + 2 * (BANDS - 1))

    def send_start(half, chain, base_to):
        copy(
            mine.at[half, chain], every.at[0, base, chain], ag_s.at[chain], ag_r.at[chain],
            band, base_to,
        ).start()

    for chain in range(2):
        for dz, dx in FAR:
            for c in range(2):
                send_start(c, chain, 2 * at(dz, dx) + c)
        send_start(1 - core, chain, sibling)
    names_copy = copy(names.at[0], names.at[1], one.at[0], one.at[1], band, sibling)
    away_copy = copy(away.at[0], away.at[1], one.at[2], one.at[3], band, sibling)
    names_copy.start()
    away_copy.start()

    row = iota((SOLS, CHANS), 0)
    sol = band * SOLS + ((row // HALF + core) % 2) * HALF + row % HALF
    member = (jnp.broadcast_to(chan[...], (SOLS, CHANS)) == sol).astype(F32)
    where_c = (band * CHANS + iota((SOLS, CHANS), 1)).astype(F32)
    xpos = -1.0 + (2.0 * where_c + 1.0) / (CHANS * BANDS)
    chans = jnp.sum(member, axis=1, keepdims=True)
    centre = jnp.sum(member * xpos, axis=1, keepdims=True) / chans
    centre = jnp.broadcast_to(centre[:HALF], (HALF, LANES))
    cheb = [jnp.ones_like(centre), centre]
    for _ in range(2, NPOLY):
        cheb.append(2.0 * centre * cheb[-1] - cheb[-2])
    for k in range(NPOLY):
        basis[k] = cheb[k]
    member3 = jnp.concatenate([member] * 3, axis=1).astype(BF16)

    for c in local[5:]:
        c.wait()

    def collapse(t, carry):
        w = jnp.where(t == 0, weights[0], weights[1])
        for k in range(8):
            vf[k] = vis[k, t].astype(F32)
            mf[k] = mdl[k, t].astype(F32) * w

        def put(n, product):
            high = product.astype(BF16)
            rest = product - high.astype(F32)
            middle = rest.astype(BF16)
            low = (rest - middle.astype(F32)).astype(BF16)
            out = jnp.dot(
                member3, jnp.concatenate([high, middle, low], axis=0), preferred_element_type=F32
            )
            coef[t, n] = out[:HALF]
            half_out[t, n] = out[HALF:]

        for ab in range(4):
            vr, vi = vf[ab], vf[4 + ab]
            for cd in range(4):
                mr, mi = mf[cd], mf[4 + cd]
                put(4 * ab + cd, vr * mr + vi * mi)
                put(16 + 4 * ab + cd, vi * mr - vr * mi)
        for ab in range(4):
            put(32 + ab, mf[ab] * mf[ab] + mf[4 + ab] * mf[4 + ab])
        for n, (x, y) in enumerate(PAIRS):
            put(36 + 2 * n, mf[x] * mf[y] + mf[4 + x] * mf[4 + y])
            put(37 + 2 * n, mf[4 + x] * mf[y] - mf[x] * mf[4 + y])
        copy(
            half_out.at[t], coef.at[TILES + t, pl.ds(0, NCOEF)], one.at[4], one.at[5], band, sibling
        ).start()
        return carry

    lax.fori_loop(0, TILES, collapse, 0)

    names_copy.wait_recv()
    away_copy.wait_recv()
    for t in range(TILES):
        for side in range(2):
            ends[TILES + t, side] = names[1, 2 * t + side, 0]

    def weight_rows(k):
        out = jnp.zeros((8, LANES), F32)
        for own in range(2):
            for e in range(2 * TILES):
                hit = row8 + 2 * k == names[own, e : e + 1, :]
                at_end = jnp.broadcast_to(away[own, e : e + 1, :], (8, LANES))
                out = out + jnp.where(hit, at_end, 0.0)
        return out

    for dz, dx in FAR:
        k = at(dz, dx)
        wsend[k] = weight_rows(k)
        copy(
            wsend.at[k], wrec.at[chip], one.at[6], one.at[7], band, 2 * k + core
        ).start()
    wrec[chip] = weight_rows(chip)
    own_pen = jnp.broadcast_to(away[0, 4:5, :], (SUB, LANES))
    its_pen = jnp.broadcast_to(away[1, 4:5, :], (SUB, LANES))
    pen[...] = jnp.concatenate(
        [jnp.where(core == 0, own_pen, its_pen), jnp.where(core == 0, its_pen, own_pen)], axis=0
    )
    for own in range(2):
        for e in range(2 * TILES):
            named_at[2 * TILES * own + e] = jnp.broadcast_to(names[own, e : e + 1, :], (8, LANES))

    def arrived(ref, sem):
        pltpu.make_async_copy(ref, ref, sem).wait()

    arrived(half_out, one.at[5])
    for t in range(2 * TILES):
        for n in range(16):
            coef[t, NCOEF + n] = coef[t, n] + coef[t, 16 + n]

    pad = [jnp.zeros((16 - NPOLY, LANES), F32)]
    me = 2 * band + core

    def along_basis(part):
        return [jnp.sum(basis[k] * part, axis=0, keepdims=True) for k in range(NPOLY)] + pad

    def of_block(b):
        return jnp.concatenate([mixed[c, SUB * b : SUB * (b + 1), :] for c in range(2)], axis=0)

    def total_of(it):
        column = iota((HALF, LANES), 1)
        columns = jnp.zeros((HALF, LANES), F32)
        for k in range(NPOLY):
            columns = jnp.where(column == k, basis[k], columns)
        out = along_basis(of_block(0)) + along_basis(of_block(1)) + along_basis(columns)
        prec[it, me] = jnp.concatenate(out, axis=0)

        def send(band_to, base_to):
            copy(
                prec.at[it, me], prec.at[it, me], ps_s.at[it], ps_r.at[it], band_to, base_to
            ).start()

        for d in (2, 1, 3):
            for c in range(2):
                send((band + d) % BANDS, 2 * chip + c)
        send(band, sibling)

    def total_at(it):
        arrived(prec.at[it, pl.ds(0, 2 * BANDS - 1)], ps_r.at[it])
        return functools.reduce(lambda a, b: a + b, [prec[it, k] for k in range(2 * BANDS)])

    def solve_gram(rhs):
        x = ginv[0] * rhs[0:1, :]
        for k in range(1, NPOLY):
            x = x + ginv[k] * rhs[k : k + 1, :]
        return x

    def from_total(total, first):
        @pl.when(first)
        def _():
            r, l = iota((16, LANES), 0), iota((16, LANES), 1)
            m = total[32:, :] + jnp.where((r == l) & (r < NPOLY), RIDGE, 0.0)
            m = m + jnp.where((l == r + 16) & (r < NPOLY), 1.0, 0.0)
            for p in range(NPOLY):
                pivot = m[p : p + 1, :] / m[p : p + 1, p : p + 1]
                m = jnp.where(r == p, pivot, m - m[:, p : p + 1] * pivot)
            for k in range(NPOLY):
                ginv[k] = jnp.broadcast_to(m[:, 16 + k : 17 + k], (16, LANES))

        return [solve_gram(total[16 * b : 16 * b + 16, :]) for b in range(2)]

    inner = lane8 % BLOCK
    station = lane8 // BLOCK
    natural_g = (lane8 % 8) * BLOCK + (inner // 8) * 8 + station
    natural_h = (lane8 % 8) * BLOCK + (inner // 8) * 8 + (station % 4) * 2
    own_blocks = pl.ds(2 * chip, 2)

    def tile_terms(it, c):
        rows = pl.ds(pl.multiple_of(SUB * c, SUB), SUB)
        tiles = range(2 * TILES)
        hold[...] = every[it, :, c]
        of_p = [hold[ends[t, 0]] for t in tiles]
        of_q = [hold[ends[t, 1]] for t in tiles]
        for k in range(8):
            for t in tiles:
                jq_at[t, k] = lanes(of_q[t], k * BLOCK + inner)
        for k in range(8):
            for half in range(2):
                for t in tiles:
                    jp_at[t, half, k] = lanes(of_p[t], k * BLOCK + half * 8 + station)
        for t in tiles:
            jq = [jq_at[t, k] for k in range(8)]
            sums = []
            outer_q = outer(jq)
            for half in range(2):
                jp = [jp_at[t, half, k] for k in range(8)]

                def load(n):
                    return coef[t, n, rows, pl.ds(half * LANES, LANES)]

                gp, hp, gq, hq = station_terms(load, jp, jq, outer_q)
                for n, x in enumerate(gp):
                    raw[t, 8 * half + n] = x
                for n, x in enumerate(hp):
                    raw[t, 16 + 4 * half + n] = x
                sums.append(gq + hq)
            for n, (x, y) in enumerate(zip(*sums)):
                raw[t, 24 + n] = x + y
        gp = [[raw[t, n] for n in range(16)] for t in tiles]
        hp = [[raw[t, 16 + n] for n in range(8)] for t in tiles]
        gq = [[raw[t, 24 + n] for n in range(8)] for t in tiles]
        hq = [[raw[t, 32 + n] for n in range(4)] for t in tiles]
        gp, hp, gq = level(gp, lane8, 8), level(hp, lane8, 8), level(gq, lane8, 64)
        gp, hp, gq, hq = [level(x, lane8, b) for x, b in ((gp, 4), (hp, 4), (gq, 32), (hq, 32))]
        gp, hp, gq, hq = [level(x, lane8, b) for x, b in ((gp, 2), (hp, 2), (gq, 16), (hq, 16))]
        gp = [x for (x,) in level(gp, lane8, 1)]
        hp = [x + lanes(x, lane8 ^ 1) for (x,) in hp]
        gq = [x for (x,) in gq]
        hq = [x + pltpu.roll(x, 64, 1) for (x,) in hq]
        for t in tiles:
            term_g[2 * t] = lanes(gp[t], natural_g)
            term_g[2 * t + 1] = gq[t]
            term_h[2 * t] = lanes(hp[t], natural_h)
            term_h[2 * t + 1] = hq[t]

    def share(k):
        out = [jnp.zeros((SUB, LANES), F32) for _ in range(3)]
        side = 2 * k + lane8 // 64
        for e in range(4 * TILES):
            name = named_at[e]
            out[0] = out[0] + jnp.where(name == 2 * k, term_g[e], 0.0)
            out[1] = out[1] + jnp.where(name == 2 * k + 1, term_g[e], 0.0)
            out[2] = out[2] + jnp.where(name == side, term_h[e], 0.0)
        return jnp.concatenate(out, axis=0)

    lane = iota((HALF, LANES), 1)

    def solve(it, c):
        normal = functools.reduce(lambda x, y: x + y, [rbuf[it, c, k] for k in range(CHIPS)])
        part = lane % BLOCK
        upper = (lane & BLOCK) != 0
        sign = jnp.where(upper == (lane < 64), 1.0, -1.0)
        packed = normal[2 * SUB :, :]
        both = jnp.concatenate([packed, packed], axis=0)
        part = part + 64 * (iota((HALF, LANES), 0) // SUB)
        per = scale[c]
        rho = pen[...]
        rhs = normal[: 2 * SUB, :] * per + rho * (cons[c] - dual[c])
        h_diag = lanes(both, jnp.where(upper, part, BLOCK + part)) * per + rho
        h_swap = lanes(both, jnp.where(upper, BLOCK + part, part)) * per + rho
        h_real = lanes(both, 2 * BLOCK + part) * per
        h_imag = lanes(both, 3 * BLOCK + part) * per
        determ = h_diag * h_swap - h_real * h_real - h_imag * h_imag
        return (
            rhs * h_diag
            - lanes(rhs, lane ^ BLOCK) * h_real
            + sign * lanes(rhs, lane ^ (64 + BLOCK)) * h_imag
        ) / determ

    def iteration(it, carry):
        def send_terms(c, carry):
            chain = 2 * it + c

            @pl.when(it > 0)
            def _():
                arrived(every.at[it, pl.ds(0, 2 * CHIPS - 2), c], ag_r.at[chain])

            @pl.when(it == 0)
            def _():
                arrived(every.at[0, pl.ds(0, 2 * CHIPS - 1), c], ag_r.at[c])

            tile_terms(it, c)
            for dz, dx in FAR:
                k = at(dz, dx)
                sbuf[it, c, k] = share(k)
                copy(
                    sbuf.at[it, c, k], rbuf.at[it, c, chip], rs_s.at[chain], rs_r.at[chain],
                    band, 2 * k + core,
                ).start()
            rbuf[it, c, chip] = share(chip)
            return carry

        lax.fori_loop(0, 2, send_terms, 0)

        @pl.when(it > 0)
        def _():
            coeff = from_total(total_at(it - 1), it == 1)
            for b in range(2):
                agreed = basis[0] * coeff[b][0:1, :]
                for k in range(1, NPOLY):
                    agreed = agreed + basis[k] * coeff[b][k : k + 1, :]
                rows = pl.ds(SUB * b, SUB)
                for c in range(2):
                    new = agreed[SUB * c : SUB * (c + 1), :]
                    dual[c, rows] = mixed[c, rows] - new
                    cons[c, rows] = new

        @pl.when(it == 0)
        def _():
            for c in range(2):
                for b in range(2):
                    cons[c, pl.ds(SUB * b, SUB)] = every[0, 2 * chip + b, c]
            dual[...] = jnp.zeros((2, HALF, LANES), F32)

        @pl.when(it == 0)
        def _():
            arrived(wrec.at[pl.ds(0, CHIPS - 1)], one.at[7])
            total = functools.reduce(lambda a, b: a + b, [wrec[k] for k in range(CHIPS)])
            for c in range(2):
                for b in range(2):
                    at_station = jnp.broadcast_to(total[b : b + 1, :], (SUB, LANES))
                    counts = chans[SUB * c : SUB * (c + 1)] * at_station
                    scale[c, pl.ds(SUB * b, SUB)] = 1.0 / jnp.maximum(counts, 1.0)

        def send_gains(c, carry):
            chain = 2 * it + c
            arrived(rbuf.at[it, c, pl.ds(0, CHIPS - 1)], rs_r.at[chain])
            solved = solve(it, c)
            every[it + 1, 2 * chip, c] = solved[:SUB]
            every[it + 1, 2 * chip + 1, c] = solved[SUB:]

            @pl.when(it + 1 < ITERS)
            def _():
                for dz, dx in FAR:
                    copy(
                        every.at[it + 1, own_blocks, c], every.at[it + 1, own_blocks, c],
                        ag_s.at[chain + 2], ag_r.at[chain + 2], band, 2 * at(dz, dx) + core,
                    ).start()

            mixed[c] = solved + dual[c]
            return carry

        lax.fori_loop(0, 2, send_gains, 0)

        @pl.when(it + 1 < ITERS)
        def _():
            total_of(it)

        return carry

    lax.fori_loop(0, ITERS, iteration, 0)

    for c in range(2):
        last[c] = jnp.concatenate(along_basis(of_block(c)), axis=0)

    def send_last(c, band_to, base_to):
        copy(
            last.at[c], last.at[2 + me], one.at[10], one.at[11], band_to, base_to
        ).start()

    for d in (2, 1, 3):
        for c in range(2):
            send_last(c, (band + d) % BANDS, 2 * chip + c)
    send_last(1 - core, band, sibling)
    final_copy = copy(
        every.at[ITERS, sibling], final.at[core], one.at[8], one.at[9], band, sibling
    )
    final_copy.start()
    last[2 + me] = last[core]
    final[core] = every[ITERS, base]
    final_copy.wait_recv()
    gains_out[...] = final[...].reshape(SOLS, LANES).T.reshape(8, BLOCK, SOLS)
    arrived(last.at[pl.ds(0, 2 * BANDS - 1)], one.at[11])
    coeff = solve_gram(
        functools.reduce(lambda a, b: a + b, [last[2 + k] for k in range(2 * BANDS)])
    )
    for k in range(8):
        coeff_out[:, k, :] = coeff[:NPOLY, k * BLOCK : (k + 1) * BLOCK]

    names_copy.wait_send()
    away_copy.wait_send()
    final_copy.wait_send()
    arrived(half_out, one.at[4])
    arrived(wsend.at[pl.ds(0, CHIPS - 1)], one.at[6])
    for c in range(2):
        arrived(every.at[0, pl.ds(0, 2 * CHIPS - 1), c], ag_s.at[c])
    for it in range(ITERS):
        for c in range(2):
            if it > 0:
                arrived(every.at[it, pl.ds(0, 2 * CHIPS - 2), c], ag_s.at[2 * it + c])
            arrived(sbuf.at[it, c, pl.ds(0, CHIPS - 1)], rs_s.at[2 * it + c])
        if it + 1 < ITERS:
            arrived(prec.at[it, pl.ds(0, 2 * BANDS - 1)], ps_s.at[it])
    arrived(last.at[pl.ds(0, 2 * BANDS - 1)], one.at[10])


def on_device(visibilities, model, start_gains, penalty, pairs, flags, chan_band):
    vmem, dma = pltpu.VMEM, pltpu.SemaphoreType.DMA
    gains, coeff = pl.pallas_call(
        kernel,
        out_shape=(
            jax.ShapeDtypeStruct((8, BLOCK, SOLS), F32),
            jax.ShapeDtypeStruct((NPOLY, 8, BLOCK), F32),
        ),
        in_specs=[pl.BlockSpec(memory_space=pltpu.HBM)] * 7,
        out_specs=(pl.BlockSpec(memory_space=vmem), pl.BlockSpec(memory_space=vmem)),
        scratch_shapes=[
            vmem((8, TILES, CHANS, CELLS), BF16),
            vmem((8, TILES, CHANS, CELLS), BF16),
            vmem((8, BLOCK, SOLS), F32),
            vmem((1, BLOCK), F32),
            pltpu.SMEM((TILES, 2), jnp.int32),
            vmem((TILES, CELLS), jnp.int32),
            vmem((1, CHANS), jnp.int32),
            pltpu.SMEM((2 * TILES, 2), jnp.int32),
            vmem((8, CHANS, CELLS), F32),
            vmem((8, CHANS, CELLS), F32),
            vmem((2 * TILES, NCOEF + 16, HALF, CELLS), F32),
            vmem((TILES, NCOEF, HALF, CELLS), F32),
            vmem((2, 2, SUB, LANES), F32),
            vmem((ITERS + 1, 2 * CHIPS, 2, SUB, LANES), F32),
            vmem((ITERS, 2, CHIPS, ROWS, LANES), F32),
            vmem((ITERS, 2, CHIPS, ROWS, LANES), F32),
            vmem((ITERS, 2 * BANDS, 48, LANES), F32),
            vmem((2, 8, LANES), jnp.int32),
            vmem((2, 8, LANES), F32),
            vmem((CHIPS, 8, LANES), F32),
            vmem((CHIPS, 8, LANES), F32),
            vmem((2 * CHIPS, SUB, LANES), F32),
            vmem((2 * TILES, 2, 8, SUB, LANES), F32),
            vmem((2 * TILES, 8, SUB, LANES), F32),
            vmem((2 * TILES, 36, SUB, LANES), F32),
            vmem((4 * TILES, SUB, LANES), F32),
            vmem((4 * TILES, SUB, LANES), F32),
            vmem((4 * TILES, SUB, LANES), jnp.int32),
            vmem((2, HALF, LANES), F32),
            vmem((2, 2, SUB, LANES), F32),
            vmem((2 + 2 * BANDS, 16, LANES), F32),
            vmem((NPOLY, HALF, LANES), F32),
            vmem((2, HALF, LANES), F32),
            vmem((HALF, LANES), F32),
            vmem((2, HALF, LANES), F32),
            vmem((2, HALF, LANES), F32),
            vmem((NPOLY, 16, LANES), F32),
            dma((7,)),
            *[dma((2 * ITERS,))] * 4,
            *[dma((ITERS,))] * 2,
            dma((12,)),
        ],
        compiler_params=pltpu.CompilerParams(
            collective_id=0, has_side_effects=True, vmem_limit_bytes=40 * 1024 * 1024
        ),
        cost_estimate=pl.CostEstimate(
            flops=60_000_000, bytes_accessed=3_000_000, transcendentals=0
        ),
        name="admm",
    )(
        *[
            pltpu.with_memory_space_constraint(x, pltpu.HBM)
            for x in (
                visibilities, model, jnp.swapaxes(start_gains, 1, 2), penalty.reshape(1, BLOCK),
                pairs, flags, chan_band.reshape(1, CHANS),
            )
        ]
    )
    return jnp.swapaxes(gains, 1, 2), jnp.swapaxes(coeff, 0, 1)


def solution(mesh):
    in_specs = (
        P(None, "base", "band", None),
        P(None, "base", "band", None),
        P(None, "band", "base"),
        P("base"),
        P("base", None),
        P("base", None),
        P("band"),
    )
    out_specs = (P(None, "band", "base"), P(None, None, "base"))
    return jax.shard_map(
        on_device, mesh=mesh, in_specs=in_specs, out_specs=out_specs, check_vma=False
    )
```

```python
import functools

import jax
import jax.numpy as jnp
from jax import lax
from jax.experimental import pallas as pl
from jax.experimental.pallas import tpu as pltpu
from jax.sharding import PartitionSpec as P

BLOCK = 16
NPOLY = 9
ITERS = 3
RIDGE = 0.5
MESH = pl.DeviceIdType.MESH
F32 = jnp.float32
BF16 = jnp.bfloat16
SIDE = 4
CHIPS = SIDE * SIDE
BANDS = 4
TILES = 2
CHANS = 64
CELLS = BLOCK * BLOCK
SOLS = 32
LANES = 128
HALF = SOLS // 2
SUB = HALF // 2
ROWS = 3 * SUB
FAR = sorted(
    [(dz, dx) for dx in range(SIDE) for dz in range(SIDE) if dz or dx],
    key=lambda d: -sum(min(n, SIDE - n) for n in d),
)
NCOEF = 48
PAIRS = [(0, 1), (0, 2), (0, 3), (1, 2), (1, 3), (2, 3)]


def lanes(x, idx):
    numbers = lax.GatherDimensionNumbers(
        offset_dims=(),
        collapsed_slice_dims=(1,),
        start_index_map=(1,),
        operand_batching_dims=(0,),
        start_indices_batching_dims=(0,),
    )
    return lax.gather(
        x, idx[..., None], numbers, (1, 1), mode=lax.GatherScatterMode.PROMISE_IN_BOUNDS
    )


def iota(shape, axis):
    return lax.broadcasted_iota(jnp.int32, shape, axis)


def merge(a, b, lane, bit):
    clear = (lane & bit) == 0
    return jnp.where(clear, a, b) + lanes(jnp.where(clear, b, a), lane ^ bit)


def level(jobs, lane, bit):
    half = len(jobs[0]) // 2
    return [[merge(a, b, lane, bit) for a, b in zip(job[:half], job[half:])] for job in jobs]


def mul(a, b):
    return (a[0] * b[0] - a[1] * b[1], a[0] * b[1] + a[1] * b[0])


def mul_conj(a, b):
    return (a[0] * b[0] + a[1] * b[1], a[0] * b[1] - a[1] * b[0])


def conj(a):
    return (a[0], -a[1])


def add(*terms):
    re, im = terms[0]
    for t in terms[1:]:
        re, im = re + t[0], im + t[1]
    return (re, im)


def scaled(a, r):
    return (a[0] * r, a[1] * r)


def outer(j):
    c = [(j[k], j[4 + k]) for k in range(4)]
    q00 = c[0][0] * c[0][0] + c[0][1] * c[0][1] + c[2][0] * c[2][0] + c[2][1] * c[2][1]
    q11 = c[1][0] * c[1][0] + c[1][1] * c[1][1] + c[3][0] * c[3][0] + c[3][1] * c[3][1]
    q01 = add(mul_conj(c[0], c[1]), mul_conj(c[2], c[3]))
    return q00, q11, q01


def sum_of(terms):
    return functools.reduce(lambda a, b: a + b, terms)


def station_terms(load, jp, jq, outer_q):
    p = [(jp[k], jp[4 + k] - jp[k], jp[4 + k] + jp[k]) for k in range(4)]
    q = [(jq[k], jq[4 + k] - jq[k], jq[4 + k] + jq[k]) for k in range(4)]
    cross = {}
    for ab in range(4):
        for cd in range(4):
            n = 4 * ab + cd
            cross[ab, cd] = (load(n), load(16 + n), load(NCOEF + n))
    inner = [(b, c) for b in range(2) for c in range(2)]
    gp, gq = [], []
    for a in range(2):
        for d in range(2):
            x = [cross[2 * a + b, 2 * d + c] for b, c in inner]
            both = sum_of(x[n][2] * q[n][0] for n in range(4))
            re = both - sum_of(x[n][1] * q[n][2] for n in range(4))
            gp.append((re, both + sum_of(x[n][0] * q[n][1] for n in range(4))))
            x = [cross[2 * b + a, 2 * c + d] for b, c in inner]
            both = sum_of(x[n][2] * p[n][0] for n in range(4))
            re = both + sum_of(x[n][1] * p[n][1] for n in range(4))
            gq.append((re, sum_of(x[n][0] * p[n][2] for n in range(4)) - both))
    diag = [load(32 + k) for k in range(4)]
    off = {pair: (load(36 + 2 * n), load(37 + 2 * n)) for n, pair in enumerate(PAIRS)}
    q00, q11, q01 = outer_q
    two = scaled(q01, 2.0)
    hp = [
        diag[0] * q00 + diag[1] * q11 + mul_conj(conj(off[0, 1]), two)[0],
        diag[2] * q00 + diag[3] * q11 + mul_conj(conj(off[2, 3]), two)[0],
        *add(
            scaled(off[0, 2], q00),
            mul(off[0, 3], q01),
            mul_conj(q01, off[1, 2]),
            scaled(off[1, 3], q11),
        ),
    ]
    r00, r11, r01 = outer(jp)
    two = scaled(r01, 2.0)
    hq = [
        diag[0] * r00 + diag[2] * r11 + mul_conj(off[0, 2], two)[0],
        diag[1] * r00 + diag[3] * r11 + mul_conj(off[1, 3], two)[0],
        *add(
            scaled(conj(off[0, 1]), r00),
            mul_conj(off[0, 3], r01),
            mul_conj(r01, off[1, 2]),
            scaled(conj(off[2, 3]), r11),
        ),
    ]
    gp = [g[0] for g in gp] + [g[1] for g in gp]
    gq = [g[0] for g in gq] + [g[1] for g in gq]
    return gp, hp, gq, hq


def kernel(
    vis_hbm, mdl_hbm, start_hbm, pen_hbm, pairs_hbm, flags_hbm, chan_hbm,
    gains_out, coeff_out,
    vis, mdl, start, pen_in, pairs, flags, chan, ends,
    vf, mf, coef, half_out, mine, every, sbuf, rbuf, prec, names, away, wsend, wrec,
    hold, jp_at, jq_at, raw, term_g, term_h, named_at, mixed, final, last, basis, scale, pen, cons, dual, ginv,
    loc, ag_s, ag_r, rs_s, rs_r, ps_s, ps_r, one,
):
    band = lax.axis_index("band")
    base = lax.axis_index("base")
    core = base % 2
    chip = base // 2
    cz = chip // SIDE
    cx = chip % SIDE
    sibling = chip * 2 + (1 - core)

    def at(dz, dx):
        return ((cz + dz) % SIDE) * SIDE + (cx + dx) % SIDE

    def copy(src, dst, send, recv, band_to, base_to):
        return pltpu.make_async_remote_copy(
            src_ref=src, dst_ref=dst, send_sem=send, recv_sem=recv,
            device_id=(band_to, base_to), device_id_type=MESH,
        )

    barrier = pltpu.get_barrier_semaphore()

    def greet(band_to, base_to):
        pl.semaphore_signal(barrier, inc=1, device_id=(band_to, base_to), device_id_type=MESH)

    for dz, dx in FAR:
        for c in range(2):
            greet(band, 2 * at(dz, dx) + c)
    for d in (2, 1, 3):
        for c in range(2):
            greet((band + d) % BANDS, 2 * chip + c)
    greet(band, sibling)

    local = [
        pltpu.make_async_copy(src, dst, loc.at[n])
        for n, (src, dst) in enumerate(
            [
                (start_hbm, start), (pairs_hbm, pairs), (flags_hbm, flags), (chan_hbm, chan),
                (pen_hbm, pen_in), (mdl_hbm, mdl), (vis_hbm, vis),
            ]
        )
    ]
    for c in local:
        c.start()

    lane8 = iota((8, LANES), 1)
    row8 = iota((8, LANES), 0)
    for c in local[:5]:
        c.wait()
    mine[...] = start[...].reshape(8 * BLOCK, SOLS).T.reshape(2, 2, SUB, LANES)
    every[0, base] = mine[core]

    for t in range(TILES):
        for side in range(2):
            ends[t, side] = pairs[t, side]
    blocks = [pairs[t, side] for t in range(TILES) for side in range(2)]
    named = jnp.zeros((8, LANES), jnp.int32)
    for e, b in enumerate(blocks):
        named = jnp.where(row8 == e, b, named)
    names[0] = named
    cell = iota((1, CELLS), 1)
    eye = (cell // BLOCK == cell % BLOCK).astype(F32)
    weights = []
    for t in range(TILES):
        same = jnp.where(blocks[2 * t] == blocks[2 * t + 1], 1.0, 0.0)
        weights.append(flags[t : t + 1, :].astype(F32) * (1.0 - same * eye))
    both = jnp.concatenate([*weights, jnp.zeros((6, CELLS), F32)], axis=0).astype(BF16)
    fold_row = iota((CELLS, LANES), 0)
    fold_lane = iota((CELLS, LANES), 1) % BLOCK
    at_first = jnp.dot(
        both, (fold_row // BLOCK == fold_lane).astype(F32).astype(BF16),
        preferred_element_type=F32,
    )
    at_second = jnp.dot(
        both, (fold_row % BLOCK == fold_lane).astype(F32).astype(BF16),
        preferred_element_type=F32,
    )
    pen_row = jnp.concatenate([pen_in[...]] * 8, axis=1)
    away[0] = jnp.concatenate(
        [at_first[0:1], at_second[0:1], at_first[1:2], at_second[1:2], pen_row]
        + [jnp.zeros((3, LANES), F32)],
        axis=0,
    )

    pl.semaphore_wait(barrier, 2 * CHIPS - 1 + 2 * (BANDS - 1))

    def send_start(half, chain, base_to):
        copy(
            mine.at[half, chain], every.at[0, base, chain], ag_s.at[chain], ag_r.at[chain],
            band, base_to,
        ).start()

    for chain in range(2):
        for dz, dx in FAR:
            for c in range(2):
                send_start(c, chain, 2 * at(dz, dx) + c)
        send_start(1 - core, chain, sibling)
    names_copy = copy(names.at[0], names.at[1], one.at[0], one.at[1], band, sibling)
    away_copy = copy(away.at[0], away.at[1], one.at[2], one.at[3], band, sibling)
    names_copy.start()
    away_copy.start()

    row = iota((SOLS, CHANS), 0)
    sol = band * SOLS + ((row // HALF + core) % 2) * HALF + row % HALF
    member = (jnp.broadcast_to(chan[...], (SOLS, CHANS)) == sol).astype(F32)
    where_c = (band * CHANS + iota((SOLS, CHANS), 1)).astype(F32)
    xpos = -1.0 + (2.0 * where_c + 1.0) / (CHANS * BANDS)
    chans = jnp.sum(member, axis=1, keepdims=True)
    centre = jnp.sum(member * xpos, axis=1, keepdims=True) / chans
    centre = jnp.broadcast_to(centre[:HALF], (HALF, LANES))
    cheb = [jnp.ones_like(centre), centre]
    for _ in range(2, NPOLY):
        cheb.append(2.0 * centre * cheb[-1] - cheb[-2])
    for k in range(NPOLY):
        basis[k] = cheb[k]
    member3 = jnp.concatenate([member] * 3, axis=1).astype(BF16)

    for c in local[5:]:
        c.wait()

    def collapse(t, carry):
        w = jnp.where(t == 0, weights[0], weights[1])
        for k in range(8):
            vf[k] = vis[k, t].astype(F32)
            mf[k] = mdl[k, t].astype(F32) * w

        def put(n, product):
            high = product.astype(BF16)
            rest = product - high.astype(F32)
            middle = rest.astype(BF16)
            low = (rest - middle.astype(F32)).astype(BF16)
            out = jnp.dot(
                member3, jnp.concatenate([high, middle, low], axis=0), preferred_element_type=F32
            )
            coef[t, n] = out[:HALF]
            half_out[t, n] = out[HALF:]

        for ab in range(4):
            vr, vi = vf[ab], vf[4 + ab]
            for cd in range(4):
                mr, mi = mf[cd], mf[4 + cd]
                put(4 * ab + cd, vr * mr + vi * mi)
                put(16 + 4 * ab + cd, vi * mr - vr * mi)
        for ab in range(4):
            put(32 + ab, mf[ab] * mf[ab] + mf[4 + ab] * mf[4 + ab])
        for n, (x, y) in enumerate(PAIRS):
            put(36 + 2 * n, mf[x] * mf[y] + mf[4 + x] * mf[4 + y])
            put(37 + 2 * n, mf[4 + x] * mf[y] - mf[x] * mf[4 + y])
        copy(
            half_out.at[t], coef.at[TILES + t, pl.ds(0, NCOEF)], one.at[4], one.at[5], band, sibling
        ).start()
        return carry

    lax.fori_loop(0, TILES, collapse, 0)

    names_copy.wait_recv()
    away_copy.wait_recv()
    for t in range(TILES):
        for side in range(2):
            ends[TILES + t, side] = names[1, 2 * t + side, 0]

    def weight_rows(k):
        out = jnp.zeros((8, LANES), F32)
        for own in range(2):
            for e in range(2 * TILES):
                hit = row8 + 2 * k == names[own, e : e + 1, :]
                at_end = jnp.broadcast_to(away[own, e : e + 1, :], (8, LANES))
                out = out + jnp.where(hit, at_end, 0.0)
        return out

    for dz, dx in FAR:
        k = at(dz, dx)
        wsend[k] = weight_rows(k)
        copy(
            wsend.at[k], wrec.at[chip], one.at[6], one.at[7], band, 2 * k + core
        ).start()
    wrec[chip] = weight_rows(chip)
    own_pen = jnp.broadcast_to(away[0, 4:5, :], (SUB, LANES))
    its_pen = jnp.broadcast_to(away[1, 4:5, :], (SUB, LANES))
    pen[...] = jnp.concatenate(
        [jnp.where(core == 0, own_pen, its_pen), jnp.where(core == 0, its_pen, own_pen)], axis=0
    )
    for own in range(2):
        for e in range(2 * TILES):
            named_at[2 * TILES * own + e] = jnp.broadcast_to(names[own, e : e + 1, :], (8, LANES))

    def arrived(ref, sem):
        pltpu.make_async_copy(ref, ref, sem).wait()

    arrived(half_out, one.at[5])
    for t in range(2 * TILES):
        for n in range(16):
            coef[t, NCOEF + n] = coef[t, n] + coef[t, 16 + n]

    pad = [jnp.zeros((16 - NPOLY, LANES), F32)]
    me = 2 * band + core

    def along_basis(part):
        return [jnp.sum(basis[k] * part, axis=0, keepdims=True) for k in range(NPOLY)] + pad

    def of_block(b):
        return jnp.concatenate([mixed[c, SUB * b : SUB * (b + 1), :] for c in range(2)], axis=0)

    def total_of(it):
        column = iota((HALF, LANES), 1)
        columns = jnp.zeros((HALF, LANES), F32)
        for k in range(NPOLY):
            columns = jnp.where(column == k, basis[k], columns)
        out = along_basis(of_block(0)) + along_basis(of_block(1)) + along_basis(columns)
        prec[it, me] = jnp.concatenate(out, axis=0)

        def send(band_to, base_to):
            copy(
                prec.at[it, me], prec.at[it, me], ps_s.at[it], ps_r.at[it], band_to, base_to
            ).start()

        for d in (2, 1, 3):
            for c in range(2):
                send((band + d) % BANDS, 2 * chip + c)
        send(band, sibling)

    def total_at(it):
        arrived(prec.at[it, pl.ds(0, 2 * BANDS - 1)], ps_r.at[it])
        return functools.reduce(lambda a, b: a + b, [prec[it, k] for k in range(2 * BANDS)])

    def solve_gram(rhs):
        x = ginv[0] * rhs[0:1, :]
        for k in range(1, NPOLY):
            x = x + ginv[k] * rhs[k : k + 1, :]
        return x

    def from_total(total, first):
        @pl.when(first)
        def _():
            r, l = iota((16, LANES), 0), iota((16, LANES), 1)
            m = total[32:, :] + jnp.where((r == l) & (r < NPOLY), RIDGE, 0.0)
            m = m + jnp.where((l == r + 16) & (r < NPOLY), 1.0, 0.0)
            for p in range(NPOLY):
                pivot = m[p : p + 1, :] / m[p : p + 1, p : p + 1]
                m = jnp.where(r == p, pivot, m - m[:, p : p + 1] * pivot)
            for k in range(NPOLY):
                ginv[k] = jnp.broadcast_to(m[:, 16 + k : 17 + k], (16, LANES))

        return [solve_gram(total[16 * b : 16 * b + 16, :]) for b in range(2)]

    inner = lane8 % BLOCK
    station = lane8 // BLOCK
    natural_g = (lane8 % 8) * BLOCK + (inner // 8) * 8 + station
    natural_h = (lane8 % 8) * BLOCK + (inner // 8) * 8 + (station % 4) * 2
    own_blocks = pl.ds(2 * chip, 2)

    def tile_terms(it, c):
        rows = pl.ds(pl.multiple_of(SUB * c, SUB), SUB)
        tiles = range(2 * TILES)
        hold[...] = every[it, :, c]
        of_p = [hold[ends[t, 0]] for t in tiles]
        of_q = [hold[ends[t, 1]] for t in tiles]
        for k in range(8):
            for t in tiles:
                jq_at[t, k] = lanes(of_q[t], k * BLOCK + inner)
        for k in range(8):
            for half in range(2):
                for t in tiles:
                    jp_at[t, half, k] = lanes(of_p[t], k * BLOCK + half * 8 + station)
        for t in tiles:
            jq = [jq_at[t, k] for k in range(8)]
            sums = []
            outer_q = outer(jq)
            for half in range(2):
                jp = [jp_at[t, half, k] for k in range(8)]

                def load(n):
                    return coef[t, n, rows, pl.ds(half * LANES, LANES)]

                gp, hp, gq, hq = station_terms(load, jp, jq, outer_q)
                for n, x in enumerate(gp):
                    raw[t, 8 * half + n] = x
                for n, x in enumerate(hp):
                    raw[t, 16 + 4 * half + n] = x
                sums.append(gq + hq)
            for n, (x, y) in enumerate(zip(*sums)):
                raw[t, 24 + n] = x + y
        gp = [[raw[t, n] for n in range(16)] for t in tiles]
        hp = [[raw[t, 16 + n] for n in range(8)] for t in tiles]
        gq = [[raw[t, 24 + n] for n in range(8)] for t in tiles]
        hq = [[raw[t, 32 + n] for n in range(4)] for t in tiles]
        gp, hp, gq = level(gp, lane8, 8), level(hp, lane8, 8), level(gq, lane8, 64)
        gp, hp, gq, hq = [level(x, lane8, b) for x, b in ((gp, 4), (hp, 4), (gq, 32), (hq, 32))]
        gp, hp, gq, hq = [level(x, lane8, b) for x, b in ((gp, 2), (hp, 2), (gq, 16), (hq, 16))]
        gp = [x for (x,) in level(gp, lane8, 1)]
        hp = [x + lanes(x, lane8 ^ 1) for (x,) in hp]
        gq = [x for (x,) in gq]
        hq = [x + pltpu.roll(x, 64, 1) for (x,) in hq]
        for t in tiles:
            term_g[2 * t] = lanes(gp[t], natural_g)
            term_g[2 * t + 1] = gq[t]
            term_h[2 * t] = lanes(hp[t], natural_h)
            term_h[2 * t + 1] = hq[t]

    def share(k):
        out = [jnp.zeros((SUB, LANES), F32) for _ in range(3)]
        side = 2 * k + lane8 // 64
        for e in range(4 * TILES):
            name = named_at[e]
            out[0] = out[0] + jnp.where(name == 2 * k, term_g[e], 0.0)
            out[1] = out[1] + jnp.where(name == 2 * k + 1, term_g[e], 0.0)
            out[2] = out[2] + jnp.where(name == side, term_h[e], 0.0)
        return jnp.concatenate(out, axis=0)

    lane = iota((HALF, LANES), 1)

    def solve(it, c):
        normal = functools.reduce(lambda x, y: x + y, [rbuf[it, c, k] for k in range(CHIPS)])
        part = lane % BLOCK
        upper = (lane & BLOCK) != 0
        sign = jnp.where(upper == (lane < 64), 1.0, -1.0)
        packed = normal[2 * SUB :, :]
        both = jnp.concatenate([packed, packed], axis=0)
        part = part + 64 * (iota((HALF, LANES), 0) // SUB)
        per = scale[c]
        rho = pen[...]
        rhs = normal[: 2 * SUB, :] * per + rho * (cons[c] - dual[c])
        h_diag = lanes(both, jnp.where(upper, part, BLOCK + part)) * per + rho
        h_swap = lanes(both, jnp.where(upper, BLOCK + part, part)) * per + rho
        h_real = lanes(both, 2 * BLOCK + part) * per
        h_imag = lanes(both, 3 * BLOCK + part) * per
        determ = h_diag * h_swap - h_real * h_real - h_imag * h_imag
        return (
            rhs * h_diag
            - lanes(rhs, lane ^ BLOCK) * h_real
            + sign * lanes(rhs, lane ^ (64 + BLOCK)) * h_imag
        ) / determ

    def iteration(it, carry):
        def send_terms(c, carry):
            chain = 2 * it + c

            @pl.when(it > 0)
            def _():
                arrived(every.at[it, pl.ds(0, 2 * CHIPS - 2), c], ag_r.at[chain])

            @pl.when(it == 0)
            def _():
                arrived(every.at[0, pl.ds(0, 2 * CHIPS - 1), c], ag_r.at[c])

            tile_terms(it, c)
            for dz, dx in FAR:
                k = at(dz, dx)
                sbuf[it, c, k] = share(k)
                copy(
                    sbuf.at[it, c, k], rbuf.at[it, c, chip], rs_s.at[chain], rs_r.at[chain],
                    band, 2 * k + core,
                ).start()
            rbuf[it, c, chip] = share(chip)
            return carry

        lax.fori_loop(0, 2, send_terms, 0, unroll=True)

        @pl.when(it > 0)
        def _():
            coeff = from_total(total_at(it - 1), it == 1)
            for b in range(2):
                agreed = basis[0] * coeff[b][0:1, :]
                for k in range(1, NPOLY):
                    agreed = agreed + basis[k] * coeff[b][k : k + 1, :]
                rows = pl.ds(SUB * b, SUB)
                for c in range(2):
                    new = agreed[SUB * c : SUB * (c + 1), :]
                    dual[c, rows] = mixed[c, rows] - new
                    cons[c, rows] = new

        @pl.when(it == 0)
        def _():
            for c in range(2):
                for b in range(2):
                    cons[c, pl.ds(SUB * b, SUB)] = every[0, 2 * chip + b, c]
            dual[...] = jnp.zeros((2, HALF, LANES), F32)

        @pl.when(it == 0)
        def _():
            arrived(wrec.at[pl.ds(0, CHIPS - 1)], one.at[7])
            total = functools.reduce(lambda a, b: a + b, [wrec[k] for k in range(CHIPS)])
            for c in range(2):
                for b in range(2):
                    at_station = jnp.broadcast_to(total[b : b + 1, :], (SUB, LANES))
                    counts = chans[SUB * c : SUB * (c + 1)] * at_station
                    scale[c, pl.ds(SUB * b, SUB)] = 1.0 / jnp.maximum(counts, 1.0)

        def send_gains(c, carry):
            chain = 2 * it + c
            arrived(rbuf.at[it, c, pl.ds(0, CHIPS - 1)], rs_r.at[chain])
            solved = solve(it, c)
            every[it + 1, 2 * chip, c] = solved[:SUB]
            every[it + 1, 2 * chip + 1, c] = solved[SUB:]

            @pl.when(it + 1 < ITERS)
            def _():
                for dz, dx in FAR:
                    copy(
                        every.at[it + 1, own_blocks, c], every.at[it + 1, own_blocks, c],
                        ag_s.at[chain + 2], ag_r.at[chain + 2], band, 2 * at(dz, dx) + core,
                    ).start()

            mixed[c] = solved + dual[c]
            return carry

        lax.fori_loop(0, 2, send_gains, 0, unroll=True)

        @pl.when(it + 1 < ITERS)
        def _():
            total_of(it)

        return carry

    lax.fori_loop(0, ITERS, iteration, 0)

    for c in range(2):
        last[c] = jnp.concatenate(along_basis(of_block(c)), axis=0)

    def send_last(c, band_to, base_to):
        copy(
            last.at[c], last.at[2 + me], one.at[10], one.at[11], band_to, base_to
        ).start()

    for d in (2, 1, 3):
        for c in range(2):
            send_last(c, (band + d) % BANDS, 2 * chip + c)
    send_last(1 - core, band, sibling)
    final_copy = copy(
        every.at[ITERS, sibling], final.at[core], one.at[8], one.at[9], band, sibling
    )
    final_copy.start()
    last[2 + me] = last[core]
    final[core] = every[ITERS, base]
    final_copy.wait_recv()
    gains_out[...] = final[...].reshape(SOLS, LANES).T.reshape(8, BLOCK, SOLS)
    arrived(last.at[pl.ds(0, 2 * BANDS - 1)], one.at[11])
    coeff = solve_gram(
        functools.reduce(lambda a, b: a + b, [last[2 + k] for k in range(2 * BANDS)])
    )
    for k in range(8):
        coeff_out[:, k, :] = coeff[:NPOLY, k * BLOCK : (k + 1) * BLOCK]

    names_copy.wait_send()
    away_copy.wait_send()
    final_copy.wait_send()
    arrived(half_out, one.at[4])
    arrived(wsend.at[pl.ds(0, CHIPS - 1)], one.at[6])
    for c in range(2):
        arrived(every.at[0, pl.ds(0, 2 * CHIPS - 1), c], ag_s.at[c])
    for it in range(ITERS):
        for c in range(2):
            if it > 0:
                arrived(every.at[it, pl.ds(0, 2 * CHIPS - 2), c], ag_s.at[2 * it + c])
            arrived(sbuf.at[it, c, pl.ds(0, CHIPS - 1)], rs_s.at[2 * it + c])
        if it + 1 < ITERS:
            arrived(prec.at[it, pl.ds(0, 2 * BANDS - 1)], ps_s.at[it])
    arrived(last.at[pl.ds(0, 2 * BANDS - 1)], one.at[10])


def on_device(visibilities, model, start_gains, penalty, pairs, flags, chan_band):
    vmem, dma = pltpu.VMEM, pltpu.SemaphoreType.DMA
    gains, coeff = pl.pallas_call(
        kernel,
        out_shape=(
            jax.ShapeDtypeStruct((8, BLOCK, SOLS), F32),
            jax.ShapeDtypeStruct((NPOLY, 8, BLOCK), F32),
        ),
        in_specs=[pl.BlockSpec(memory_space=pltpu.HBM)] * 7,
        out_specs=(pl.BlockSpec(memory_space=vmem), pl.BlockSpec(memory_space=vmem)),
        scratch_shapes=[
            vmem((8, TILES, CHANS, CELLS), BF16),
            vmem((8, TILES, CHANS, CELLS), BF16),
            vmem((8, BLOCK, SOLS), F32),
            vmem((1, BLOCK), F32),
            pltpu.SMEM((TILES, 2), jnp.int32),
            vmem((TILES, CELLS), jnp.int32),
            vmem((1, CHANS), jnp.int32),
            pltpu.SMEM((2 * TILES, 2), jnp.int32),
            vmem((8, CHANS, CELLS), F32),
            vmem((8, CHANS, CELLS), F32),
            vmem((2 * TILES, NCOEF + 16, HALF, CELLS), F32),
            vmem((TILES, NCOEF, HALF, CELLS), F32),
            vmem((2, 2, SUB, LANES), F32),
            vmem((ITERS + 1, 2 * CHIPS, 2, SUB, LANES), F32),
            vmem((ITERS, 2, CHIPS, ROWS, LANES), F32),
            vmem((ITERS, 2, CHIPS, ROWS, LANES), F32),
            vmem((ITERS, 2 * BANDS, 48, LANES), F32),
            vmem((2, 8, LANES), jnp.int32),
            vmem((2, 8, LANES), F32),
            vmem((CHIPS, 8, LANES), F32),
            vmem((CHIPS, 8, LANES), F32),
            vmem((2 * CHIPS, SUB, LANES), F32),
            vmem((2 * TILES, 2, 8, SUB, LANES), F32),
            vmem((2 * TILES, 8, SUB, LANES), F32),
            vmem((2 * TILES, 36, SUB, LANES), F32),
            vmem((4 * TILES, SUB, LANES), F32),
            vmem((4 * TILES, SUB, LANES), F32),
            vmem((4 * TILES, SUB, LANES), jnp.int32),
            vmem((2, HALF, LANES), F32),
            vmem((2, 2, SUB, LANES), F32),
            vmem((2 + 2 * BANDS, 16, LANES), F32),
            vmem((NPOLY, HALF, LANES), F32),
            vmem((2, HALF, LANES), F32),
            vmem((HALF, LANES), F32),
            vmem((2, HALF, LANES), F32),
            vmem((2, HALF, LANES), F32),
            vmem((NPOLY, 16, LANES), F32),
            dma((7,)),
            *[dma((2 * ITERS,))] * 4,
            *[dma((ITERS,))] * 2,
            dma((12,)),
        ],
        compiler_params=pltpu.CompilerParams(
            collective_id=0, has_side_effects=True, vmem_limit_bytes=40 * 1024 * 1024
        ),
        cost_estimate=pl.CostEstimate(
            flops=60_000_000, bytes_accessed=3_000_000, transcendentals=0
        ),
        name="admm",
    )(
        *[
            pltpu.with_memory_space_constraint(x, pltpu.HBM)
            for x in (
                visibilities, model, jnp.swapaxes(start_gains, 1, 2), penalty.reshape(1, BLOCK),
                pairs, flags, chan_band.reshape(1, CHANS),
            )
        ]
    )
    return jnp.swapaxes(gains, 1, 2), jnp.swapaxes(coeff, 0, 1)


def solution(mesh):
    in_specs = (
        P(None, "base", "band", None),
        P(None, "base", "band", None),
        P(None, "band", "base"),
        P("base"),
        P("base", None),
        P("base", None),
        P("band"),
    )
    out_specs = (P(None, "band", "base"), P(None, None, "base"))
    return jax.shard_map(
        on_device, mesh=mesh, in_specs=in_specs, out_specs=out_specs, check_vma=False
    )
```
